512 devices in a mesh: lon: 64 (over x_hi, z, core), lat: 8 (over y, x_lo).
Axes of the slice: x: 4 (x_hi: 2, x_lo: 2; x = x_hi * 2 + x_lo), y: 4, z: 16, core: 2. Of those that a mesh axis runs over, the one named last changes fastest.
Arguments:
- tokens: bfloat16 [128, 512, 1024], P('lat', 'lon'), may hold values from -6 to 6
- labels: int32 [128, 512], P('lat', 'lon'), may hold values from 0 to 3
- w_qkv: bfloat16 [1024, 1536], replicated, may hold values from -0.1875 to 0.1875
- w_proj: bfloat16 [512, 1024], replicated, may hold values from -0.25 to 0.25
- logit_scale: float32 [16], replicated, may hold values from 0 to 2
- bias_table: float32 [16, 225], replicated, may hold values from -6 to 6
- norm_gain: float32 [1024], replicated, may hold values from 0.1 to 1.9
- norm_shift: float32 [1024], replicated, may hold values from -3 to 3
- merge_gain: float32 [4096], replicated, may hold values from 0.1 to 1.9
- cotangent: bfloat16 [64, 256, 4096], P('lat', 'lon'), may hold values from -6 to 6
Outputs:
- d_tokens: bfloat16 [128, 512, 1024], P('lat', 'lon')
The draws below stay inside these ranges and needn't reach their ends.
All inputs are finite; a program needn't handle non-finite values.
Results may differ from the reference program's by a relative error of at most 0.0065.
Values may be sent and summed in bfloat16 or wider, within the bound.
No kernel may reach another device: no remote copies, remote signals or barrier semaphores. Data moves between devices by JAX's collectives and lax.ppermute only.
A program may use at most 64 MiB of HBM per device.

```python
import math
import jax
import jax.numpy as jnp
from jax import lax

D = 1024
HEADS = 16
WIN = 8
LABELS = 4
ATT = 512
NROWS = 128
NCOLS = 512


def touch_ends(drawn, key, smallest, top_value):
    longest = drawn.shape.index(max(drawn.shape))
    spots = []
    for shift in (0, 1):
        where = [jax.random.randint(jax.random.fold_in(key, axis), (), 0, length) for axis, length in enumerate(drawn.shape)]
        where[longest] = (where[longest] + shift) % drawn.shape[longest]
        spots.append(tuple(where))
    return drawn.at[spots[0]].set(smallest).at[spots[1]].set(top_value)


def shard_levels(own_key, extent, cuts, low, largest):
    level = 1.0
    for axis_at, blocks in cuts:
        draws = jax.random.uniform(jax.random.fold_in(jax.random.fold_in(own_key, 6), axis_at), (blocks,), jnp.float32, low / len(cuts), largest / len(cuts))
        level = level * jnp.repeat(jnp.exp(draws), extent[axis_at] // blocks).reshape((-1,) + (1,) * (len(extent) - 1 - axis_at))
    return level


def scatter_about(stream_key, extent, scale, most, split=(), held_as=jnp.bfloat16):
    loudness = shard_levels(stream_key, extent, split, -0.22, 0.18) if split else 1.0
    values = jax.random.normal(stream_key, extent, jnp.float32) * scale * loudness
    return jnp.minimum(jnp.maximum(values, -most), most).astype(held_as)


def setup_inputs(seed: int = 0) -> dict:
    key_of = jax.random.split(jax.random.key(seed), 11)
    return {
        "tokens": scatter_about(key_of[0], (NROWS, NCOLS, D), 1.0, 6.0, ((0, 8), (1, 64))),
        "labels": touch_ends(jax.random.randint(key_of[1], (NROWS, NCOLS), 0, LABELS), jax.random.fold_in(key_of[1], 1), 0, LABELS - 1).astype(jnp.int32),
        "w_qkv": scatter_about(key_of[2], (D, 3 * ATT), D ** -0.5, 0.1875),
        "w_proj": scatter_about(key_of[3], (ATT, D), ATT ** -0.5, 0.25),
        "logit_scale": jnp.clip(jax.random.uniform(key_of[4], (HEADS,), jnp.float32, 0.0, 2.0), 0.0, 2.0),
        "bias_table": scatter_about(key_of[5], (HEADS, (2 * WIN - 1) * (2 * WIN - 1)), 1.5, 6.0, (), jnp.float32),
        "norm_gain": jnp.clip(1.0 + 0.18 * jax.random.normal(key_of[6], (D,), jnp.float32), 0.1, 1.9),
        "norm_shift": scatter_about(key_of[7], (D,), 0.5, 3.0, (), jnp.float32),
        "merge_gain": jnp.clip(1.0 + 0.18 * jax.random.normal(key_of[8], (4 * D,), jnp.float32), 0.1, 1.9),
        "cotangent": scatter_about(key_of[9], (NROWS // 2, NCOLS // 2, 4 * D), 1.0, 6.0, ((0, 8), (1, 64))),
    }


norm_eps = 1e-05
unit_eps = 1e-06
highest = lax.Precision.HIGHEST

def to_windows(array):
    row_count, col_count, feature = array.shape
    blocks = array.reshape(row_count // WIN, WIN, col_count // WIN, WIN, feature)
    return blocks.transpose(0, 2, 1, 3, 4).reshape(-1, WIN * WIN, feature)

def from_windows(array, row_count, col_count):
    feature = array.shape[-1]
    blocks = array.reshape(row_count // WIN, col_count // WIN, WIN, WIN, feature)
    return blocks.transpose(0, 2, 1, 3, 4).reshape(row_count, col_count, feature)

def relative_bias(bias_table):
    spread = 2 * WIN - 1
    cell_ids = jnp.arange(WIN * WIN, dtype=jnp.int32)
    row_in = cell_ids // WIN
    col_in = cell_ids % WIN
    offset = (row_in[:, None] - row_in[None, :] + WIN - 1) * spread + (col_in[:, None] - col_in[None, :] + WIN - 1)
    onehot = (offset[:, :, None] == jnp.arange(spread * spread, dtype=jnp.int32)).astype(jnp.float32)
    raw_bias = jnp.einsum('ijr,hr->hij', onehot, bias_table.astype(jnp.float32), precision=highest)
    return 16.0 * jax.nn.sigmoid(raw_bias)

def window_mask(labels, wrapped):
    label_win = to_windows(labels[:, :, None])[:, :, 0]
    wrap_win = to_windows(wrapped[:, :, None])[:, :, 0]
    same_label = label_win[:, :, None] == label_win[:, None, :]
    same_side = wrap_win[:, :, None] == wrap_win[:, None, :]
    return same_label & same_side

def attend_forward(packed, allowed, temper, rel_bias):
    win_count = packed.shape[0]
    head_count = rel_bias.shape[0]
    att_width = packed.shape[-1] // 3
    split_heads = packed.reshape(win_count, WIN * WIN, 3, head_count, att_width // head_count)
    queries = split_heads[:, :, 0].astype(jnp.float32)
    key_heads = split_heads[:, :, 1].astype(jnp.float32)
    val_heads = split_heads[:, :, 2]
    query_inv = lax.rsqrt(lax.optimization_barrier(jnp.sum(queries * queries, -1, keepdims=True)) + unit_eps)
    key_inv = lax.rsqrt(lax.optimization_barrier(jnp.sum(key_heads * key_heads, -1, keepdims=True)) + unit_eps)
    query_unit = queries * query_inv
    key_unit = key_heads * key_inv
    cosine = jnp.einsum('nihd,njhd->nhij', query_unit, key_unit, precision=highest)
    scores = cosine * temper[None, :, None, None] + rel_bias[None]
    mask_gate = allowed[:, None]
    row_max = lax.optimization_barrier(jnp.max(jnp.where(mask_gate, scores, -jnp.inf), -1, keepdims=True))
    exponent = jnp.where(mask_gate, jnp.exp(scores - row_max), 0.0)
    attn_prob = exponent / lax.optimization_barrier(jnp.sum(exponent, -1, keepdims=True))
    weights = attn_prob.astype(jnp.bfloat16)
    attended = jnp.einsum('nhij,njhd->nihd', weights.astype(jnp.float32), val_heads.astype(jnp.float32), precision=highest)
    attended = attended.reshape(win_count, WIN * WIN, att_width).astype(jnp.bfloat16)
    return (attended, (query_unit, key_unit, query_inv, key_inv, attn_prob, weights, val_heads))

def attend_backward(grad_out, stored, temper):
    query_unit, key_unit, query_inv, key_inv, attn_prob, weights, val_heads = stored
    win_count, cell_count, head_count, head_width = query_unit.shape
    grad_heads = grad_out.astype(jnp.float32).reshape(win_count, cell_count, head_count, head_width)
    grad_prob = jnp.einsum('nihd,njhd->nhij', grad_heads, val_heads.astype(jnp.float32), precision=highest)
    grad_val = jnp.einsum('nhij,nihd->njhd', weights.astype(jnp.float32), grad_heads, precision=highest)
    grad_score = attn_prob * (grad_prob - lax.optimization_barrier(jnp.sum(attn_prob * grad_prob, -1, keepdims=True)))
    grad_cos = grad_score * temper[None, :, None, None]
    grad_qunit = jnp.einsum('nhij,njhd->nihd', grad_cos, key_unit, precision=highest)
    grad_kunit = jnp.einsum('nhij,nihd->njhd', grad_cos, query_unit, precision=highest)
    grad_query = query_inv * (grad_qunit - query_unit * lax.optimization_barrier(jnp.sum(query_unit * grad_qunit, -1, keepdims=True)))
    grad_key = key_inv * (grad_kunit - key_unit * lax.optimization_barrier(jnp.sum(key_unit * grad_kunit, -1, keepdims=True)))
    stacked = jnp.stack([grad_query, grad_key, grad_val], 2)
    return stacked.reshape(win_count, cell_count, -1).astype(jnp.bfloat16)

def merge_tokens(mixed):
    row_count, col_count, width_d = mixed.shape
    grouped = mixed.reshape(row_count // 2, 2, col_count // 2, 2, width_d)
    return grouped.transpose(0, 2, 3, 1, 4).reshape(row_count // 2, col_count // 2, 4 * width_d)

def split_tokens(merged, width_d):
    row_half, col_half, fourfold = merged.shape
    grouped = merged.reshape(row_half, col_half, 2, 2, width_d)
    return grouped.transpose(0, 3, 1, 2, 4).reshape(row_half * 2, col_half * 2, width_d)

def token_backward(attended, rolled, cot, w_proj, norm_gain, norm_shift, merge_gain):
    row_count, col_count, att_width = attended.shape
    width_d = w_proj.shape[1]
    projected = jnp.dot(attended.reshape(-1, att_width), w_proj, preferred_element_type=jnp.float32)
    centered = projected - lax.optimization_barrier(jnp.mean(projected, -1, keepdims=True))
    inv_std = lax.rsqrt(lax.optimization_barrier(jnp.mean(centered * centered, -1, keepdims=True)) + norm_eps)
    normed = centered * inv_std
    mixed = rolled.reshape(-1, width_d).astype(jnp.float32) + normed * norm_gain + norm_shift
    merged = merge_tokens(mixed.reshape(row_count, col_count, width_d))
    merge_cent = merged - lax.optimization_barrier(jnp.mean(merged, -1, keepdims=True))
    merge_inv = lax.rsqrt(lax.optimization_barrier(jnp.mean(merge_cent * merge_cent, -1, keepdims=True)) + norm_eps)
    merge_hat = merge_cent * merge_inv
    grad_hat = cot.astype(jnp.float32) * merge_gain
    grad_merged = merge_inv * (grad_hat - lax.optimization_barrier(jnp.mean(grad_hat, -1, keepdims=True)) - merge_hat * lax.optimization_barrier(jnp.mean(grad_hat * merge_hat, -1, keepdims=True)))
    grad_mixed = split_tokens(grad_merged, width_d).reshape(-1, width_d)
    grad_norm = grad_mixed * norm_gain
    grad_proj = inv_std * (grad_norm - lax.optimization_barrier(jnp.mean(grad_norm, -1, keepdims=True)) - normed * lax.optimization_barrier(jnp.mean(grad_norm * normed, -1, keepdims=True)))
    grad_proj = grad_proj.astype(jnp.bfloat16)
    grad_att = lax.dot_general(grad_proj, w_proj, (((1,), (1,)), ((), ())), preferred_element_type=jnp.float32)
    grad_att = grad_att.astype(jnp.bfloat16)
    return (grad_att.reshape(row_count, col_count, att_width), grad_mixed.reshape(row_count, col_count, width_d))

def finish_grad(grad_mixed, grad_packed, w_qkv):
    row_count, col_count, width_d = grad_mixed.shape
    flat_packed = grad_packed.reshape(row_count * col_count, -1)
    through = lax.dot_general(flat_packed, w_qkv, (((1,), (1,)), ((), ())), preferred_element_type=jnp.float32)
    total = grad_mixed.reshape(-1, width_d) + through
    return total.astype(jnp.bfloat16).reshape(row_count, col_count, width_d)

def region_grad(rolled, labels, wrapped, cot, w_qkv, w_proj, temper, rel_bias, norm_gain, norm_shift, merge_gain):
    row_count, col_count, width_d = rolled.shape
    packed = jnp.dot(rolled.reshape(-1, width_d), w_qkv, preferred_element_type=jnp.float32)
    packed = packed.astype(jnp.bfloat16).reshape(row_count, col_count, -1)
    allowed = window_mask(labels, wrapped)
    attended, stored = attend_forward(to_windows(packed), allowed, temper, rel_bias)
    attended_grid = from_windows(attended, row_count, col_count)
    grad_att, grad_mixed = token_backward(attended_grid, rolled, cot, w_proj, norm_gain, norm_shift, merge_gain)
    grad_packed = from_windows(attend_backward(to_windows(grad_att), stored, temper), row_count, col_count)
    return finish_grad(grad_mixed, grad_packed, w_qkv)

def reference(tokens, labels, w_qkv, w_proj, logit_scale, bias_table, norm_gain, norm_shift, merge_gain, cotangent):
    half_win = WIN // 2
    rolled = jnp.roll(tokens, (-half_win, -half_win), (0, 1))
    rolled_labels = jnp.roll(labels, (-half_win, -half_win), (0, 1))
    rolled_cot = jnp.roll(cotangent, (-(half_win // 2), -(half_win // 2)), (0, 1))
    row_ids = jnp.arange(NROWS, dtype=jnp.int32)
    wrapped = jnp.broadcast_to((row_ids >= NROWS - half_win)[:, None], (NROWS, NCOLS)).astype(jnp.int32)
    temper = jnp.exp(jnp.minimum(logit_scale, math.log(100.0)))
    rel_bias = relative_bias(bias_table)

    def one_band(band_index):
        band_start = band_index * WIN
        band_tokens = lax.dynamic_slice_in_dim(rolled, band_start, WIN, 0)
        band_labels = lax.dynamic_slice_in_dim(rolled_labels, band_start, WIN, 0)
        band_wrap = lax.dynamic_slice_in_dim(wrapped, band_start, WIN, 0)
        band_cot = lax.dynamic_slice_in_dim(rolled_cot, band_index * (WIN // 2), WIN // 2, 0)
        return region_grad(band_tokens, band_labels, band_wrap, band_cot, w_qkv, w_proj, temper, rel_bias, norm_gain, norm_shift, merge_gain)
    grads = lax.map(one_band, jnp.arange(NROWS // WIN, dtype=jnp.int32))
    grads = grads.reshape(NROWS, NCOLS, D)
    return jnp.roll(grads, (half_win, half_win), (0, 1))
```

```python
import math

import numpy as np
import jax
import jax.numpy as jnp
from jax import lax
from jax.experimental import pallas as pl
from jax.experimental.pallas import tpu as pltpu
from jax.sharding import PartitionSpec as P

WIN = 8
D = 1024
HEADS = 16
ATT = 512
QUAD = 16
CELLS = 64
BLOCKS = 4
WIDE = 2 * D + 128

norm_eps = 1e-05
unit_eps = 1e-06
f32 = jnp.float32
bf16 = jnp.bfloat16
MIB = 1024 * 1024


def quad_cells():
    cells = [None] * QUAD
    for r in range(4):
        for c in range(4):
            s = (r % 2) + 2 * (c % 2)
            g = (r // 2) * 2 + c // 2
            cells[s * 4 + g] = (r, c)
    return cells


def sorted_cells():
    corners = [(4, 4), (8, 4), (12, 4), (4, 0), (8, 0), (12, 0), (0, 4), (0, 0)]
    return [(r0 + r, c0 + c) for r0, c0 in corners for r, c in quad_cells()]


def window_cells():
    corners = [(0, 0), (0, 4), (4, 0), (4, 4)]
    return [(r0 + r, c0 + c) for r0, c0 in corners for r, c in quad_cells()]


def constants():
    cells = sorted_cells()
    token_sort = np.zeros((128, 128), np.float32)
    cot_sort = np.zeros((128, 128), np.float32)
    label_row = np.zeros((128, 16), np.float32)
    label_col = np.zeros((128, 8), np.float32)
    for n, (r, c) in enumerate(cells):
        token_sort[n, r * 8 + c] = 1
        s = (r % 2) + 2 * (c % 2)
        cot_sort[n, s * 32 + (r // 2) * 4 + c // 2] = 1
        label_row[n, r] = 1
        label_col[n, c] = 1
    table_spread = np.zeros((225, 256), np.float32)
    for m in range(15):
        for c in range(15):
            table_spread[224 - (15 * m + c), 16 * m + c] = 1
    order = window_cells()
    toeplitz = np.zeros((256, 512), np.float32)
    row_order = np.zeros((64, 64), np.float32)
    for n, (ra, rb) in enumerate(order):
        row_order[n, ra * 8 + rb] = 1
        for a in range(8):
            toeplitz[16 * (ra - a + 7) + rb, a * 64 + n] = 1
    return (token_sort, cot_sort, label_row, label_col, table_spread, toeplitz, row_order)


def halves(value):
    high = value.astype(bf16)
    low = (value - high.astype(f32)).astype(bf16)
    return high, low


def mm(a, b):
    return jnp.dot(a, b, preferred_element_type=f32)


def mm_nt(a, b):
    return lax.dot_general(a, b, (((1,), (1,)), ((), ())), preferred_element_type=f32)


def mm_tn(a, b):
    return lax.dot_general(a, b, (((0,), (0,)), ((), ())), preferred_element_type=f32)


def pack_kernel(
    tokens, labels, cot, token_sort, cot_sort, label_row, label_col, own, lon, lat, dia, cot_rows
):
    outs = ((own, 0, 48), (lon, 48, 96), (lat, 96, 112), (dia, 112, 128))
    flat = tokens[...].reshape(128, D)
    moved = mm(token_sort[...], flat).astype(bf16)
    for ref, lo, hi in outs:
        ref[:, 0:D] = moved[lo:hi]
    for r in range(8):
        cot_rows[4 * r : 4 * r + 4, :] = cot[r].astype(f32)
    stacked = jnp.concatenate(
        [cot_rows[:, s * D : (s + 1) * D].astype(bf16) for s in range(4)], axis=0
    )
    moved_cot = mm(cot_sort[...], stacked).astype(bf16)
    for ref, lo, hi in outs:
        ref[:, D : 2 * D] = moved_cot[lo:hi]
    first = lax.axis_index("lat") == 0
    rows = lax.broadcasted_iota(jnp.int32, (16, 8), 0)
    code = labels[...] + jnp.where(rows < 4, jnp.where(first, 4, 0), 0)
    spread = mm(label_row[...], code.astype(f32).astype(bf16)) * label_col[...]
    column = jnp.sum(spread, axis=1, keepdims=True)
    wide = jnp.broadcast_to(column, (128, 128)).astype(bf16)
    for ref, lo, hi in outs:
        ref[:, 2 * D :] = wide[lo:hi]


def pack(tokens, labels, cot, consts):
    token_sort, cot_sort, label_row, label_col = consts
    shapes = [jax.ShapeDtypeStruct((n, WIDE), bf16) for n in (48, 48, 16, 16)]
    return pl.pallas_call(
        pack_kernel,
        out_shape=shapes,
        scratch_shapes=[pltpu.VMEM((32, 4 * D), f32)],
        compiler_params=pltpu.CompilerParams(vmem_limit_bytes=16 * MIB),
        name="pack",
    )(
        tokens,
        labels,
        cot,
        jnp.asarray(token_sort, bf16),
        jnp.asarray(cot_sort, bf16),
        jnp.asarray(label_row, bf16),
        jnp.asarray(label_col, f32),
    )


def prep_kernel(table, scale, table_spread, toeplitz, row_order, ebias, temper, natural):
    gate = 16.0 / (1.0 + jnp.exp(-table[...]))
    high, low = halves(gate)
    spread = mm(high, table_spread[...]) + mm(low, table_spread[...])
    pieces = []
    for h in range(HEADS):
        row = jnp.broadcast_to(spread[h : h + 1, :], (8, 256))
        pieces.append(pltpu.roll(row, 249, 1, stride=1, stride_axis=0))
    shifted = jnp.concatenate(pieces, axis=0)
    high, low = halves(shifted)
    blocks = mm(high, toeplitz[...]) + mm(low, toeplitz[...])
    left = lax.broadcasted_iota(jnp.int32, (8, 128), 1) < 64
    for q in range(8):
        for p in range(4):
            even = blocks[16 * q : 16 * q + 8, 128 * p : 128 * p + 128]
            odd = blocks[16 * q + 8 : 16 * q + 16, 128 * p : 128 * p + 128]
            lanes = slice(128 * q, 128 * q + 128)
            natural[16 * p : 16 * p + 8, lanes] = jnp.where(left, even, pltpu.roll(odd, 64, 1))
            natural[16 * p + 8 : 16 * p + 16, lanes] = jnp.where(
                left, pltpu.roll(even, 64, 1), odd
            )
    high, low = halves(natural[...])
    ordered = mm(row_order[...], high) + mm(row_order[...], low)
    ebias[...] = jnp.exp(ordered)
    per_head = jnp.exp(jnp.minimum(scale[...], math.log(100.0)))
    head_of = lax.broadcasted_iota(jnp.int32, (1, ATT), 1) // 32
    row = jnp.zeros((1, ATT), f32)
    for h in range(HEADS):
        row = jnp.where(head_of == h, per_head[0:1, h : h + 1], row)
    temper[...] = row


def prep(table, scale, consts):
    table_spread, toeplitz, row_order = consts
    return pl.pallas_call(
        prep_kernel,
        out_shape=[
            jax.ShapeDtypeStruct((CELLS, HEADS * CELLS), f32),
            jax.ShapeDtypeStruct((1, ATT), f32),
        ],
        scratch_shapes=[pltpu.VMEM((CELLS, HEADS * CELLS), f32)],
        compiler_params=pltpu.CompilerParams(vmem_limit_bytes=16 * MIB),
        cost_estimate=pl.CostEstimate(flops=100_000_000, bytes_accessed=700_000, transcendentals=80_000),
        name="prep",
    )(
        table,
        scale,
        jnp.asarray(table_spread, bf16),
        jnp.asarray(toeplitz, bf16),
        jnp.asarray(row_order, bf16),
    )


def group_total(column):
    pair = column[0:8] + column[8:16]
    pair = pair + pltpu.roll(pair, 4, 0)
    return jnp.concatenate([pair, pair], axis=0)


def row_total(value):
    return jnp.sum(value, axis=1, keepdims=True)


def main_kernel(
    own,
    lon,
    lat,
    dia,
    ebias,
    temper,
    w_qkv,
    w_proj,
    gain,
    shift,
    merge_gain,
    out_own,
    out_lon,
    out_lat,
    out_dia,
    x_s,
    qkv_s,
    unit_s,
    inv_s,
    qk_s,
    prob_s,
    att_s,
    att16_s,
    proj_s,
    mixed_s,
    gproj_s,
    ga_s,
    gpack_s,
):
    quads = (
        (own, out_own, 0),
        (lon, out_lon, 0),
        (own, out_own, 16),
        (lon, out_lon, 16),
        (own, out_own, 32),
        (lon, out_lon, 32),
        (lat, out_lat, 0),
        (dia, out_dia, 0),
    )
    for n, (ref, _, lo) in enumerate(quads):
        x_s[16 * n : 16 * n + 16, :] = ref[lo : lo + 16, 0:D]
    for n in range(6):
        cols = slice(256 * n, 256 * n + 256)
        qkv_s[:, cols] = mm(x_s[...], w_qkv[:, cols]).astype(bf16)

    lane = lax.broadcasted_iota(jnp.int32, (256, 128), 1)
    line = lax.broadcasted_iota(jnp.int32, (256, 128), 0)
    seg = ((line % 128) // 32 == lane // 32).astype(f32).astype(bf16)
    bd_mask = line // 64 == lane // 32
    lane2 = lax.broadcasted_iota(jnp.int32, (256, 256), 1)
    line2 = lax.broadcasted_iota(jnp.int32, (256, 256), 0)
    ones4 = (line2 // 64 == lane2 // 64).astype(f32).astype(bf16)
    expand = ((line2 % 128) // 32 == lane2 // 64).astype(f32).astype(bf16)

    def segment(value):
        high, low = halves(value)
        return mm(jnp.concatenate([high, low], axis=1), seg)

    for part in range(2):
        for b in range(BLOCKS):
            cols = slice(part * ATT + 128 * b, part * ATT + 128 * b + 128)
            raw = qkv_s[:, cols].astype(f32)
            inv = lax.rsqrt(segment(raw * raw) + unit_eps)
            unit = raw * inv
            inv_s[:, cols] = inv
            unit_s[:, cols] = unit
            if part == 0:
                unit = unit * temper[:, 128 * b : 128 * b + 128]
            qk_s[:, cols] = unit.astype(bf16)

    def block_diagonal(value):
        tiled = jnp.concatenate([value] * 4, axis=0)
        return jnp.where(bd_mask, tiled, jnp.zeros_like(tiled))

    code_lane = lax.broadcasted_iota(jnp.int32, (16, 128), 1)
    for w in range(2):
        rows = slice(64 * w, 64 * w + 64)
        hot = jnp.concatenate(
            [
                (ref[lo : lo + 16, 2 * D :].astype(f32).astype(jnp.int32) == code_lane)
                .astype(f32)
                .astype(bf16)
                for ref, _, lo in quads[4 * w : 4 * w + 4]
            ],
            axis=0,
        )
        allowed = mm_nt(hot, jnp.concatenate([hot] * 4, axis=0))
        for b in range(BLOCKS):
            cols = slice(128 * b, 128 * b + 128)
            wide = slice(256 * b, 256 * b + 256)
            kbd = block_diagonal(qk_s[rows, ATT + 128 * b : ATT + 128 * b + 128])
            vbd = block_diagonal(qkv_s[rows, 2 * ATT + 128 * b : 2 * ATT + 128 * b + 128])
            score = mm_nt(qk_s[rows, cols], kbd)
            weight = jnp.exp(score) * ebias[:, wide] * allowed
            total = mm(weight.astype(bf16), ones4)
            prob = weight / total
            prob_s[rows, wide] = prob
            att = mm(prob.astype(bf16), vbd)
            att_s[rows, cols] = att
            att16_s[rows, cols] = att.astype(bf16)

    for n in range(4):
        cols = slice(256 * n, 256 * n + 256)
        proj_s[:, cols] = mm(att16_s[...], w_proj[:, cols])

    low_rows = lax.broadcasted_iota(jnp.int32, (8, D), 0) < 4
    mgain = jnp.concatenate(
        [
            jnp.where(low_rows, merge_gain[:, 0:D], merge_gain[:, D : 2 * D]),
            jnp.where(low_rows, merge_gain[:, 2 * D : 3 * D], merge_gain[:, 3 * D : 4 * D]),
        ],
        axis=0,
    )
    for n, (ref, _, lo) in enumerate(quads):
        rows = slice(16 * n, 16 * n + 16)
        projected = proj_s[rows, :]
        centered = projected - row_total(projected) * (1.0 / D)
        inv_std = lax.rsqrt(row_total(centered * centered) * (1.0 / D) + norm_eps)
        normed = centered * inv_std
        mixed = x_s[rows, :].astype(f32) + normed * gain[...] + shift[...]
        cent = mixed - group_total(row_total(mixed)) * (0.25 / D)
        merge_inv = lax.rsqrt(group_total(row_total(cent * cent)) * (0.25 / D) + norm_eps)
        hat = cent * merge_inv
        ghat = ref[lo : lo + 16, D : 2 * D].astype(f32) * mgain
        mean_g = group_total(row_total(ghat)) * (0.25 / D)
        mean_gh = group_total(row_total(ghat * hat)) * (0.25 / D)
        gmixed = merge_inv * (ghat - mean_g - hat * mean_gh)
        mixed_s[rows, :] = gmixed
        gnorm = gmixed * gain[...]
        mean_e = row_total(gnorm) * (1.0 / D)
        mean_en = row_total(gnorm * normed) * (1.0 / D)
        gproj_s[rows, :] = (inv_std * (gnorm - mean_e - normed * mean_en)).astype(bf16)

    for n in range(2):
        cols = slice(256 * n, 256 * n + 256)
        ga_s[:, cols] = mm_nt(gproj_s[...], w_proj[cols, :]).astype(bf16)

    head_lane = lax.broadcasted_iota(jnp.int32, (64, 128), 1) // 32

    def diagonal(value):
        out = value[192:256]
        for h in range(3):
            out = jnp.where(head_lane == h, value[64 * h : 64 * h + 64], out)
        return out

    for w in range(2):
        rows = slice(64 * w, 64 * w + 64)
        for b in range(BLOCKS):
            cols = slice(128 * b, 128 * b + 128)
            kcols = slice(ATT + 128 * b, ATT + 128 * b + 128)
            vcols = slice(2 * ATT + 128 * b, 2 * ATT + 128 * b + 128)
            wide = slice(256 * b, 256 * b + 256)
            kbd = block_diagonal(qk_s[rows, kcols])
            vbd = block_diagonal(qkv_s[rows, vcols])
            ga = ga_s[rows, cols]
            prob = prob_s[rows, wide]
            gprob = mm_nt(ga, vbd)
            high, low = halves(ga.astype(f32) * att_s[rows, cols])
            dots = mm(jnp.concatenate([high, low], axis=1), expand)
            gscore = (prob * (gprob - dots)).astype(bf16)
            gq = mm(gscore, kbd) * temper[:, cols]
            gk = diagonal(mm_tn(gscore, qk_s[rows, cols]))
            gv = diagonal(mm_tn(prob.astype(bf16), ga))
            q_unit = unit_s[rows, cols]
            k_unit = unit_s[rows, kcols]
            gq = inv_s[rows, cols] * (gq - q_unit * segment(q_unit * gq))
            gk = inv_s[rows, kcols] * (gk - k_unit * segment(k_unit * gk))
            gpack_s[rows, cols] = gq.astype(bf16)
            gpack_s[rows, kcols] = gk.astype(bf16)
            gpack_s[rows, vcols] = gv.astype(bf16)

    for n in range(4):
        cols = slice(256 * n, 256 * n + 256)
        total = (mixed_s[:, cols] + mm_nt(gpack_s[...], w_qkv[cols, :])).astype(bf16)
        for m, (_, ref, lo) in enumerate(quads):
            ref[lo : lo + 16, cols] = total[16 * m : 16 * m + 16]


def main(own, lon, lat, dia, ebias, temper, w_qkv, w_proj, gain, shift, merge_gain):
    return pl.pallas_call(
        main_kernel,
        out_shape=[jax.ShapeDtypeStruct((n, D), bf16) for n in (48, 48, 16, 16)],
        scratch_shapes=[
            pltpu.VMEM((128, D), bf16),
            pltpu.VMEM((128, 3 * ATT), bf16),
            pltpu.VMEM((128, 2 * ATT), f32),
            pltpu.VMEM((128, 2 * ATT), f32),
            pltpu.VMEM((128, 2 * ATT), bf16),
            pltpu.VMEM((128, HEADS * CELLS), f32),
            pltpu.VMEM((128, ATT), f32),
            pltpu.VMEM((128, ATT), bf16),
            pltpu.VMEM((128, D), f32),
            pltpu.VMEM((128, D), f32),
            pltpu.VMEM((128, D), bf16),
            pltpu.VMEM((128, ATT), bf16),
            pltpu.VMEM((128, 3 * ATT), bf16),
        ],
        compiler_params=pltpu.CompilerParams(vmem_limit_bytes=32 * MIB),
        cost_estimate=pl.CostEstimate(
            flops=1_500_000_000, bytes_accessed=6_000_000, transcendentals=150_000
        ),
        name="main",
    )(own, lon, lat, dia, ebias, temper, w_qkv, w_proj, gain, shift, merge_gain)


def final_kernel(own, lon, lat, dia, token_place, out):
    rows = jnp.concatenate([own[...], lon[...], lat[...], dia[...]], axis=0)
    out[...] = mm(token_place[...], rows).reshape(16, 8, D).astype(bf16)


def final(own, lon, lat, dia, token_place):
    return pl.pallas_call(
        final_kernel,
        out_shape=jax.ShapeDtypeStruct((16, 8, D), bf16),
        compiler_params=pltpu.CompilerParams(vmem_limit_bytes=16 * MIB),
        name="final",
    )(own, lon, lat, dia, jnp.asarray(token_place, bf16))


def shift_by(block, lat_step, lon_step):
    lats, lons = lax.axis_size("lat"), lax.axis_size("lon")
    route = [
        (j * lats + i, ((j + lon_step) % lons) * lats + (i + lat_step) % lats)
        for j in range(lons)
        for i in range(lats)
    ]
    return lax.ppermute(block, ("lon", "lat"), route)


def shards(
    tokens,
    labels,
    w_qkv,
    w_proj,
    logit_scale,
    bias_table,
    norm_gain,
    norm_shift,
    merge_gain,
    cotangent,
):
    consts = constants()
    own, lon, lat, dia = pack(tokens, labels, cotangent, consts[:4])
    lon = shift_by(lon, 0, -1)
    lat = shift_by(lat, -1, 0)
    dia = shift_by(dia, -1, -1)
    ebias, temper = prep(bias_table, logit_scale.reshape(1, HEADS), consts[4:])
    own, lon, lat, dia = main(
        own,
        lon,
        lat,
        dia,
        ebias,
        temper,
        w_qkv,
        w_proj,
        norm_gain.reshape(1, D),
        norm_shift.reshape(1, D),
        merge_gain.reshape(1, 4 * D),
    )
    lon = shift_by(lon, 0, 1)
    lat = shift_by(lat, 1, 0)
    dia = shift_by(dia, 1, 1)
    return final(own, lon, lat, dia, consts[0].T)


def solution(mesh):
    placed = (
        P("lat", "lon", None),
        P("lat", "lon"),
        P(),
        P(),
        P(),
        P(),
        P(),
        P(),
        P(),
        P("lat", "lon", None),
    )
    return jax.shard_map(
        shards, mesh=mesh, in_specs=placed, out_specs=P("lat", "lon", None), check_vma=False
    )
```

```python
import math

import jax
import jax.numpy as jnp
from jax import lax
from jax.experimental import pallas as pl
from jax.experimental.pallas import tpu as pltpu
from jax.sharding import PartitionSpec as P

WIN = 8
D = 1024
HEADS = 16
ATT = 512
QUAD = 16
CELLS = 64
BLOCKS = 4
WIDE = 2 * D + 128

norm_eps = 1e-05
unit_eps = 1e-06
f32 = jnp.float32
bf16 = jnp.bfloat16
MIB = 1024 * 1024
BUSY = pl.CostEstimate(flops=10_000_000_000, bytes_accessed=30_000_000, transcendentals=0)


def sorted_place(n):
    quad = n // 16
    s = (n // 4) % 4
    g = n % 4
    row = jnp.where(quad < 6, 4 + 4 * (quad % 3), 0) + 2 * (g // 2) + s % 2
    col = jnp.where((quad // 3 == 1) | (quad == 7), 4, 0) + 2 * (g % 2) + s // 2
    return row, col, s


def window_place(n):
    row = 4 * (n // 32) + 2 * ((n // 2) % 2) + (n // 4) % 2
    col = 4 * ((n // 16) % 2) + 2 * (n % 2) + (n // 8) % 2
    return row, col


def iota(shape, axis):
    return lax.broadcasted_iota(jnp.int32, shape, axis)


def onehot(match):
    return match.astype(f32).astype(bf16)


def halves(value):
    high = value.astype(bf16)
    low = (value - high.astype(f32)).astype(bf16)
    return high, low


def mm(a, b):
    return jnp.dot(a, b, preferred_element_type=f32)


def mm_nt(a, b):
    return lax.dot_general(a, b, (((1,), (1,)), ((), ())), preferred_element_type=f32)


def mm_tn(a, b):
    return lax.dot_general(a, b, (((0,), (0,)), ((), ())), preferred_element_type=f32)


def places_kernel(token_sort, cot_sort, label_row, label_col):
    row, col, s = sorted_place(iota((128, 128), 0))
    lane = iota((128, 128), 1)
    token_sort[...] = onehot(lane == row * 8 + col)
    cot_sort[...] = onehot(lane == s * 32 + (row // 2) * 4 + col // 2)
    row, _, _ = sorted_place(iota((128, 16), 0))
    label_row[...] = (iota((128, 16), 1) == row).astype(f32)
    _, col, _ = sorted_place(iota((128, 8), 0))
    label_col[...] = onehot(iota((128, 8), 1) == col)


def places():
    return pl.pallas_call(
        places_kernel,
        out_shape=[
            jax.ShapeDtypeStruct((128, 128), bf16),
            jax.ShapeDtypeStruct((128, 128), bf16),
            jax.ShapeDtypeStruct((128, 16), f32),
            jax.ShapeDtypeStruct((128, 8), bf16),
        ],
        compiler_params=pltpu.CompilerParams(vmem_limit_bytes=8 * MIB),
        cost_estimate=BUSY,
        name="places",
    )()


def pack_kernel(
    token_sort, cot_sort, label_row, label_col, tokens, labels, cot, own, lon, lat, dia, cot_rows
):
    outs = ((own, 0, 48), (lon, 48, 96), (lat, 96, 112), (dia, 112, 128))
    moved = mm(token_sort[...], tokens[...].reshape(128, D)).astype(bf16)
    for ref, lo, hi in outs:
        ref[:, 0:D] = moved[lo:hi]
    first = lax.axis_index("lat") == 0
    code = labels[...] + jnp.where(iota((8, 16), 1) < 4, jnp.where(first, 4, 0), 0)
    spread = mm(label_col[...], code.astype(f32).astype(bf16)) * label_row[...]
    column = jnp.sum(spread, axis=1, keepdims=True)
    wide = jnp.broadcast_to(column, (128, 128)).astype(bf16)
    for ref, lo, hi in outs:
        ref[:, 2 * D :] = wide[lo:hi]
    for r in range(8):
        cot_rows[4 * r : 4 * r + 4, :] = cot[r].astype(f32)
    stacked = jnp.concatenate(
        [cot_rows[:, s * D : (s + 1) * D].astype(bf16) for s in range(4)], axis=0
    )
    moved_cot = mm(cot_sort[...], stacked).astype(bf16)
    for ref, lo, hi in outs:
        ref[:, D : 2 * D] = moved_cot[lo:hi]


def pack(tokens, labels, cot, sorts):
    shapes = [jax.ShapeDtypeStruct((n, WIDE), bf16) for n in (48, 48, 16, 16)]
    return pl.pallas_call(
        pack_kernel,
        out_shape=shapes,
        scratch_shapes=[pltpu.VMEM((32, 4 * D), f32)],
        compiler_params=pltpu.CompilerParams(vmem_limit_bytes=12 * MIB),
        cost_estimate=BUSY,
        name="pack",
    )(*sorts, tokens, labels, cot)


def relative_bias(table, natural, ebias):
    entry, place = iota((225, 256), 0), iota((225, 256), 1)
    table_spread = onehot((entry == 15 * (place // 16) + place % 16) & (place % 16 < 15))
    entry, place = iota((256, 512), 0), iota((256, 512), 1)
    row, col = window_place(place % 64)
    toeplitz = onehot(entry == 16 * (row - place // 64 + 7) + col)
    row, col = window_place(iota((64, 64), 0))
    row_order = onehot(iota((64, 64), 1) == row * 8 + col)
    gate = 16.0 / (1.0 + jnp.exp(-table))
    high, low = halves(gate)
    spread = mm(high, table_spread) + mm(low, table_spread)
    pieces = []
    for h in range(HEADS):
        line = jnp.broadcast_to(spread[h : h + 1, :], (8, 256))
        pieces.append(pltpu.roll(line, 249, 1, stride=1, stride_axis=0))
    high, low = halves(jnp.concatenate(pieces, axis=0))
    blocks = mm(high, toeplitz) + mm(low, toeplitz)
    left = iota((8, 128), 1) < 64
    for q in range(8):
        for p in range(4):
            even = blocks[16 * q : 16 * q + 8, 128 * p : 128 * p + 128]
            odd = blocks[16 * q + 8 : 16 * q + 16, 128 * p : 128 * p + 128]
            lanes = slice(128 * q, 128 * q + 128)
            natural[16 * p : 16 * p + 8, lanes] = jnp.where(left, even, pltpu.roll(odd, 64, 1))
            natural[16 * p + 8 : 16 * p + 16, lanes] = jnp.where(
                left, pltpu.roll(even, 64, 1), odd
            )
    high, low = halves(natural[...])
    ebias[...] = jnp.exp(mm(row_order, high) + mm(row_order, low))


def prep_kernel(table, scale, ebias, temper, natural):
    relative_bias(table[...], natural, ebias)
    per_head = jnp.exp(jnp.minimum(scale[...], math.log(100.0)))
    head_of = iota((1, ATT), 1) // 32
    line = jnp.zeros((1, ATT), f32)
    for h in range(HEADS):
        line = jnp.where(head_of == h, per_head[0:1, h : h + 1], line)
    temper[...] = line


def prep(table, scale):
    return pl.pallas_call(
        prep_kernel,
        out_shape=[
            jax.ShapeDtypeStruct((CELLS, HEADS * CELLS), f32),
            jax.ShapeDtypeStruct((1, ATT), f32),
        ],
        scratch_shapes=[pltpu.VMEM((CELLS, HEADS * CELLS), f32)],
        compiler_params=pltpu.CompilerParams(vmem_limit_bytes=12 * MIB),
        cost_estimate=pl.CostEstimate(
            flops=100_000_000, bytes_accessed=400_000, transcendentals=80_000
        ),
        name="prep",
    )(table, scale)


def group_total(column):
    pair = column[0:8] + column[8:16]
    pair = pair + pltpu.roll(pair, 4, 0)
    return jnp.concatenate([pair, pair], axis=0)


def row_total(value):
    return jnp.sum(value, axis=1, keepdims=True)


def col_total(value):
    return jnp.sum(value, axis=0, keepdims=True)


def main_kernel(
    own,
    lon,
    lat,
    dia,
    ebias,
    temper,
    w_qkv,
    w_proj,
    gain,
    shift,
    merge,
    out_own,
    out_lon,
    out_lat,
    out_dia,
    x_s,
    qkv_s,
    unit_s,
    inv_s,
    unit16_s,
    seg_s,
    qbd_s,
    prob_s,
    prob16_s,
    att_s,
    proj_s,
    mixed_s,
    gproj_s,
    ga_s,
    gpack_s,
    mgain,
):
    quads = (
        (lon, out_lon, 0),
        (own, out_own, 0),
        (lon, out_lon, 16),
        (own, out_own, 16),
        (lon, out_lon, 32),
        (own, out_own, 32),
        (dia, out_dia, 0),
        (lat, out_lat, 0),
    )
    pairs = [(w, b) for w in range(2) for b in range(BLOCKS)]
    for n, (ref, _, lo) in enumerate(quads):
        x_s[16 * n : 16 * n + 16, :] = ref[lo : lo + 16, 0:D]
    for n in range(6):
        cols = slice(256 * n, 256 * n + 256)
        qkv_s[:, cols] = mm(x_s[...], w_qkv[:, cols]).astype(bf16)

    line, lane = iota((256, 128), 0), iota((256, 128), 1)
    seg = onehot((line % 128) // 32 == lane // 32)
    head_lane = iota((64, 128), 1) // 32
    head_mask = [onehot(head_lane == h) for h in range(4)]

    def store_halves(n, value):
        high, low = halves(value)
        seg_s[128 * n : 128 * n + 128, 0:128] = high
        seg_s[128 * n : 128 * n + 128, 128:256] = low

    def block_diagonal(value):
        return jnp.concatenate([value * head_mask[h] for h in range(4)], axis=0)

    def diagonal(value):
        out = value[192:256]
        for h in range(3):
            out = jnp.where(head_lane == h, value[64 * h : 64 * h + 64], out)
        return out

    for n in range(8):
        raw = qkv_s[:, 128 * n : 128 * n + 128].astype(f32)
        store_halves(n, raw * raw)
    squares = mm(seg_s[...], seg)
    for n in range(8):
        cols = slice(128 * n, 128 * n + 128)
        inv = lax.rsqrt(squares[cols] + unit_eps)
        unit = qkv_s[:, cols].astype(f32) * inv
        inv_s[:, cols] = inv
        unit_s[:, cols] = unit
        if n < BLOCKS:
            unit = unit * temper[:, cols]
        unit16_s[:, cols] = unit.astype(bf16)

    code_lane = iota((16, 128), 1)
    allowed = []
    for w in range(2):
        hot = jnp.concatenate(
            [
                onehot(ref[lo : lo + 16, 2 * D :].astype(f32).astype(jnp.int32) == code_lane)
                for ref, _, lo in quads[4 * w : 4 * w + 4]
            ],
            axis=0,
        )
        allowed.append(mm_nt(hot, jnp.concatenate([hot] * 4, axis=0)))
    for n, (w, b) in enumerate(pairs):
        rows = slice(64 * w, 64 * w + 64)
        wide = slice(256 * b, 256 * b + 256)
        qbd = block_diagonal(unit16_s[rows, 128 * b : 128 * b + 128])
        qbd_s[256 * n : 256 * n + 256, :] = qbd
        score = mm_nt(unit16_s[rows, ATT + 128 * b : ATT + 128 * b + 128], qbd)
        weight = jnp.exp(score) * ebias[:, wide] * allowed[w]
        prob = weight * (1.0 / col_total(weight))
        prob_s[rows, wide] = prob
        prob16_s[rows, wide] = prob.astype(bf16)
    for w, b in pairs:
        rows = slice(64 * w, 64 * w + 64)
        vals = qkv_s[rows, 2 * ATT + 128 * b : 2 * ATT + 128 * b + 128]
        att = diagonal(mm_tn(prob16_s[rows, 256 * b : 256 * b + 256], vals))
        att_s[rows, 128 * b : 128 * b + 128] = att.astype(bf16)

    for n in range(4):
        cols = slice(256 * n, 256 * n + 256)
        proj_s[:, cols] = mm(att_s[...], w_proj[:, cols])

    spans = [slice(16 * n, 16 * n + 16) for n in range(8)]

    def ghat_of(n):
        ref, _, lo = quads[n]
        return ref[lo : lo + 16, D : 2 * D].astype(f32) * mgain[...]

    for s in range(4):
        mgain[4 * s : 4 * s + 4, :] = jnp.broadcast_to(merge[:, s * D : (s + 1) * D], (4, D))
    mean = [row_total(proj_s[rows, :]) * (1.0 / D) for rows in spans]
    inv_std = []
    for n, rows in enumerate(spans):
        centered = proj_s[rows, :] - mean[n]
        inv_std.append(lax.rsqrt(row_total(centered * centered) * (1.0 / D) + norm_eps))
    mean_m, mean_g = [], []
    for n, rows in enumerate(spans):
        normed = (proj_s[rows, :] - mean[n]) * inv_std[n]
        proj_s[rows, :] = normed
        mixed = x_s[rows, :].astype(f32) + normed * gain[...] + shift[...]
        mixed_s[rows, :] = mixed
        mean_m.append(group_total(row_total(mixed)) * (0.25 / D))
        mean_g.append(group_total(row_total(ghat_of(n))) * (0.25 / D))
    merge_inv, slope = [], []
    for n, rows in enumerate(spans):
        cent = mixed_s[rows, :] - mean_m[n]
        ghat = ghat_of(n)
        inv = lax.rsqrt(group_total(row_total(cent * cent)) * (0.25 / D) + norm_eps)
        merge_inv.append(inv)
        slope.append(group_total(row_total(ghat * cent)) * (0.25 / D) * inv * inv)
    mean_e, mean_en = [], []
    for n, rows in enumerate(spans):
        cent = mixed_s[rows, :] - mean_m[n]
        gmixed = merge_inv[n] * (ghat_of(n) - mean_g[n] - cent * slope[n])
        mixed_s[rows, :] = gmixed
        gnorm = gmixed * gain[...]
        mean_e.append(row_total(gnorm) * (1.0 / D))
        mean_en.append(row_total(gnorm * proj_s[rows, :]) * (1.0 / D))
    for n, rows in enumerate(spans):
        gnorm = mixed_s[rows, :] * gain[...]
        gproj = inv_std[n] * (gnorm - mean_e[n] - proj_s[rows, :] * mean_en[n])
        gproj_s[rows, :] = gproj.astype(bf16)

    for n in range(2):
        cols = slice(256 * n, 256 * n + 256)
        ga_s[:, cols] = mm_nt(gproj_s[...], w_proj[cols, :]).astype(bf16)

    grad_k, grad_q = [], []
    for n, (w, b) in enumerate(pairs):
        rows = slice(64 * w, 64 * w + 64)
        wide = slice(256 * b, 256 * b + 256)
        vcols = slice(2 * ATT + 128 * b, 2 * ATT + 128 * b + 128)
        gabd = block_diagonal(ga_s[rows, 128 * b : 128 * b + 128])
        gprob = mm_nt(qkv_s[rows, vcols], gabd)
        gpack_s[rows, vcols] = mm(prob16_s[rows, wide], gabd).astype(bf16)
        prob = prob_s[rows, wide]
        gscore = prob * (gprob - col_total(prob * gprob))
        prob16_s[rows, wide] = gscore.astype(bf16)
    for n, (w, b) in enumerate(pairs):
        rows = slice(64 * w, 64 * w + 64)
        gscore = prob16_s[rows, 256 * b : 256 * b + 256]
        qcols = slice(128 * b, 128 * b + 128)
        kcols = slice(ATT + 128 * b, ATT + 128 * b + 128)
        gk = mm(gscore, qbd_s[256 * n : 256 * n + 256, :])
        gq = diagonal(mm_tn(gscore, unit16_s[rows, kcols])) * temper[:, qcols]
        proj_s[rows, qcols] = gq
        proj_s[rows, kcols] = gk
    for n in range(8):
        cols = slice(128 * n, 128 * n + 128)
        store_halves(n, unit_s[:, cols] * proj_s[:, cols])
    along = mm(seg_s[...], seg)
    for n in range(8):
        cols = slice(128 * n, 128 * n + 128)
        grad = inv_s[:, cols] * (proj_s[:, cols] - unit_s[:, cols] * along[cols])
        gpack_s[:, cols] = grad.astype(bf16)

    for n in range(4):
        cols = slice(256 * n, 256 * n + 256)
        total = (mixed_s[:, cols] + mm_nt(gpack_s[...], w_qkv[cols, :])).astype(bf16)
        for m, (_, ref, lo) in enumerate(quads):
            ref[lo : lo + 16, cols] = total[16 * m : 16 * m + 16]


def main(own, lon, lat, dia, *params):
    return pl.pallas_call(
        main_kernel,
        out_shape=[jax.ShapeDtypeStruct((n, D), bf16) for n in (48, 48, 16, 16)],
        scratch_shapes=[
            pltpu.VMEM((128, D), bf16),
            pltpu.VMEM((128, 3 * ATT), bf16),
            pltpu.VMEM((128, 2 * ATT), f32),
            pltpu.VMEM((128, 2 * ATT), f32),
            pltpu.VMEM((128, 2 * ATT), bf16),
            pltpu.VMEM((1024, 256), bf16),
            pltpu.VMEM((2048, 128), bf16),
            pltpu.VMEM((128, HEADS * CELLS), f32),
            pltpu.VMEM((128, HEADS * CELLS), bf16),
            pltpu.VMEM((128, ATT), bf16),
            pltpu.VMEM((128, D), f32),
            pltpu.VMEM((128, D), f32),
            pltpu.VMEM((128, D), bf16),
            pltpu.VMEM((128, ATT), bf16),
            pltpu.VMEM((128, 3 * ATT), bf16),
            pltpu.VMEM((16, D), f32),
        ],
        compiler_params=pltpu.CompilerParams(vmem_limit_bytes=24 * MIB),
        cost_estimate=pl.CostEstimate(
            flops=1_500_000_000, bytes_accessed=6_000_000, transcendentals=150_000
        ),
        name="main",
    )(own, lon, lat, dia, *params)


def final_kernel(own, lon, lat, dia, out):
    rows = jnp.concatenate([own[...], lon[...], lat[...], dia[...]], axis=0)
    row, col, _ = sorted_place(iota((128, 128), 1))
    token_place = onehot(iota((128, 128), 0) == row * 8 + col)
    out[...] = mm(token_place, rows).reshape(16, 8, D).astype(bf16)


def final(own, lon, lat, dia):
    return pl.pallas_call(
        final_kernel,
        out_shape=jax.ShapeDtypeStruct((16, 8, D), bf16),
        compiler_params=pltpu.CompilerParams(vmem_limit_bytes=8 * MIB),
        name="final",
    )(own, lon, lat, dia)


def shift_by(block, lat_step, lon_step):
    lats, lons = lax.axis_size("lat"), lax.axis_size("lon")
    route = [
        (j * lats + i, ((j + lon_step) % lons) * lats + (i + lat_step) % lats)
        for j in range(lons)
        for i in range(lats)
    ]
    return lax.ppermute(block, ("lon", "lat"), route)


def shards(
    tokens,
    labels,
    w_qkv,
    w_proj,
    logit_scale,
    bias_table,
    norm_gain,
    norm_shift,
    merge_gain,
    cotangent,
):
    own, lon, lat, dia = pack(tokens, labels.T, cotangent, places())
    lon = shift_by(lon, 0, 1)
    dia = shift_by(dia, -1, 1)
    lat = shift_by(lat, -1, 0)
    ebias, temper = prep(bias_table, logit_scale.reshape(1, HEADS))
    own, lon, lat, dia = main(
        own,
        lon,
        lat,
        dia,
        ebias,
        temper,
        w_qkv,
        w_proj,
        norm_gain.reshape(1, D),
        norm_shift.reshape(1, D),
        merge_gain.reshape(1, 4 * D),
    )
    lon = shift_by(lon, 0, -1)
    dia = shift_by(dia, 1, -1)
    lat = shift_by(lat, 1, 0)
    return final(own, lon, lat, dia)


def solution(mesh):
    placed = (
        P("lat", "lon", None),
        P("lat", "lon"),
        P(),
        P(),
        P(),
        P(),
        P(),
        P(),
        P(),
        P("lat", "lon", None),
    )
    return jax.shard_map(
        shards, mesh=mesh, in_specs=placed, out_specs=P("lat", "lon", None), check_vma=False
    )
```

```python
import math

import jax
import jax.numpy as jnp
from jax import lax
from jax.experimental import pallas as pl
from jax.experimental.pallas import tpu as pltpu
from jax.sharding import PartitionSpec as P

WIN = 8
D = 1024
HEADS = 16
ATT = 512
QUAD = 16
CELLS = 64
BLOCKS = 4
WIDE = 2 * D + 128

norm_eps = 1e-05
unit_eps = 1e-06
f32 = jnp.float32
bf16 = jnp.bfloat16
MIB = 1024 * 1024
BUSY = pl.CostEstimate(flops=10_000_000_000, bytes_accessed=30_000_000, transcendentals=0)


def sorted_place(n):
    quad = n // 16
    s = (n // 4) % 4
    g = n % 4
    row = 4 * (quad % 4) + 2 * (g // 2) + s % 2
    col = 4 * (quad // 4) + 2 * (g % 2) + s // 2
    return row, col, s


def window_place(n):
    row = 4 * (n // 32) + 2 * ((n // 2) % 2) + (n // 4) % 2
    col = 4 * ((n // 16) % 2) + 2 * (n % 2) + (n // 8) % 2
    return row, col


def iota(shape, axis):
    return lax.broadcasted_iota(jnp.int32, shape, axis)


def onehot(match):
    return match.astype(f32).astype(bf16)


def halves(value):
    high = value.astype(bf16)
    low = (value - high.astype(f32)).astype(bf16)
    return high, low


def mm(a, b):
    return jnp.dot(a, b, preferred_element_type=f32)


def mm_nt(a, b):
    return lax.dot_general(a, b, (((1,), (1,)), ((), ())), preferred_element_type=f32)


def mm_tn(a, b):
    return lax.dot_general(a, b, (((0,), (0,)), ((), ())), preferred_element_type=f32)


def places_kernel(token_sort, cot_sort, label_row, label_col):
    row, col, s = sorted_place(iota((128, 128), 0))
    lane = iota((128, 128), 1)
    token_sort[...] = onehot(lane == row * 8 + col)
    cot_sort[...] = onehot(lane == s * 32 + (row // 2) * 4 + col // 2)
    row, _, _ = sorted_place(iota((128, 16), 0))
    label_row[...] = (iota((128, 16), 1) == row).astype(f32)
    _, col, _ = sorted_place(iota((128, 8), 0))
    label_col[...] = onehot(iota((128, 8), 1) == col)


def places():
    return pl.pallas_call(
        places_kernel,
        out_shape=[
            jax.ShapeDtypeStruct((128, 128), bf16),
            jax.ShapeDtypeStruct((128, 128), bf16),
            jax.ShapeDtypeStruct((128, 16), f32),
            jax.ShapeDtypeStruct((128, 8), bf16),
        ],
        compiler_params=pltpu.CompilerParams(vmem_limit_bytes=8 * MIB),
        cost_estimate=BUSY,
        name="places",
    )()


def pack_kernel(
    token_sort, cot_sort, label_row, label_col, tokens, labels, cot, own, lon, cot_rows
):
    outs = ((own, 0, 64), (lon, 64, 128))
    moved = mm(token_sort[...], tokens[...].reshape(128, D)).astype(bf16)
    for ref, lo, hi in outs:
        ref[:, 0:D] = moved[lo:hi]
    first = lax.axis_index("lat") == 0
    code = labels[...] + jnp.where(iota((8, 16), 1) < 4, jnp.where(first, 4, 0), 0)
    spread = mm(label_col[...], code.astype(f32).astype(bf16)) * label_row[...]
    column = jnp.sum(spread, axis=1, keepdims=True)
    wide = jnp.broadcast_to(column, (128, 128)).astype(bf16)
    for ref, lo, hi in outs:
        ref[:, 2 * D :] = wide[lo:hi]
    for r in range(8):
        cot_rows[4 * r : 4 * r + 4, :] = cot[r].astype(f32)
    stacked = jnp.concatenate(
        [cot_rows[:, s * D : (s + 1) * D].astype(bf16) for s in range(4)], axis=0
    )
    moved_cot = mm(cot_sort[...], stacked).astype(bf16)
    for ref, lo, hi in outs:
        ref[:, D : 2 * D] = moved_cot[lo:hi]


def pack(tokens, labels, cot, sorts):
    shapes = [jax.ShapeDtypeStruct((64, WIDE), bf16)] * 2
    return pl.pallas_call(
        pack_kernel,
        out_shape=shapes,
        scratch_shapes=[pltpu.VMEM((32, 4 * D), f32)],
        compiler_params=pltpu.CompilerParams(vmem_limit_bytes=12 * MIB),
        cost_estimate=BUSY,
        name="pack",
    )(*sorts, tokens, labels, cot)


def strips_kernel(own, lon, top, bottom):
    top[0:16, :] = lon[0:16, :]
    top[16:32, :] = own[0:16, :]
    bottom[0:16, :] = lon[48:64, :]
    bottom[16:32, :] = own[48:64, :]


def strips(own, lon):
    return pl.pallas_call(
        strips_kernel,
        out_shape=[jax.ShapeDtypeStruct((32, WIDE), bf16)] * 2,
        compiler_params=pltpu.CompilerParams(vmem_limit_bytes=4 * MIB),
        name="strips",
    )(own, lon)


def relative_bias(table, natural, ebias):
    entry, place = iota((225, 256), 0), iota((225, 256), 1)
    table_spread = onehot((entry == 15 * (place // 16) + place % 16) & (place % 16 < 15))
    entry, place = iota((256, 512), 0), iota((256, 512), 1)
    row, col = window_place(place % 64)
    toeplitz = onehot(entry == 16 * (row - place // 64 + 7) + col)
    row, col = window_place(iota((64, 64), 0))
    row_order = onehot(iota((64, 64), 1) == row * 8 + col)
    gate = 16.0 / (1.0 + jnp.exp(-table))
    high, low = halves(gate)
    spread = mm(high, table_spread) + mm(low, table_spread)
    pieces = []
    for h in range(HEADS):
        line = jnp.broadcast_to(spread[h : h + 1, :], (8, 256))
        pieces.append(pltpu.roll(line, 249, 1, stride=1, stride_axis=0))
    high, low = halves(jnp.concatenate(pieces, axis=0))
    blocks = mm(high, toeplitz) + mm(low, toeplitz)
    left = iota((8, 128), 1) < 64
    for q in range(8):
        for p in range(4):
            even = blocks[16 * q : 16 * q + 8, 128 * p : 128 * p + 128]
            odd = blocks[16 * q + 8 : 16 * q + 16, 128 * p : 128 * p + 128]
            lanes = slice(128 * q, 128 * q + 128)
            natural[16 * p : 16 * p + 8, lanes] = jnp.where(left, even, pltpu.roll(odd, 64, 1))
            natural[16 * p + 8 : 16 * p + 16, lanes] = jnp.where(
                left, pltpu.roll(even, 64, 1), odd
            )
    high, low = halves(natural[...])
    ebias[...] = jnp.exp(mm(row_order, high) + mm(row_order, low))


def prep_kernel(table, scale, ebias, temper, natural):
    relative_bias(table[...], natural, ebias)
    per_head = jnp.exp(jnp.minimum(scale[...], math.log(100.0)))
    head_of = iota((1, ATT), 1) // 32
    line = jnp.zeros((1, ATT), f32)
    for h in range(HEADS):
        line = jnp.where(head_of == h, per_head[0:1, h : h + 1], line)
    temper[...] = line


def prep(table, scale):
    return pl.pallas_call(
        prep_kernel,
        out_shape=[
            jax.ShapeDtypeStruct((CELLS, HEADS * CELLS), f32),
            jax.ShapeDtypeStruct((1, ATT), f32),
        ],
        scratch_shapes=[pltpu.VMEM((CELLS, HEADS * CELLS), f32)],
        compiler_params=pltpu.CompilerParams(vmem_limit_bytes=12 * MIB),
        cost_estimate=pl.CostEstimate(
            flops=100_000_000, bytes_accessed=400_000, transcendentals=80_000
        ),
        name="prep",
    )(table, scale)


def group_total(column):
    pair = column[0:8] + column[8:16]
    pair = pair + pltpu.roll(pair, 4, 0)
    return jnp.concatenate([pair, pair], axis=0)


def row_total(value):
    return jnp.sum(value, axis=1, keepdims=True)


def col_total(value):
    return jnp.sum(value, axis=0, keepdims=True)


def windows(quads, kept, emit, params, scratch):
    ebias, temper, w_qkv, w_proj, gain, shift, merge = params
    (
        x_s,
        qkv_s,
        unit_s,
        inv_s,
        unit16_s,
        seg_s,
        qbd_s,
        prob_s,
        prob16_s,
        att_s,
        proj_s,
        mixed_s,
        gproj_s,
        ga_s,
        gpack_s,
        mgain,
    ) = scratch
    count = 16 * len(quads)
    pairs = [(w, b) for w in range(count // 64) for b in range(BLOCKS)]
    for n, (ref, lo) in enumerate(quads):
        x_s[16 * n : 16 * n + 16, :] = ref[lo : lo + 16, 0:D]
    for n in range(6):
        cols = slice(256 * n, 256 * n + 256)
        qkv_s[:, cols] = mm(x_s[...], w_qkv[:, cols]).astype(bf16)

    line, lane = iota((256, 128), 0), iota((256, 128), 1)
    seg = onehot((line % 128) // 32 == lane // 32)
    head_lane = iota((64, 128), 1) // 32
    head_mask = [onehot(head_lane == h) for h in range(4)]

    def store_halves(n, value):
        high, low = halves(value)
        seg_s[count * n : count * n + count, 0:128] = high
        seg_s[count * n : count * n + count, 128:256] = low

    def block_diagonal(value):
        return jnp.concatenate([value * head_mask[h] for h in range(4)], axis=0)

    def diagonal(value):
        out = value[192:256]
        for h in range(3):
            out = jnp.where(head_lane == h, value[64 * h : 64 * h + 64], out)
        return out

    for n in range(8):
        raw = qkv_s[:, 128 * n : 128 * n + 128].astype(f32)
        store_halves(n, raw * raw)
    squares = mm(seg_s[...], seg)
    for n in range(8):
        cols = slice(128 * n, 128 * n + 128)
        inv = lax.rsqrt(squares[count * n : count * n + count] + unit_eps)
        unit = qkv_s[:, cols].astype(f32) * inv
        inv_s[:, cols] = inv
        unit_s[:, cols] = unit
        if n < BLOCKS:
            unit = unit * temper[:, cols]
        unit16_s[:, cols] = unit.astype(bf16)

    code_lane = iota((16, 128), 1)
    allowed = []
    for w in range(count // 64):
        hot = jnp.concatenate(
            [
                onehot(ref[lo : lo + 16, 2 * D :].astype(f32).astype(jnp.int32) == code_lane)
                for ref, lo in quads[4 * w : 4 * w + 4]
            ],
            axis=0,
        )
        allowed.append(mm_nt(hot, jnp.concatenate([hot] * 4, axis=0)))
    for n, (w, b) in enumerate(pairs):
        rows = slice(64 * w, 64 * w + 64)
        wide = slice(256 * b, 256 * b + 256)
        qbd = block_diagonal(unit16_s[rows, 128 * b : 128 * b + 128])
        qbd_s[256 * n : 256 * n + 256, :] = qbd
        score = mm_nt(unit16_s[rows, ATT + 128 * b : ATT + 128 * b + 128], qbd)
        weight = jnp.exp(score) * ebias[:, wide] * allowed[w]
        prob = weight * (1.0 / col_total(weight))
        prob_s[rows, wide] = prob
        prob16_s[rows, wide] = prob.astype(bf16)
    for w, b in pairs:
        rows = slice(64 * w, 64 * w + 64)
        vals = qkv_s[rows, 2 * ATT + 128 * b : 2 * ATT + 128 * b + 128]
        att = diagonal(mm_tn(prob16_s[rows, 256 * b : 256 * b + 256], vals))
        att_s[rows, 128 * b : 128 * b + 128] = att.astype(bf16)

    for n in range(4):
        cols = slice(256 * n, 256 * n + 256)
        proj_s[:, cols] = mm(att_s[...], w_proj[:, cols])

    spans = [slice(16 * n, 16 * n + 16) for n in range(len(quads))]

    def ghat_of(n):
        ref, lo = quads[n]
        return ref[lo : lo + 16, D : 2 * D].astype(f32) * mgain[...]

    for s in range(4):
        mgain[4 * s : 4 * s + 4, :] = jnp.broadcast_to(merge[:, s * D : (s + 1) * D], (4, D))
    mean = [row_total(proj_s[rows, :]) * (1.0 / D) for rows in spans]
    inv_std = []
    for n, rows in enumerate(spans):
        centered = proj_s[rows, :] - mean[n]
        inv_std.append(lax.rsqrt(row_total(centered * centered) * (1.0 / D) + norm_eps))
    mean_m, mean_g = [], []
    for n, rows in enumerate(spans):
        normed = (proj_s[rows, :] - mean[n]) * inv_std[n]
        proj_s[rows, :] = normed
        mixed = x_s[rows, :].astype(f32) + normed * gain[...] + shift[...]
        mixed_s[rows, :] = mixed
        mean_m.append(group_total(row_total(mixed)) * (0.25 / D))
        mean_g.append(group_total(row_total(ghat_of(n))) * (0.25 / D))
    merge_inv, slope = [], []
    for n, rows in enumerate(spans):
        cent = mixed_s[rows, :] - mean_m[n]
        ghat = ghat_of(n)
        inv = lax.rsqrt(group_total(row_total(cent * cent)) * (0.25 / D) + norm_eps)
        merge_inv.append(inv)
        slope.append(group_total(row_total(ghat * cent)) * (0.25 / D) * inv * inv)
    mean_e, mean_en = [], []
    for n, rows in enumerate(spans):
        cent = mixed_s[rows, :] - mean_m[n]
        gmixed = merge_inv[n] * (ghat_of(n) - mean_g[n] - cent * slope[n])
        mixed_s[rows, :] = gmixed
        gnorm = gmixed * gain[...]
        mean_e.append(row_total(gnorm) * (1.0 / D))
        mean_en.append(row_total(gnorm * proj_s[rows, :]) * (1.0 / D))
    for n, rows in enumerate(spans):
        gnorm = mixed_s[rows, :] * gain[...]
        gproj = inv_std[n] * (gnorm - mean_e[n] - proj_s[rows, :] * mean_en[n])
        gproj_s[rows, :] = gproj.astype(bf16)

    for n in range(2):
        cols = slice(256 * n, 256 * n + 256)
        ga_s[:, cols] = mm_nt(gproj_s[...], w_proj[cols, :]).astype(bf16)

    grad_k, grad_q = [], []
    for n, (w, b) in enumerate(pairs):
        rows = slice(64 * w, 64 * w + 64)
        wide = slice(256 * b, 256 * b + 256)
        vcols = slice(2 * ATT + 128 * b, 2 * ATT + 128 * b + 128)
        gabd = block_diagonal(ga_s[rows, 128 * b : 128 * b + 128])
        gprob = mm_nt(qkv_s[rows, vcols], gabd)
        gpack_s[rows, vcols] = mm(prob16_s[rows, wide], gabd).astype(bf16)
        prob = prob_s[rows, wide]
        gscore = prob * (gprob - col_total(prob * gprob))
        prob16_s[rows, wide] = gscore.astype(bf16)
    for n, (w, b) in enumerate(pairs):
        rows = slice(64 * w, 64 * w + 64)
        gscore = prob16_s[rows, 256 * b : 256 * b + 256]
        qcols = slice(128 * b, 128 * b + 128)
        kcols = slice(ATT + 128 * b, ATT + 128 * b + 128)
        gk = mm(gscore, qbd_s[256 * n : 256 * n + 256, :])
        gq = diagonal(mm_tn(gscore, unit16_s[rows, kcols])) * temper[:, qcols]
        proj_s[rows, qcols] = gq
        proj_s[rows, kcols] = gk
    for n in range(8):
        cols = slice(128 * n, 128 * n + 128)
        store_halves(n, unit_s[:, cols] * proj_s[:, cols])
    along = mm(seg_s[...], seg)
    for n in range(8):
        cols = slice(128 * n, 128 * n + 128)
        grad = inv_s[:, cols] * (proj_s[:, cols] - unit_s[:, cols] * along[count * n : count * n + count])
        gpack_s[:, cols] = grad.astype(bf16)

    for n in range(4):
        cols = slice(256 * n, 256 * n + 256)
        total = mixed_s[kept, cols] + mm_nt(gpack_s[kept, :], w_qkv[cols, :])
        emit(cols, total.astype(bf16))


def scratch_for(count):
    return [
        pltpu.VMEM((count, D), bf16),
        pltpu.VMEM((count, 3 * ATT), bf16),
        pltpu.VMEM((count, 2 * ATT), f32),
        pltpu.VMEM((count, 2 * ATT), f32),
        pltpu.VMEM((count, 2 * ATT), bf16),
        pltpu.VMEM((8 * count, 256), bf16),
        pltpu.VMEM((16 * count, 128), bf16),
        pltpu.VMEM((count, HEADS * CELLS), f32),
        pltpu.VMEM((count, HEADS * CELLS), bf16),
        pltpu.VMEM((count, ATT), bf16),
        pltpu.VMEM((count, D), f32),
        pltpu.VMEM((count, D), f32),
        pltpu.VMEM((count, D), bf16),
        pltpu.VMEM((count, ATT), bf16),
        pltpu.VMEM((count, 3 * ATT), bf16),
        pltpu.VMEM((16, D), f32),
    ]


def inner_kernel(own, lon, *refs):
    params, (out_own, out_lon), scratch = refs[:7], refs[7:9], refs[9:]
    quads = ((lon, 16), (own, 16), (lon, 32), (own, 32))

    def emit(cols, total):
        out_lon[0:16, cols] = total[0:16]
        out_own[0:16, cols] = total[16:32]
        out_lon[16:32, cols] = total[32:48]
        out_own[16:32, cols] = total[48:64]

    windows(quads, slice(0, 64), emit, params, scratch)


def inner(own, lon, params):
    return pl.pallas_call(
        inner_kernel,
        out_shape=[jax.ShapeDtypeStruct((32, D), bf16)] * 2,
        scratch_shapes=scratch_for(64),
        compiler_params=pltpu.CompilerParams(vmem_limit_bytes=16 * MIB),
        cost_estimate=pl.CostEstimate(
            flops=3_000_000_000, bytes_accessed=6_000_000, transcendentals=150_000
        ),
        name="inner",
    )(own, lon, *params)


def outer_kernel(own, lon, above, below, in_own, in_lon, *refs):
    params, (out_own, out_lon), scratch = refs[:7], refs[7:9], refs[9:]
    quads = (
        (above, 0),
        (above, 16),
        (lon, 0),
        (own, 0),
        (lon, 48),
        (own, 48),
        (below, 0),
        (below, 16),
    )
    out_own[16:48, :] = in_own[...]
    out_lon[16:48, :] = in_lon[...]

    def emit(cols, total):
        out_lon[0:16, cols] = total[0:16]
        out_own[0:16, cols] = total[16:32]
        out_lon[48:64, cols] = total[32:48]
        out_own[48:64, cols] = total[48:64]

    windows(quads, slice(32, 96), emit, params, scratch)


def outer(own, lon, above, below, in_own, in_lon, params):
    return pl.pallas_call(
        outer_kernel,
        out_shape=[jax.ShapeDtypeStruct((64, D), bf16)] * 2,
        scratch_shapes=scratch_for(128),
        compiler_params=pltpu.CompilerParams(vmem_limit_bytes=24 * MIB),
        cost_estimate=pl.CostEstimate(
            flops=3_000_000_000, bytes_accessed=6_000_000, transcendentals=150_000
        ),
        name="outer",
    )(own, lon, above, below, in_own, in_lon, *params)


def final_kernel(own, lon, out):
    rows = jnp.concatenate([own[...], lon[...]], axis=0)
    row, col, _ = sorted_place(iota((128, 128), 1))
    token_place = onehot(iota((128, 128), 0) == row * 8 + col)
    out[...] = mm(token_place, rows).reshape(16, 8, D).astype(bf16)


def final(own, lon):
    return pl.pallas_call(
        final_kernel,
        out_shape=jax.ShapeDtypeStruct((16, 8, D), bf16),
        compiler_params=pltpu.CompilerParams(vmem_limit_bytes=8 * MIB),
        name="final",
    )(own, lon)


def passed_along(block, axis, distance):
    count = lax.axis_size(axis)
    route = [(i, (i + distance) % count) for i in range(count)]
    return lax.ppermute(block, axis, route)


def shards(
    tokens,
    labels,
    w_qkv,
    w_proj,
    logit_scale,
    bias_table,
    norm_gain,
    norm_shift,
    merge_gain,
    cotangent,
):
    own, lon = pack(tokens, labels.T, cotangent, places())
    lon = passed_along(lon, "lon", 1)
    ebias, temper = prep(bias_table, logit_scale.reshape(1, HEADS))
    params = (
        ebias,
        temper,
        w_qkv,
        w_proj,
        norm_gain.reshape(1, D),
        norm_shift.reshape(1, D),
        merge_gain.reshape(1, 4 * D),
    )
    top, bottom = strips(own, lon)
    below = passed_along(top, "lat", -1)
    above = passed_along(bottom, "lat", 1)
    in_own, in_lon = inner(own, lon, params)
    own, lon = outer(own, lon, above, below, in_own, in_lon, params)
    lon = passed_along(lon, "lon", -1)
    return final(own, lon)


def solution(mesh):
    placed = (
        P("lat", "lon", None),
        P("lat", "lon"),
        P(),
        P(),
        P(),
        P(),
        P(),
        P(),
        P(),
        P("lat", "lon", None),
    )
    return jax.shard_map(
        shards, mesh=mesh, in_specs=placed, out_specs=P("lat", "lon", None), check_vma=False
    )
```

```python
import math

import jax
import jax.numpy as jnp
from jax import lax
from jax.experimental import pallas as pl
from jax.experimental.pallas import tpu as pltpu
from jax.sharding import PartitionSpec as P

WIN = 8
D = 1024
HEADS = 16
ATT = 512
QUAD = 16
CELLS = 64
BLOCKS = 4
WIDE = 2 * D + 128

norm_eps = 1e-05
unit_eps = 1e-06
f32 = jnp.float32
bf16 = jnp.bfloat16
MIB = 1024 * 1024
BUSY = pl.CostEstimate(flops=10_000_000_000, bytes_accessed=30_000_000, transcendentals=0)


def sorted_place(n):
    quad = n // 16
    s = (n // 4) % 4
    g = n % 4
    row = jnp.where(quad < 6, 4 + 4 * (quad % 3), 0) + 2 * (g // 2) + s % 2
    col = jnp.where((quad // 3 == 1) | (quad == 7), 4, 0) + 2 * (g % 2) + s // 2
    return row, col, s


def window_place(n):
    row = 4 * (n // 32) + 2 * ((n // 2) % 2) + (n // 4) % 2
    col = 4 * ((n // 16) % 2) + 2 * (n % 2) + (n // 8) % 2
    return row, col


def iota(shape, axis):
    return lax.broadcasted_iota(jnp.int32, shape, axis)


def onehot(match):
    return match.astype(f32).astype(bf16)


def halves(value):
    high = value.astype(bf16)
    low = (value - high.astype(f32)).astype(bf16)
    return high, low


def mm(a, b):
    return jnp.dot(a, b, preferred_element_type=f32)


def mm_nt(a, b):
    return lax.dot_general(a, b, (((1,), (1,)), ((), ())), preferred_element_type=f32)


def mm_tn(a, b):
    return lax.dot_general(a, b, (((0,), (0,)), ((), ())), preferred_element_type=f32)


def places_kernel(token_sort, cot_sort, label_row, label_col):
    row, col, s = sorted_place(iota((128, 128), 0))
    lane = iota((128, 128), 1)
    token_sort[...] = onehot(lane == row * 8 + col)
    cot_sort[...] = onehot(lane == s * 32 + (row // 2) * 4 + col // 2)
    row, _, _ = sorted_place(iota((128, 16), 0))
    label_row[...] = (iota((128, 16), 1) == row).astype(f32)
    _, col, _ = sorted_place(iota((128, 8), 0))
    label_col[...] = onehot(iota((128, 8), 1) == col)


def places():
    return pl.pallas_call(
        places_kernel,
        out_shape=[
            jax.ShapeDtypeStruct((128, 128), bf16),
            jax.ShapeDtypeStruct((128, 128), bf16),
            jax.ShapeDtypeStruct((128, 16), f32),
            jax.ShapeDtypeStruct((128, 8), bf16),
        ],
        compiler_params=pltpu.CompilerParams(vmem_limit_bytes=8 * MIB),
        cost_estimate=BUSY,
        name="places",
    )()


def pack_kernel(
    token_sort, cot_sort, label_row, label_col, tokens, labels, cot, own, lon, lat, dia, cot_rows
):
    outs = ((own, 0, 48), (lon, 48, 96), (lat, 96, 112), (dia, 112, 128))
    moved = mm(token_sort[...], tokens[...].reshape(128, D)).astype(bf16)
    for ref, lo, hi in outs:
        ref[:, 0:D] = moved[lo:hi]
    first = lax.axis_index("lat") == 0
    code = labels[...] + jnp.where(iota((8, 16), 1) < 4, jnp.where(first, 4, 0), 0)
    spread = mm(label_col[...], code.astype(f32).astype(bf16)) * label_row[...]
    column = jnp.sum(spread, axis=1, keepdims=True)
    wide = jnp.broadcast_to(column, (128, 128)).astype(bf16)
    for ref, lo, hi in outs:
        ref[:, 2 * D :] = wide[lo:hi]
    for r in range(8):
        cot_rows[4 * r : 4 * r + 4, :] = cot[r].astype(f32)
    stacked = jnp.concatenate(
        [cot_rows[:, s * D : (s + 1) * D].astype(bf16) for s in range(4)], axis=0
    )
    moved_cot = mm(cot_sort[...], stacked).astype(bf16)
    for ref, lo, hi in outs:
        ref[:, D : 2 * D] = moved_cot[lo:hi]


def pack(tokens, labels, cot, sorts):
    shapes = [jax.ShapeDtypeStruct((n, WIDE), bf16) for n in (48, 48, 16, 16)]
    return pl.pallas_call(
        pack_kernel,
        out_shape=shapes,
        scratch_shapes=[pltpu.VMEM((32, 4 * D), f32)],
        compiler_params=pltpu.CompilerParams(vmem_limit_bytes=12 * MIB),
        cost_estimate=BUSY,
        name="pack",
    )(*sorts, tokens, labels, cot)


def relative_bias(table, natural, ebias):
    entry, place = iota((225, 256), 0), iota((225, 256), 1)
    table_spread = onehot((entry == 15 * (place // 16) + place % 16) & (place % 16 < 15))
    entry, place = iota((256, 512), 0), iota((256, 512), 1)
    row, col = window_place(place % 64)
    toeplitz = onehot(entry == 16 * (row - place // 64 + 7) + col)
    row, col = window_place(iota((64, 64), 0))
    row_order = onehot(iota((64, 64), 1) == row * 8 + col)
    gate = 16.0 / (1.0 + jnp.exp(-table))
    high, low = halves(gate)
    spread = mm(high, table_spread) + mm(low, table_spread)
    pieces = []
    for h in range(HEADS):
        line = jnp.broadcast_to(spread[h : h + 1, :], (8, 256))
        pieces.append(pltpu.roll(line, 249, 1, stride=1, stride_axis=0))
    high, low = halves(jnp.concatenate(pieces, axis=0))
    blocks = mm(high, toeplitz) + mm(low, toeplitz)
    left = iota((8, 128), 1) < 64
    for q in range(8):
        for p in range(4):
            even = blocks[16 * q : 16 * q + 8, 128 * p : 128 * p + 128]
            odd = blocks[16 * q + 8 : 16 * q + 16, 128 * p : 128 * p + 128]
            lanes = slice(128 * q, 128 * q + 128)
            natural[16 * p : 16 * p + 8, lanes] = jnp.where(left, even, pltpu.roll(odd, 64, 1))
            natural[16 * p + 8 : 16 * p + 16, lanes] = jnp.where(
                left, pltpu.roll(even, 64, 1), odd
            )
    high, low = halves(natural[...])
    ebias[...] = jnp.exp(mm(row_order, high) + mm(row_order, low))


def prep_kernel(table, scale, ebias, temper, natural):
    relative_bias(table[...], natural, ebias)
    per_head = jnp.exp(jnp.minimum(scale[...], math.log(100.0)))
    head_of = iota((1, ATT), 1) // 32
    line = jnp.zeros((1, ATT), f32)
    for h in range(HEADS):
        line = jnp.where(head_of == h, per_head[0:1, h : h + 1], line)
    temper[...] = line


def prep(table, scale):
    return pl.pallas_call(
        prep_kernel,
        out_shape=[
            jax.ShapeDtypeStruct((CELLS, HEADS * CELLS), f32),
            jax.ShapeDtypeStruct((1, ATT), f32),
        ],
        scratch_shapes=[pltpu.VMEM((CELLS, HEADS * CELLS), f32)],
        compiler_params=pltpu.CompilerParams(vmem_limit_bytes=12 * MIB),
        cost_estimate=pl.CostEstimate(
            flops=100_000_000, bytes_accessed=400_000, transcendentals=80_000
        ),
        name="prep",
    )(table, scale)


def group_total(column):
    pair = column[0:8] + column[8:16]
    pair = pair + pltpu.roll(pair, 4, 0)
    return jnp.concatenate([pair, pair], axis=0)


def row_total(value):
    return jnp.sum(value, axis=1, keepdims=True)


def col_total(value):
    return jnp.sum(value, axis=0, keepdims=True)


def main_kernel(
    own,
    lon,
    dia,
    lat,
    ebias,
    temper,
    w_qkv,
    w_proj,
    gain,
    shift,
    merge,
    out_own,
    out_lon,
    out_lat,
    out_dia,
    x_s,
    qkv_s,
    unit_s,
    inv_s,
    unit16_s,
    seg_s,
    qbd_s,
    prob_s,
    prob16_s,
    att_s,
    proj_s,
    mixed_s,
    gproj_s,
    ga_s,
    gpack_s,
    mgain,
):
    quads = (
        (lon, out_lon, 0),
        (own, out_own, 0),
        (lon, out_lon, 16),
        (own, out_own, 16),
        (lon, out_lon, 32),
        (own, out_own, 32),
        (dia, out_dia, 0),
        (lat, out_lat, 0),
    )
    pairs = [(w, b) for w in range(2) for b in range(BLOCKS)]
    for n, (ref, _, lo) in enumerate(quads):
        x_s[16 * n : 16 * n + 16, :] = ref[lo : lo + 16, 0:D]
    for n in range(6):
        cols = slice(256 * n, 256 * n + 256)
        qkv_s[:, cols] = mm(x_s[...], w_qkv[:, cols]).astype(bf16)

    line, lane = iota((256, 128), 0), iota((256, 128), 1)
    seg = onehot((line % 128) // 32 == lane // 32)
    head_lane = iota((64, 128), 1) // 32
    head_mask = [onehot(head_lane == h) for h in range(4)]

    def store_halves(n, value):
        high, low = halves(value)
        seg_s[128 * n : 128 * n + 128, 0:128] = high
        seg_s[128 * n : 128 * n + 128, 128:256] = low

    def block_diagonal(value):
        return jnp.concatenate([value * head_mask[h] for h in range(4)], axis=0)

    def diagonal(value):
        out = value[192:256]
        for h in range(3):
            out = jnp.where(head_lane == h, value[64 * h : 64 * h + 64], out)
        return out

    for n in range(8):
        raw = qkv_s[:, 128 * n : 128 * n + 128].astype(f32)
        store_halves(n, raw * raw)
    squares = mm(seg_s[...], seg)
    for n in range(8):
        cols = slice(128 * n, 128 * n + 128)
        inv = lax.rsqrt(squares[cols] + unit_eps)
        unit = qkv_s[:, cols].astype(f32) * inv
        inv_s[:, cols] = inv
        unit_s[:, cols] = unit
        if n < BLOCKS:
            unit = unit * temper[:, cols]
        unit16_s[:, cols] = unit.astype(bf16)

    code_lane = iota((16, 128), 1)
    allowed = []
    for w in range(2):
        hot = jnp.concatenate(
            [
                onehot(ref[lo : lo + 16, 2 * D :].astype(f32).astype(jnp.int32) == code_lane)
                for ref, _, lo in quads[4 * w : 4 * w + 4]
            ],
            axis=0,
        )
        allowed.append(mm_nt(hot, jnp.concatenate([hot] * 4, axis=0)))
    for n, (w, b) in enumerate(pairs):
        rows = slice(64 * w, 64 * w + 64)
        wide = slice(256 * b, 256 * b + 256)
        qbd = block_diagonal(unit16_s[rows, 128 * b : 128 * b + 128])
        qbd_s[256 * n : 256 * n + 256, :] = qbd
        score = mm_nt(unit16_s[rows, ATT + 128 * b : ATT + 128 * b + 128], qbd)
        weight = jnp.exp(score) * ebias[:, wide] * allowed[w]
        prob = weight * (1.0 / col_total(weight))
        prob_s[rows, wide] = prob
        prob16_s[rows, wide] = prob.astype(bf16)
    for w, b in pairs:
        rows = slice(64 * w, 64 * w + 64)
        vals = qkv_s[rows, 2 * ATT + 128 * b : 2 * ATT + 128 * b + 128]
        att = diagonal(mm_tn(prob16_s[rows, 256 * b : 256 * b + 256], vals))
        att_s[rows, 128 * b : 128 * b + 128] = att.astype(bf16)

    for n in range(4):
        cols = slice(256 * n, 256 * n + 256)
        proj_s[:, cols] = mm(att_s[...], w_proj[:, cols])

    spans = [slice(16 * n, 16 * n + 16) for n in range(8)]

    def ghat_of(n):
        ref, _, lo = quads[n]
        return ref[lo : lo + 16, D : 2 * D].astype(f32) * mgain[...]

    for s in range(4):
        mgain[4 * s : 4 * s + 4, :] = jnp.broadcast_to(merge[:, s * D : (s + 1) * D], (4, D))
    mean = [row_total(proj_s[rows, :]) * (1.0 / D) for rows in spans]
    inv_std = []
    for n, rows in enumerate(spans):
        centered = proj_s[rows, :] - mean[n]
        inv_std.append(lax.rsqrt(row_total(centered * centered) * (1.0 / D) + norm_eps))
    mean_m, mean_g = [], []
    for n, rows in enumerate(spans):
        normed = (proj_s[rows, :] - mean[n]) * inv_std[n]
        proj_s[rows, :] = normed
        mixed = x_s[rows, :].astype(f32) + normed * gain[...] + shift[...]
        mixed_s[rows, :] = mixed
        mean_m.append(group_total(row_total(mixed)) * (0.25 / D))
        mean_g.append(group_total(row_total(ghat_of(n))) * (0.25 / D))
    merge_inv, slope = [], []
    for n, rows in enumerate(spans):
        cent = mixed_s[rows, :] - mean_m[n]
        ghat = ghat_of(n)
        inv = lax.rsqrt(group_total(row_total(cent * cent)) * (0.25 / D) + norm_eps)
        merge_inv.append(inv)
        slope.append(group_total(row_total(ghat * cent)) * (0.25 / D) * inv * inv)
    mean_e, mean_en = [], []
    for n, rows in enumerate(spans):
        cent = mixed_s[rows, :] - mean_m[n]
        gmixed = merge_inv[n] * (ghat_of(n) - mean_g[n] - cent * slope[n])
        mixed_s[rows, :] = gmixed
        gnorm = gmixed * gain[...]
        mean_e.append(row_total(gnorm) * (1.0 / D))
        mean_en.append(row_total(gnorm * proj_s[rows, :]) * (1.0 / D))
    for n, rows in enumerate(spans):
        gnorm = mixed_s[rows, :] * gain[...]
        gproj = inv_std[n] * (gnorm - mean_e[n] - proj_s[rows, :] * mean_en[n])
        gproj_s[rows, :] = gproj.astype(bf16)

    for n in range(2):
        cols = slice(256 * n, 256 * n + 256)
        ga_s[:, cols] = mm_nt(gproj_s[...], w_proj[cols, :]).astype(bf16)

    grad_k, grad_q = [], []
    for n, (w, b) in enumerate(pairs):
        rows = slice(64 * w, 64 * w + 64)
        wide = slice(256 * b, 256 * b + 256)
        vcols = slice(2 * ATT + 128 * b, 2 * ATT + 128 * b + 128)
        gabd = block_diagonal(ga_s[rows, 128 * b : 128 * b + 128])
        gprob = mm_nt(qkv_s[rows, vcols], gabd)
        gpack_s[rows, vcols] = mm(prob16_s[rows, wide], gabd).astype(bf16)
        prob = prob_s[rows, wide]
        gscore = prob * (gprob - col_total(prob * gprob))
        prob16_s[rows, wide] = gscore.astype(bf16)
    for n, (w, b) in enumerate(pairs):
        rows = slice(64 * w, 64 * w + 64)
        gscore = prob16_s[rows, 256 * b : 256 * b + 256]
        qcols = slice(128 * b, 128 * b + 128)
        kcols = slice(ATT + 128 * b, ATT + 128 * b + 128)
        gk = mm(gscore, qbd_s[256 * n : 256 * n + 256, :])
        gq = diagonal(mm_tn(gscore, unit16_s[rows, kcols])) * temper[:, qcols]
        proj_s[rows, qcols] = gq
        proj_s[rows, kcols] = gk
    for n in range(8):
        cols = slice(128 * n, 128 * n + 128)
        store_halves(n, unit_s[:, cols] * proj_s[:, cols])
    along = mm(seg_s[...], seg)
    for n in range(8):
        cols = slice(128 * n, 128 * n + 128)
        grad = inv_s[:, cols] * (proj_s[:, cols] - unit_s[:, cols] * along[cols])
        gpack_s[:, cols] = grad.astype(bf16)

    for n in range(4):
        cols = slice(256 * n, 256 * n + 256)
        total = (mixed_s[:, cols] + mm_nt(gpack_s[...], w_qkv[cols, :])).astype(bf16)
        for m, (_, ref, lo) in enumerate(quads):
            ref[lo : lo + 16, cols] = total[16 * m : 16 * m + 16]


def main(own, lon, dia, lat, *params):
    return pl.pallas_call(
        main_kernel,
        out_shape=[jax.ShapeDtypeStruct((n, D), bf16) for n in (48, 48, 16, 16)],
        scratch_shapes=[
            pltpu.VMEM((128, D), bf16),
            pltpu.VMEM((128, 3 * ATT), bf16),
            pltpu.VMEM((128, 2 * ATT), f32),
            pltpu.VMEM((128, 2 * ATT), f32),
            pltpu.VMEM((128, 2 * ATT), bf16),
            pltpu.VMEM((1024, 256), bf16),
            pltpu.VMEM((2048, 128), bf16),
            pltpu.VMEM((128, HEADS * CELLS), f32),
            pltpu.VMEM((128, HEADS * CELLS), bf16),
            pltpu.VMEM((128, ATT), bf16),
            pltpu.VMEM((128, D), f32),
            pltpu.VMEM((128, D), f32),
            pltpu.VMEM((128, D), bf16),
            pltpu.VMEM((128, ATT), bf16),
            pltpu.VMEM((128, 3 * ATT), bf16),
            pltpu.VMEM((16, D), f32),
        ],
        compiler_params=pltpu.CompilerParams(vmem_limit_bytes=24 * MIB),
        cost_estimate=pl.CostEstimate(
            flops=1_500_000_000, bytes_accessed=6_000_000, transcendentals=150_000
        ),
        name="main",
    )(own, lon, dia, lat, *params)


def final_kernel(own, lat, lon, dia, out):
    rows = jnp.concatenate([own[...], lon[...], lat[...], dia[...]], axis=0)
    row, col, _ = sorted_place(iota((128, 128), 1))
    token_place = onehot(iota((128, 128), 0) == row * 8 + col)
    out[...] = mm(token_place, rows).reshape(16, 8, D).astype(bf16)


def final(own, lon, lat, dia):
    return pl.pallas_call(
        final_kernel,
        out_shape=jax.ShapeDtypeStruct((16, 8, D), bf16),
        compiler_params=pltpu.CompilerParams(vmem_limit_bytes=8 * MIB),
        name="final",
    )(own, lat, lon, dia)


def shift_by(block, lat_step, lon_step):
    lats, lons = lax.axis_size("lat"), lax.axis_size("lon")
    route = [
        (j * lats + i, ((j + lon_step) % lons) * lats + (i + lat_step) % lats)
        for j in range(lons)
        for i in range(lats)
    ]
    return lax.ppermute(block, ("lon", "lat"), route)


def shards(
    tokens,
    labels,
    w_qkv,
    w_proj,
    logit_scale,
    bias_table,
    norm_gain,
    norm_shift,
    merge_gain,
    cotangent,
):
    own, lon, lat, dia = pack(tokens, labels.T, cotangent, places())
    lon = shift_by(lon, 0, 1)
    dia = shift_by(dia, -1, 1)
    lat = shift_by(lat, -1, 0)
    ebias, temper = prep(bias_table, logit_scale.reshape(1, HEADS))
    own, lon, lat, dia = main(
        own,
        lon,
        dia,
        lat,
        ebias,
        temper,
        w_qkv,
        w_proj,
        norm_gain.reshape(1, D),
        norm_shift.reshape(1, D),
        merge_gain.reshape(1, 4 * D),
    )
    lon = shift_by(lon, 0, -1)
    dia = shift_by(dia, 1, -1)
    lat = shift_by(lat, 1, 0)
    return final(own, lon, lat, dia)


def solution(mesh):
    placed = (
        P("lat", "lon", None),
        P("lat", "lon"),
        P(),
        P(),
        P(),
        P(),
        P(),
        P(),
        P(),
        P("lat", "lon", None),
    )
    return jax.shard_map(
        shards, mesh=mesh, in_specs=placed, out_specs=P("lat", "lon", None), check_vma=False
    )
```

```python
import math

import jax
import jax.numpy as jnp
from jax import lax
from jax.experimental import pallas as pl
from jax.experimental.pallas import tpu as pltpu
from jax.sharding import PartitionSpec as P

WIN = 8
D = 1024
HEADS = 16
ATT = 512
QUAD = 16
CELLS = 64
BLOCKS = 4
WIDE = 2 * D + 128

norm_eps = 1e-05
unit_eps = 1e-06
f32 = jnp.float32
bf16 = jnp.bfloat16
MIB = 1024 * 1024
BUSY = pl.CostEstimate(flops=10_000_000_000, bytes_accessed=30_000_000, transcendentals=0)


def sorted_place(n):
    quad = n // 16
    s = (n // 4) % 4
    g = n % 4
    row = 4 * (quad % 4) + 2 * (g // 2) + s % 2
    col = 4 * (quad // 4) + 2 * (g % 2) + s // 2
    return row, col, s


def window_place(n):
    row = 4 * (n // 32) + 2 * ((n // 2) % 2) + (n // 4) % 2
    col = 4 * ((n // 16) % 2) + 2 * (n % 2) + (n // 8) % 2
    return row, col


def iota(shape, axis):
    return lax.broadcasted_iota(jnp.int32, shape, axis)


def onehot(match):
    return match.astype(f32).astype(bf16)


def halves(value):
    high = value.astype(bf16)
    low = (value - high.astype(f32)).astype(bf16)
    return high, low


def mm(a, b):
    return jnp.dot(a, b, preferred_element_type=f32)


def mm_nt(a, b):
    return lax.dot_general(a, b, (((1,), (1,)), ((), ())), preferred_element_type=f32)


def mm_tn(a, b):
    return lax.dot_general(a, b, (((0,), (0,)), ((), ())), preferred_element_type=f32)


def places_kernel(token_sort, cot_sort, label_row, label_col):
    row, col, s = sorted_place(iota((128, 128), 0))
    lane = iota((128, 128), 1)
    token_sort[...] = onehot(lane == row * 8 + col)
    cot_sort[...] = onehot(lane == s * 32 + (row // 2) * 4 + col // 2)
    row, _, _ = sorted_place(iota((128, 16), 0))
    label_row[...] = (iota((128, 16), 1) == row).astype(f32)
    _, col, _ = sorted_place(iota((128, 8), 0))
    label_col[...] = onehot(iota((128, 8), 1) == col)


def places():
    return pl.pallas_call(
        places_kernel,
        out_shape=[
            jax.ShapeDtypeStruct((128, 128), bf16),
            jax.ShapeDtypeStruct((128, 128), bf16),
            jax.ShapeDtypeStruct((128, 16), f32),
            jax.ShapeDtypeStruct((128, 8), bf16),
        ],
        compiler_params=pltpu.CompilerParams(vmem_limit_bytes=8 * MIB),
        cost_estimate=BUSY,
        name="places",
    )()


def pack_kernel(
    token_sort, cot_sort, label_row, label_col, tokens, labels, cot, own, lon, cot_rows
):
    outs = ((own, 0, 64), (lon, 64, 128))
    moved = mm(token_sort[...], tokens[...].reshape(128, D)).astype(bf16)
    for ref, lo, hi in outs:
        ref[:, 0:D] = moved[lo:hi]
    first = lax.axis_index("lat") == 0
    code = labels[...] + jnp.where(iota((8, 16), 1) < 4, jnp.where(first, 4, 0), 0)
    spread = mm(label_col[...], code.astype(f32).astype(bf16)) * label_row[...]
    column = jnp.sum(spread, axis=1, keepdims=True)
    wide = jnp.broadcast_to(column, (128, 128)).astype(bf16)
    for ref, lo, hi in outs:
        ref[:, 2 * D :] = wide[lo:hi]
    for r in range(8):
        cot_rows[4 * r : 4 * r + 4, :] = cot[r].astype(f32)
    stacked = jnp.concatenate(
        [cot_rows[:, s * D : (s + 1) * D].astype(bf16) for s in range(4)], axis=0
    )
    moved_cot = mm(cot_sort[...], stacked).astype(bf16)
    for ref, lo, hi in outs:
        ref[:, D : 2 * D] = moved_cot[lo:hi]


def pack(tokens, labels, cot, sorts):
    shapes = [jax.ShapeDtypeStruct((64, WIDE), bf16)] * 2
    return pl.pallas_call(
        pack_kernel,
        out_shape=shapes,
        scratch_shapes=[pltpu.VMEM((32, 4 * D), f32)],
        compiler_params=pltpu.CompilerParams(vmem_limit_bytes=12 * MIB),
        cost_estimate=BUSY,
        name="pack",
    )(*sorts, tokens, labels, cot)


def strips_kernel(own, lon, to_first, to_second):
    odd = lax.axis_index("lat") % 2 == 1
    for n, ref in enumerate((lon, own)):
        rows = slice(16 * n, 16 * n + 16)
        top, bottom = ref[0:16, :], ref[48:64, :]
        to_first[rows, :] = jnp.where(odd, top, bottom)
        to_second[rows, :] = jnp.where(odd, bottom, top)


def strips(own, lon):
    return pl.pallas_call(
        strips_kernel,
        out_shape=[jax.ShapeDtypeStruct((32, WIDE), bf16)] * 2,
        compiler_params=pltpu.CompilerParams(vmem_limit_bytes=4 * MIB),
        name="strips",
    )(own, lon)


def relative_bias(table, natural, ebias):
    entry, place = iota((225, 256), 0), iota((225, 256), 1)
    table_spread = onehot((entry == 15 * (place // 16) + place % 16) & (place % 16 < 15))
    entry, place = iota((256, 512), 0), iota((256, 512), 1)
    row, col = window_place(place % 64)
    toeplitz = onehot(entry == 16 * (row - place // 64 + 7) + col)
    row, col = window_place(iota((64, 64), 0))
    row_order = onehot(iota((64, 64), 1) == row * 8 + col)
    gate = 16.0 / (1.0 + jnp.exp(-table))
    high, low = halves(gate)
    spread = mm(high, table_spread) + mm(low, table_spread)
    pieces = []
    for h in range(HEADS):
        line = jnp.broadcast_to(spread[h : h + 1, :], (8, 256))
        pieces.append(pltpu.roll(line, 249, 1, stride=1, stride_axis=0))
    high, low = halves(jnp.concatenate(pieces, axis=0))
    blocks = mm(high, toeplitz) + mm(low, toeplitz)
    left = iota((8, 128), 1) < 64
    for q in range(8):
        for p in range(4):
            even = blocks[16 * q : 16 * q + 8, 128 * p : 128 * p + 128]
            odd = blocks[16 * q + 8 : 16 * q + 16, 128 * p : 128 * p + 128]
            lanes = slice(128 * q, 128 * q + 128)
            natural[16 * p : 16 * p + 8, lanes] = jnp.where(left, even, pltpu.roll(odd, 64, 1))
            natural[16 * p + 8 : 16 * p + 16, lanes] = jnp.where(
                left, pltpu.roll(even, 64, 1), odd
            )
    high, low = halves(natural[...])
    ebias[...] = jnp.exp(mm(row_order, high) + mm(row_order, low))


def prep_kernel(table, scale, ebias, temper, natural):
    relative_bias(table[...], natural, ebias)
    per_head = jnp.exp(jnp.minimum(scale[...], math.log(100.0)))
    head_of = iota((1, ATT), 1) // 32
    line = jnp.zeros((1, ATT), f32)
    for h in range(HEADS):
        line = jnp.where(head_of == h, per_head[0:1, h : h + 1], line)
    temper[...] = line


def prep(table, scale):
    return pl.pallas_call(
        prep_kernel,
        out_shape=[
            jax.ShapeDtypeStruct((CELLS, HEADS * CELLS), f32),
            jax.ShapeDtypeStruct((1, ATT), f32),
        ],
        scratch_shapes=[pltpu.VMEM((CELLS, HEADS * CELLS), f32)],
        compiler_params=pltpu.CompilerParams(vmem_limit_bytes=12 * MIB),
        cost_estimate=pl.CostEstimate(
            flops=100_000_000, bytes_accessed=400_000, transcendentals=80_000
        ),
        name="prep",
    )(table, scale)


def group_total(column):
    pair = column[0:8] + column[8:16]
    pair = pair + pltpu.roll(pair, 4, 0)
    return jnp.concatenate([pair, pair], axis=0)


def row_total(value):
    return jnp.sum(value, axis=1, keepdims=True)


def col_total(value):
    return jnp.sum(value, axis=0, keepdims=True)


def windows(quads, kept, emit, params, scratch):
    ebias, temper, w_qkv, w_proj, gain, shift, merge = params
    (
        x_s,
        qkv_s,
        unit_s,
        inv_s,
        unit16_s,
        seg_s,
        qbd_s,
        prob_s,
        prob16_s,
        att_s,
        proj_s,
        mixed_s,
        gproj_s,
        ga_s,
        gpack_s,
        mgain,
    ) = scratch
    count = 16 * len(quads)
    pairs = [(w, b) for w in range(count // 64) for b in range(BLOCKS)]
    for n, (ref, lo) in enumerate(quads):
        x_s[16 * n : 16 * n + 16, :] = ref[lo : lo + 16, 0:D]
    for n in range(6):
        cols = slice(256 * n, 256 * n + 256)
        qkv_s[:, cols] = mm(x_s[...], w_qkv[:, cols]).astype(bf16)

    line, lane = iota((256, 128), 0), iota((256, 128), 1)
    seg = onehot((line % 128) // 32 == lane // 32)
    head_lane = iota((64, 128), 1) // 32
    head_mask = [onehot(head_lane == h) for h in range(4)]

    def store_halves(n, value):
        high, low = halves(value)
        seg_s[count * n : count * n + count, 0:128] = high
        seg_s[count * n : count * n + count, 128:256] = low

    def block_diagonal(value):
        return jnp.concatenate([value * head_mask[h] for h in range(4)], axis=0)

    def diagonal(value):
        out = value[192:256]
        for h in range(3):
            out = jnp.where(head_lane == h, value[64 * h : 64 * h + 64], out)
        return out

    for n in range(8):
        raw = qkv_s[:, 128 * n : 128 * n + 128].astype(f32)
        store_halves(n, raw * raw)
    squares = mm(seg_s[...], seg)
    for n in range(8):
        cols = slice(128 * n, 128 * n + 128)
        inv = lax.rsqrt(squares[count * n : count * n + count] + unit_eps)
        unit = qkv_s[:, cols].astype(f32) * inv
        inv_s[:, cols] = inv
        unit_s[:, cols] = unit
        if n < BLOCKS:
            unit = unit * temper[:, cols]
        unit16_s[:, cols] = unit.astype(bf16)

    code_lane = iota((16, 128), 1)
    allowed = []
    for w in range(count // 64):
        hot = jnp.concatenate(
            [
                onehot(ref[lo : lo + 16, 2 * D :].astype(f32).astype(jnp.int32) == code_lane)
                for ref, lo in quads[4 * w : 4 * w + 4]
            ],
            axis=0,
        )
        allowed.append(mm_nt(hot, jnp.concatenate([hot] * 4, axis=0)))
    for n, (w, b) in enumerate(pairs):
        rows = slice(64 * w, 64 * w + 64)
        wide = slice(256 * b, 256 * b + 256)
        qbd = block_diagonal(unit16_s[rows, 128 * b : 128 * b + 128])
        qbd_s[256 * n : 256 * n + 256, :] = qbd
        score = mm_nt(unit16_s[rows, ATT + 128 * b : ATT + 128 * b + 128], qbd)
        weight = jnp.exp(score) * ebias[:, wide] * allowed[w]
        prob = weight * (1.0 / col_total(weight))
        prob_s[rows, wide] = prob
        prob16_s[rows, wide] = prob.astype(bf16)
    for w, b in pairs:
        rows = slice(64 * w, 64 * w + 64)
        vals = qkv_s[rows, 2 * ATT + 128 * b : 2 * ATT + 128 * b + 128]
        att = diagonal(mm_tn(prob16_s[rows, 256 * b : 256 * b + 256], vals))
        att_s[rows, 128 * b : 128 * b + 128] = att.astype(bf16)

    for n in range(4):
        cols = slice(256 * n, 256 * n + 256)
        proj_s[:, cols] = mm(att_s[...], w_proj[:, cols])

    spans = [slice(16 * n, 16 * n + 16) for n in range(len(quads))]

    def ghat_of(n):
        ref, lo = quads[n]
        return ref[lo : lo + 16, D : 2 * D].astype(f32) * mgain[...]

    for s in range(4):
        mgain[4 * s : 4 * s + 4, :] = jnp.broadcast_to(merge[:, s * D : (s + 1) * D], (4, D))
    mean = [row_total(proj_s[rows, :]) * (1.0 / D) for rows in spans]
    inv_std = []
    for n, rows in enumerate(spans):
        centered = proj_s[rows, :] - mean[n]
        inv_std.append(lax.rsqrt(row_total(centered * centered) * (1.0 / D) + norm_eps))
    mean_m, mean_g = [], []
    for n, rows in enumerate(spans):
        normed = (proj_s[rows, :] - mean[n]) * inv_std[n]
        proj_s[rows, :] = normed
        mixed = x_s[rows, :].astype(f32) + normed * gain[...] + shift[...]
        mixed_s[rows, :] = mixed
        mean_m.append(group_total(row_total(mixed)) * (0.25 / D))
        mean_g.append(group_total(row_total(ghat_of(n))) * (0.25 / D))
    merge_inv, slope = [], []
    for n, rows in enumerate(spans):
        cent = mixed_s[rows, :] - mean_m[n]
        ghat = ghat_of(n)
        inv = lax.rsqrt(group_total(row_total(cent * cent)) * (0.25 / D) + norm_eps)
        merge_inv.append(inv)
        slope.append(group_total(row_total(ghat * cent)) * (0.25 / D) * inv * inv)
    mean_e, mean_en = [], []
    for n, rows in enumerate(spans):
        cent = mixed_s[rows, :] - mean_m[n]
        gmixed = merge_inv[n] * (ghat_of(n) - mean_g[n] - cent * slope[n])
        mixed_s[rows, :] = gmixed
        gnorm = gmixed * gain[...]
        mean_e.append(row_total(gnorm) * (1.0 / D))
        mean_en.append(row_total(gnorm * proj_s[rows, :]) * (1.0 / D))
    for n, rows in enumerate(spans):
        gnorm = mixed_s[rows, :] * gain[...]
        gproj = inv_std[n] * (gnorm - mean_e[n] - proj_s[rows, :] * mean_en[n])
        gproj_s[rows, :] = gproj.astype(bf16)

    for n in range(2):
        cols = slice(256 * n, 256 * n + 256)
        ga_s[:, cols] = mm_nt(gproj_s[...], w_proj[cols, :]).astype(bf16)

    grad_k, grad_q = [], []
    for n, (w, b) in enumerate(pairs):
        rows = slice(64 * w, 64 * w + 64)
        wide = slice(256 * b, 256 * b + 256)
        vcols = slice(2 * ATT + 128 * b, 2 * ATT + 128 * b + 128)
        gabd = block_diagonal(ga_s[rows, 128 * b : 128 * b + 128])
        gprob = mm_nt(qkv_s[rows, vcols], gabd)
        gpack_s[rows, vcols] = mm(prob16_s[rows, wide], gabd).astype(bf16)
        prob = prob_s[rows, wide]
        gscore = prob * (gprob - col_total(prob * gprob))
        prob16_s[rows, wide] = gscore.astype(bf16)
    for n, (w, b) in enumerate(pairs):
        rows = slice(64 * w, 64 * w + 64)
        gscore = prob16_s[rows, 256 * b : 256 * b + 256]
        qcols = slice(128 * b, 128 * b + 128)
        kcols = slice(ATT + 128 * b, ATT + 128 * b + 128)
        gk = mm(gscore, qbd_s[256 * n : 256 * n + 256, :])
        gq = diagonal(mm_tn(gscore, unit16_s[rows, kcols])) * temper[:, qcols]
        proj_s[rows, qcols] = gq
        proj_s[rows, kcols] = gk
    for n in range(8):
        cols = slice(128 * n, 128 * n + 128)
        store_halves(n, unit_s[:, cols] * proj_s[:, cols])
    along = mm(seg_s[...], seg)
    for n in range(8):
        cols = slice(128 * n, 128 * n + 128)
        grad = inv_s[:, cols] * (proj_s[:, cols] - unit_s[:, cols] * along[count * n : count * n + count])
        gpack_s[:, cols] = grad.astype(bf16)

    for n in range(4):
        cols = slice(256 * n, 256 * n + 256)
        total = mixed_s[kept, cols] + mm_nt(gpack_s[kept, :], w_qkv[cols, :])
        emit(cols, total.astype(bf16))


def scratch_for(count):
    return [
        pltpu.VMEM((count, D), bf16),
        pltpu.VMEM((count, 3 * ATT), bf16),
        pltpu.VMEM((count, 2 * ATT), f32),
        pltpu.VMEM((count, 2 * ATT), f32),
        pltpu.VMEM((count, 2 * ATT), bf16),
        pltpu.VMEM((8 * count, 256), bf16),
        pltpu.VMEM((16 * count, 128), bf16),
        pltpu.VMEM((count, HEADS * CELLS), f32),
        pltpu.VMEM((count, HEADS * CELLS), bf16),
        pltpu.VMEM((count, ATT), bf16),
        pltpu.VMEM((count, D), f32),
        pltpu.VMEM((count, D), f32),
        pltpu.VMEM((count, D), bf16),
        pltpu.VMEM((count, ATT), bf16),
        pltpu.VMEM((count, 3 * ATT), bf16),
        pltpu.VMEM((16, D), f32),
    ]


def inner_kernel(own, lon, *refs):
    params, (out_own, out_lon), scratch = refs[:7], refs[7:9], refs[9:]
    quads = ((lon, 16), (own, 16), (lon, 32), (own, 32))

    def emit(cols, total):
        out_lon[0:16, cols] = total[0:16]
        out_own[0:16, cols] = total[16:32]
        out_lon[16:32, cols] = total[32:48]
        out_own[16:32, cols] = total[48:64]

    windows(quads, slice(0, 64), emit, params, scratch)


def inner(own, lon, params):
    return pl.pallas_call(
        inner_kernel,
        out_shape=[jax.ShapeDtypeStruct((32, D), bf16)] * 2,
        scratch_shapes=scratch_for(64),
        compiler_params=pltpu.CompilerParams(vmem_limit_bytes=16 * MIB),
        cost_estimate=pl.CostEstimate(
            flops=3_000_000_000, bytes_accessed=6_000_000, transcendentals=150_000
        ),
        name="inner",
    )(own, lon, *params)


def outer_kernel(own, lon, first, second, in_own, in_lon, *refs):
    params, (out_own, out_lon, above, below), scratch = refs[:7], refs[7:11], refs[11:]
    odd = lax.axis_index("lat") % 2 == 1
    above[...] = jnp.where(odd, first[0:32, :], second[0:32, :])
    below[...] = jnp.where(odd, second[32:64, :], first[32:64, :])
    quads = (
        (above, 0),
        (above, 16),
        (lon, 0),
        (own, 0),
        (lon, 48),
        (own, 48),
        (below, 0),
        (below, 16),
    )
    out_own[16:48, :] = in_own[...]
    out_lon[16:48, :] = in_lon[...]

    def emit(cols, total):
        out_lon[0:16, cols] = total[0:16]
        out_own[0:16, cols] = total[16:32]
        out_lon[48:64, cols] = total[32:48]
        out_own[48:64, cols] = total[48:64]

    windows(quads, slice(32, 96), emit, params, scratch)


def outer(own, lon, first, second, in_own, in_lon, params):
    return pl.pallas_call(
        outer_kernel,
        out_shape=[jax.ShapeDtypeStruct((64, D), bf16)] * 2,
        scratch_shapes=[pltpu.VMEM((32, WIDE), bf16)] * 2 + scratch_for(128),
        compiler_params=pltpu.CompilerParams(vmem_limit_bytes=24 * MIB),
        cost_estimate=pl.CostEstimate(
            flops=3_000_000_000, bytes_accessed=6_000_000, transcendentals=150_000
        ),
        name="outer",
    )(own, lon, first, second, in_own, in_lon, *params)


def final_kernel(own, lon, out):
    rows = jnp.concatenate([own[...], lon[...]], axis=0)
    row, col, _ = sorted_place(iota((128, 128), 1))
    token_place = onehot(iota((128, 128), 0) == row * 8 + col)
    out[...] = mm(token_place, rows).reshape(16, 8, D).astype(bf16)


def final(own, lon):
    return pl.pallas_call(
        final_kernel,
        out_shape=jax.ShapeDtypeStruct((16, 8, D), bf16),
        compiler_params=pltpu.CompilerParams(vmem_limit_bytes=8 * MIB),
        name="final",
    )(own, lon)


def passed_along(block, axis, distance):
    count = lax.axis_size(axis)
    route = [(i, (i + distance) % count) for i in range(count)]
    return lax.ppermute(block, axis, route)


def shards(
    tokens,
    labels,
    w_qkv,
    w_proj,
    logit_scale,
    bias_table,
    norm_gain,
    norm_shift,
    merge_gain,
    cotangent,
):
    own, lon = pack(tokens, labels.T, cotangent, places())
    lon = passed_along(lon, "lon", 1)
    ebias, temper = prep(bias_table, logit_scale.reshape(1, HEADS))
    params = (
        ebias,
        temper,
        w_qkv,
        w_proj,
        norm_gain.reshape(1, D),
        norm_shift.reshape(1, D),
        merge_gain.reshape(1, 4 * D),
    )
    to_first, to_second = strips(own, lon)
    lats = lax.axis_size("lat")
    pairs = [[i, (i + 1) % lats] for i in range(lats)]
    first = lax.all_gather(to_first, "lat", axis_index_groups=pairs[0::2], tiled=True)
    second = lax.all_gather(to_second, "lat", axis_index_groups=pairs[1::2], tiled=True)
    in_own, in_lon = inner(own, lon, params)
    own, lon = outer(own, lon, first, second, in_own, in_lon, params)
    lon = passed_along(lon, "lon", -1)
    return final(own, lon)


def solution(mesh):
    placed = (
        P("lat", "lon", None),
        P("lat", "lon"),
        P(),
        P(),
        P(),
        P(),
        P(),
        P(),
        P(),
        P("lat", "lon", None),
    )
    return jax.shard_map(
        shards, mesh=mesh, in_specs=placed, out_specs=P("lat", "lon", None), check_vma=False
    )
```

```python
import math

import jax
import jax.numpy as jnp
from jax import lax
from jax.experimental import pallas as pl
from jax.experimental.pallas import tpu as pltpu
from jax.sharding import PartitionSpec as P

WIN = 8
D = 1024
HEADS = 16
ATT = 512
QUAD = 16
CELLS = 64
BLOCKS = 4
WIDE = 2 * D + 128

norm_eps = 1e-05
unit_eps = 1e-06
f32 = jnp.float32
bf16 = jnp.bfloat16
MIB = 1024 * 1024
BUSY = pl.CostEstimate(flops=10_000_000_000, bytes_accessed=30_000_000, transcendentals=0)


def sorted_place(n):
    quad = n // 16
    s = (n // 4) % 4
    g = n % 4
    row = jnp.where(quad < 6, 4 + 4 * (quad % 3), 0) + 2 * (g // 2) + s % 2
    col = jnp.where((quad // 3 == 1) | (quad == 7), 0, 4) + 2 * (g % 2) + s // 2
    return row, col, s


def window_place(n):
    row = 4 * (n // 32) + 2 * ((n // 2) % 2) + (n // 4) % 2
    col = 4 * ((n // 16) % 2) + 2 * (n % 2) + (n // 8) % 2
    return row, col


def iota(shape, axis):
    return lax.broadcasted_iota(jnp.int32, shape, axis)


def onehot(match):
    return match.astype(f32).astype(bf16)


def halves(value):
    high = value.astype(bf16)
    low = (value - high.astype(f32)).astype(bf16)
    return high, low


def mm(a, b):
    return jnp.dot(a, b, preferred_element_type=f32)


def mm_nt(a, b):
    return lax.dot_general(a, b, (((1,), (1,)), ((), ())), preferred_element_type=f32)


def mm_tn(a, b):
    return lax.dot_general(a, b, (((0,), (0,)), ((), ())), preferred_element_type=f32)


def places_kernel(token_sort, cot_sort, label_row, label_col):
    row, col, s = sorted_place(iota((128, 128), 0))
    lane = iota((128, 128), 1)
    token_sort[...] = onehot(lane == row * 8 + col)
    cot_sort[...] = onehot(lane == s * 32 + (row // 2) * 4 + col // 2)
    row, _, _ = sorted_place(iota((128, 16), 0))
    label_row[...] = (iota((128, 16), 1) == row).astype(f32)
    _, col, _ = sorted_place(iota((128, 8), 0))
    label_col[...] = onehot(iota((128, 8), 1) == col)


def places():
    return pl.pallas_call(
        places_kernel,
        out_shape=[
            jax.ShapeDtypeStruct((128, 128), bf16),
            jax.ShapeDtypeStruct((128, 128), bf16),
            jax.ShapeDtypeStruct((128, 16), f32),
            jax.ShapeDtypeStruct((128, 8), bf16),
        ],
        compiler_params=pltpu.CompilerParams(vmem_limit_bytes=8 * MIB),
        cost_estimate=BUSY,
        name="places",
    )()


def pack_kernel(
    token_sort, cot_sort, label_row, label_col, tokens, labels, cot, own, lon, lat, dia, cot_rows
):
    outs = ((own, 0, 48), (lon, 48, 96), (lat, 96, 112), (dia, 112, 128))
    moved = mm(token_sort[...], tokens[...].reshape(128, D)).astype(bf16)
    for ref, lo, hi in outs:
        ref[:, 0:D] = moved[lo:hi]
    first = lax.axis_index("lat") == 0
    code = labels[...] + jnp.where(iota((8, 16), 1) < 4, jnp.where(first, 4, 0), 0)
    spread = mm(label_col[...], code.astype(f32).astype(bf16)) * label_row[...]
    column = jnp.sum(spread, axis=1, keepdims=True)
    wide = jnp.broadcast_to(column, (128, 128)).astype(bf16)
    for ref, lo, hi in outs:
        ref[:, 2 * D :] = wide[lo:hi]
    for r in range(8):
        cot_rows[4 * r : 4 * r + 4, :] = cot[r].astype(f32)
    stacked = jnp.concatenate(
        [cot_rows[:, s * D : (s + 1) * D].astype(bf16) for s in range(4)], axis=0
    )
    moved_cot = mm(cot_sort[...], stacked).astype(bf16)
    for ref, lo, hi in outs:
        ref[:, D : 2 * D] = moved_cot[lo:hi]


def pack(tokens, labels, cot, sorts):
    shapes = [jax.ShapeDtypeStruct((n, WIDE), bf16) for n in (48, 48, 16, 16)]
    return pl.pallas_call(
        pack_kernel,
        out_shape=shapes,
        scratch_shapes=[pltpu.VMEM((32, 4 * D), f32)],
        compiler_params=pltpu.CompilerParams(vmem_limit_bytes=12 * MIB),
        cost_estimate=BUSY,
        name="pack",
    )(*sorts, tokens, labels, cot)


def relative_bias(table, natural, ebias):
    entry, place = iota((225, 256), 0), iota((225, 256), 1)
    table_spread = onehot((entry == 15 * (place // 16) + place % 16) & (place % 16 < 15))
    entry, place = iota((256, 512), 0), iota((256, 512), 1)
    row, col = window_place(place % 64)
    toeplitz = onehot(entry == 16 * (row - place // 64 + 7) + col)
    row, col = window_place(iota((64, 64), 0))
    row_order = onehot(iota((64, 64), 1) == row * 8 + col)
    gate = 16.0 / (1.0 + jnp.exp(-table))
    high, low = halves(gate)
    spread = mm(high, table_spread) + mm(low, table_spread)
    pieces = []
    for h in range(HEADS):
        line = jnp.broadcast_to(spread[h : h + 1, :], (8, 256))
        pieces.append(pltpu.roll(line, 249, 1, stride=1, stride_axis=0))
    high, low = halves(jnp.concatenate(pieces, axis=0))
    blocks = mm(high, toeplitz) + mm(low, toeplitz)
    left = iota((8, 128), 1) < 64
    for q in range(8):
        for p in range(4):
            even = blocks[16 * q : 16 * q + 8, 128 * p : 128 * p + 128]
            odd = blocks[16 * q + 8 : 16 * q + 16, 128 * p : 128 * p + 128]
            lanes = slice(128 * q, 128 * q + 128)
            natural[16 * p : 16 * p + 8, lanes] = jnp.where(left, even, pltpu.roll(odd, 64, 1))
            natural[16 * p + 8 : 16 * p + 16, lanes] = jnp.where(
                left, pltpu.roll(even, 64, 1), odd
            )
    high, low = halves(natural[...])
    ebias[...] = jnp.exp(mm(row_order, high) + mm(row_order, low))


def prep_kernel(table, scale, ebias, temper, natural):
    relative_bias(table[...], natural, ebias)
    per_head = jnp.exp(jnp.minimum(scale[...], math.log(100.0)))
    head_of = iota((1, ATT), 1) // 32
    line = jnp.zeros((1, ATT), f32)
    for h in range(HEADS):
        line = jnp.where(head_of == h, per_head[0:1, h : h + 1], line)
    temper[...] = line


def prep(table, scale):
    return pl.pallas_call(
        prep_kernel,
        out_shape=[
            jax.ShapeDtypeStruct((CELLS, HEADS * CELLS), f32),
            jax.ShapeDtypeStruct((1, ATT), f32),
        ],
        scratch_shapes=[pltpu.VMEM((CELLS, HEADS * CELLS), f32)],
        compiler_params=pltpu.CompilerParams(vmem_limit_bytes=12 * MIB),
        cost_estimate=pl.CostEstimate(
            flops=100_000_000, bytes_accessed=400_000, transcendentals=80_000
        ),
        name="prep",
    )(table, scale)


def group_total(column):
    pair = column[0:8] + column[8:16]
    pair = pair + pltpu.roll(pair, 4, 0)
    return jnp.concatenate([pair, pair], axis=0)


def row_total(value):
    return jnp.sum(value, axis=1, keepdims=True)


def col_total(value):
    return jnp.sum(value, axis=0, keepdims=True)


def main_kernel(
    own,
    lon,
    dia,
    lat,
    ebias,
    temper,
    w_qkv,
    w_proj,
    gain,
    shift,
    merge,
    out_own,
    out_lon,
    out_lat,
    out_dia,
    x_s,
    qkv_s,
    unit_s,
    inv_s,
    unit16_s,
    seg_s,
    qbd_s,
    prob_s,
    prob16_s,
    att_s,
    proj_s,
    mixed_s,
    gproj_s,
    ga_s,
    gpack_s,
    mgain,
):
    quads = (
        (own, out_own, 0),
        (lon, out_lon, 0),
        (own, out_own, 16),
        (lon, out_lon, 16),
        (own, out_own, 32),
        (lon, out_lon, 32),
        (lat, out_lat, 0),
        (dia, out_dia, 0),
    )
    pairs = [(w, b) for w in range(2) for b in range(BLOCKS)]
    for n, (ref, _, lo) in enumerate(quads):
        x_s[16 * n : 16 * n + 16, :] = ref[lo : lo + 16, 0:D]
    for n in range(6):
        cols = slice(256 * n, 256 * n + 256)
        qkv_s[:, cols] = mm(x_s[...], w_qkv[:, cols]).astype(bf16)

    line, lane = iota((256, 128), 0), iota((256, 128), 1)
    seg = onehot((line % 128) // 32 == lane // 32)
    head_lane = iota((64, 128), 1) // 32
    head_mask = [onehot(head_lane == h) for h in range(4)]

    def store_halves(n, value):
        high, low = halves(value)
        seg_s[128 * n : 128 * n + 128, 0:128] = high
        seg_s[128 * n : 128 * n + 128, 128:256] = low

    def block_diagonal(value):
        return jnp.concatenate([value * head_mask[h] for h in range(4)], axis=0)

    def diagonal(value):
        out = value[192:256]
        for h in range(3):
            out = jnp.where(head_lane == h, value[64 * h : 64 * h + 64], out)
        return out

    for n in range(8):
        raw = qkv_s[:, 128 * n : 128 * n + 128].astype(f32)
        store_halves(n, raw * raw)
    squares = mm(seg_s[...], seg)
    for n in range(8):
        cols = slice(128 * n, 128 * n + 128)
        inv = lax.rsqrt(squares[cols] + unit_eps)
        unit = qkv_s[:, cols].astype(f32) * inv
        inv_s[:, cols] = inv
        unit_s[:, cols] = unit
        if n < BLOCKS:
            unit = unit * temper[:, cols]
        unit16_s[:, cols] = unit.astype(bf16)

    code_lane = iota((16, 128), 1)
    allowed = []
    for w in range(2):
        hot = jnp.concatenate(
            [
                onehot(ref[lo : lo + 16, 2 * D :].astype(f32).astype(jnp.int32) == code_lane)
                for ref, _, lo in quads[4 * w : 4 * w + 4]
            ],
            axis=0,
        )
        allowed.append(mm_nt(hot, jnp.concatenate([hot] * 4, axis=0)))
    for n, (w, b) in enumerate(pairs):
        rows = slice(64 * w, 64 * w + 64)
        wide = slice(256 * b, 256 * b + 256)
        qbd = block_diagonal(unit16_s[rows, 128 * b : 128 * b + 128])
        qbd_s[256 * n : 256 * n + 256, :] = qbd
        score = mm_nt(unit16_s[rows, ATT + 128 * b : ATT + 128 * b + 128], qbd)
        weight = jnp.exp(score) * ebias[:, wide] * allowed[w]
        prob = weight * (1.0 / col_total(weight))
        prob_s[rows, wide] = prob
        prob16_s[rows, wide] = prob.astype(bf16)
    for w, b in pairs:
        rows = slice(64 * w, 64 * w + 64)
        vals = qkv_s[rows, 2 * ATT + 128 * b : 2 * ATT + 128 * b + 128]
        att = diagonal(mm_tn(prob16_s[rows, 256 * b : 256 * b + 256], vals))
        att_s[rows, 128 * b : 128 * b + 128] = att.astype(bf16)

    for n in range(4):
        cols = slice(256 * n, 256 * n + 256)
        proj_s[:, cols] = mm(att_s[...], w_proj[:, cols])

    spans = [slice(16 * n, 16 * n + 16) for n in range(8)]

    def ghat_of(n):
        ref, _, lo = quads[n]
        return ref[lo : lo + 16, D : 2 * D].astype(f32) * mgain[...]

    for s in range(4):
        mgain[4 * s : 4 * s + 4, :] = jnp.broadcast_to(merge[:, s * D : (s + 1) * D], (4, D))
    mean = [row_total(proj_s[rows, :]) * (1.0 / D) for rows in spans]
    inv_std = []
    for n, rows in enumerate(spans):
        centered = proj_s[rows, :] - mean[n]
        inv_std.append(lax.rsqrt(row_total(centered * centered) * (1.0 / D) + norm_eps))
    mean_m, mean_g = [], []
    for n, rows in enumerate(spans):
        normed = (proj_s[rows, :] - mean[n]) * inv_std[n]
        proj_s[rows, :] = normed
        mixed = x_s[rows, :].astype(f32) + normed * gain[...] + shift[...]
        mixed_s[rows, :] = mixed
        mean_m.append(group_total(row_total(mixed)) * (0.25 / D))
        mean_g.append(group_total(row_total(ghat_of(n))) * (0.25 / D))
    merge_inv, slope = [], []
    for n, rows in enumerate(spans):
        cent = mixed_s[rows, :] - mean_m[n]
        ghat = ghat_of(n)
        inv = lax.rsqrt(group_total(row_total(cent * cent)) * (0.25 / D) + norm_eps)
        merge_inv.append(inv)
        slope.append(group_total(row_total(ghat * cent)) * (0.25 / D) * inv * inv)
    mean_e, mean_en = [], []
    for n, rows in enumerate(spans):
        cent = mixed_s[rows, :] - mean_m[n]
        gmixed = merge_inv[n] * (ghat_of(n) - mean_g[n] - cent * slope[n])
        mixed_s[rows, :] = gmixed
        gnorm = gmixed * gain[...]
        mean_e.append(row_total(gnorm) * (1.0 / D))
        mean_en.append(row_total(gnorm * proj_s[rows, :]) * (1.0 / D))
    for n, rows in enumerate(spans):
        gnorm = mixed_s[rows, :] * gain[...]
        gproj = inv_std[n] * (gnorm - mean_e[n] - proj_s[rows, :] * mean_en[n])
        gproj_s[rows, :] = gproj.astype(bf16)

    for n in range(2):
        cols = slice(256 * n, 256 * n + 256)
        ga_s[:, cols] = mm_nt(gproj_s[...], w_proj[cols, :]).astype(bf16)

    grad_k, grad_q = [], []
    for n, (w, b) in enumerate(pairs):
        rows = slice(64 * w, 64 * w + 64)
        wide = slice(256 * b, 256 * b + 256)
        vcols = slice(2 * ATT + 128 * b, 2 * ATT + 128 * b + 128)
        gabd = block_diagonal(ga_s[rows, 128 * b : 128 * b + 128])
        gprob = mm_nt(qkv_s[rows, vcols], gabd)
        gpack_s[rows, vcols] = mm(prob16_s[rows, wide], gabd).astype(bf16)
        prob = prob_s[rows, wide]
        gscore = prob * (gprob - col_total(prob * gprob))
        prob16_s[rows, wide] = gscore.astype(bf16)
    for n, (w, b) in enumerate(pairs):
        rows = slice(64 * w, 64 * w + 64)
        gscore = prob16_s[rows, 256 * b : 256 * b + 256]
        qcols = slice(128 * b, 128 * b + 128)
        kcols = slice(ATT + 128 * b, ATT + 128 * b + 128)
        gk = mm(gscore, qbd_s[256 * n : 256 * n + 256, :])
        gq = diagonal(mm_tn(gscore, unit16_s[rows, kcols])) * temper[:, qcols]
        proj_s[rows, qcols] = gq
        proj_s[rows, kcols] = gk
    for n in range(8):
        cols = slice(128 * n, 128 * n + 128)
        store_halves(n, unit_s[:, cols] * proj_s[:, cols])
    along = mm(seg_s[...], seg)
    for n in range(8):
        cols = slice(128 * n, 128 * n + 128)
        grad = inv_s[:, cols] * (proj_s[:, cols] - unit_s[:, cols] * along[cols])
        gpack_s[:, cols] = grad.astype(bf16)

    for n in range(4):
        cols = slice(256 * n, 256 * n + 256)
        total = (mixed_s[:, cols] + mm_nt(gpack_s[...], w_qkv[cols, :])).astype(bf16)
        for m, (_, ref, lo) in enumerate(quads):
            ref[lo : lo + 16, cols] = total[16 * m : 16 * m + 16]


def main(own, lon, dia, lat, *params):
    return pl.pallas_call(
        main_kernel,
        out_shape=[jax.ShapeDtypeStruct((n, D), bf16) for n in (48, 48, 16, 16)],
        scratch_shapes=[
            pltpu.VMEM((128, D), bf16),
            pltpu.VMEM((128, 3 * ATT), bf16),
            pltpu.VMEM((128, 2 * ATT), f32),
            pltpu.VMEM((128, 2 * ATT), f32),
            pltpu.VMEM((128, 2 * ATT), bf16),
            pltpu.VMEM((1024, 256), bf16),
            pltpu.VMEM((2048, 128), bf16),
            pltpu.VMEM((128, HEADS * CELLS), f32),
            pltpu.VMEM((128, HEADS * CELLS), bf16),
            pltpu.VMEM((128, ATT), bf16),
            pltpu.VMEM((128, D), f32),
            pltpu.VMEM((128, D), f32),
            pltpu.VMEM((128, D), bf16),
            pltpu.VMEM((128, ATT), bf16),
            pltpu.VMEM((128, 3 * ATT), bf16),
            pltpu.VMEM((16, D), f32),
        ],
        compiler_params=pltpu.CompilerParams(vmem_limit_bytes=24 * MIB),
        cost_estimate=pl.CostEstimate(
            flops=1_500_000_000, bytes_accessed=6_000_000, transcendentals=150_000
        ),
        name="main",
    )(own, lon, dia, lat, *params)


def final_kernel(own, lon, dia, lat, out):
    rows = jnp.concatenate([own[...], lon[...], lat[...], dia[...]], axis=0)
    row, col, _ = sorted_place(iota((128, 128), 1))
    token_place = onehot(iota((128, 128), 0) == row * 8 + col)
    out[...] = mm(token_place, rows).reshape(16, 8, D).astype(bf16)


def final(own, lon, lat, dia):
    return pl.pallas_call(
        final_kernel,
        out_shape=jax.ShapeDtypeStruct((16, 8, D), bf16),
        compiler_params=pltpu.CompilerParams(vmem_limit_bytes=8 * MIB),
        name="final",
    )(own, lon, dia, lat)


def shift_by(block, lat_step, lon_step):
    lats, lons = lax.axis_size("lat"), lax.axis_size("lon")
    route = [
        (j * lats + i, ((j + lon_step) % lons) * lats + (i + lat_step) % lats)
        for j in range(lons)
        for i in range(lats)
    ]
    return lax.ppermute(block, ("lon", "lat"), route)


def shards(
    tokens,
    labels,
    w_qkv,
    w_proj,
    logit_scale,
    bias_table,
    norm_gain,
    norm_shift,
    merge_gain,
    cotangent,
):
    own, lon, lat, dia = pack(tokens, labels.T, cotangent, places())
    lon = shift_by(lon, 0, -1)
    dia = shift_by(dia, -1, -1)
    lat = shift_by(lat, -1, 0)
    ebias, temper = prep(bias_table, logit_scale.reshape(1, HEADS))
    own, lon, lat, dia = main(
        own,
        lon,
        dia,
        lat,
        ebias,
        temper,
        w_qkv,
        w_proj,
        norm_gain.reshape(1, D),
        norm_shift.reshape(1, D),
        merge_gain.reshape(1, 4 * D),
    )
    lon = shift_by(lon, 0, 1)
    dia = shift_by(dia, 1, 1)
    lat = shift_by(lat, 1, 0)
    return final(own, lon, lat, dia)


def solution(mesh):
    placed = (
        P("lat", "lon", None),
        P("lat", "lon"),
        P(),
        P(),
        P(),
        P(),
        P(),
        P(),
        P(),
        P("lat", "lon", None),
    )
    return jax.shard_map(
        shards, mesh=mesh, in_specs=placed, out_specs=P("lat", "lon", None), check_vma=False
    )
```

```python
import math

import jax
import jax.numpy as jnp
from jax import lax
from jax.experimental import pallas as pl
from jax.experimental.pallas import tpu as pltpu
from jax.sharding import PartitionSpec as P

WIN = 8
D = 1024
HEADS = 16
ATT = 512
QUAD = 16
CELLS = 64
BLOCKS = 4
WIDE = 2 * D + 128

norm_eps = 1e-05
unit_eps = 1e-06
f32 = jnp.float32
bf16 = jnp.bfloat16
MIB = 1024 * 1024
BUSY = pl.CostEstimate(flops=10_000_000_000, bytes_accessed=30_000_000, transcendentals=0)


def sorted_place(n):
    quad = n // 16
    s = (n // 4) % 4
    g = n % 4
    row = jnp.where(quad < 6, 4 + 4 * (quad % 3), 0) + 2 * (g // 2) + s % 2
    col = jnp.where((quad < 3) | (quad == 7), 4, 0) + 2 * (g % 2) + s // 2
    return row, col, s


def window_place(n):
    row = 4 * (n // 32) + 2 * ((n // 2) % 2) + (n // 4) % 2
    col = 4 * ((n // 16) % 2) + 2 * (n % 2) + (n // 8) % 2
    return row, col


def iota(shape, axis):
    return lax.broadcasted_iota(jnp.int32, shape, axis)


def onehot(match):
    return match.astype(f32).astype(bf16)


def halves(value):
    high = value.astype(bf16)
    low = (value - high.astype(f32)).astype(bf16)
    return high, low


def mm(a, b):
    return jnp.dot(a, b, preferred_element_type=f32)


def mm_nt(a, b):
    return lax.dot_general(a, b, (((1,), (1,)), ((), ())), preferred_element_type=f32)


def mm_tn(a, b):
    return lax.dot_general(a, b, (((0,), (0,)), ((), ())), preferred_element_type=f32)


def places_kernel(token_sort, cot_sort, label_row, label_col):
    row, col, s = sorted_place(iota((128, 128), 0))
    lane = iota((128, 128), 1)
    token_sort[...] = onehot(lane == row * 8 + col)
    cot_sort[...] = onehot(lane == s * 32 + (row // 2) * 4 + col // 2)
    row, _, _ = sorted_place(iota((128, 16), 0))
    label_row[...] = (iota((128, 16), 1) == row).astype(f32)
    _, col, _ = sorted_place(iota((128, 8), 0))
    label_col[...] = onehot(iota((128, 8), 1) == col)


def places():
    return pl.pallas_call(
        places_kernel,
        out_shape=[
            jax.ShapeDtypeStruct((128, 128), bf16),
            jax.ShapeDtypeStruct((128, 128), bf16),
            jax.ShapeDtypeStruct((128, 16), f32),
            jax.ShapeDtypeStruct((128, 8), bf16),
        ],
        compiler_params=pltpu.CompilerParams(vmem_limit_bytes=8 * MIB),
        cost_estimate=BUSY,
        name="places",
    )()


def pack_kernel(
    token_sort,
    cot_sort,
    label_row,
    label_col,
    tokens,
    labels,
    cot,
    right,
    left,
    first_row,
    first_left,
    first_right,
    cot_rows,

):
    outs = (
        (right, 0, 48),
        (left, 48, 96),
        (first_row, 96, 128),
        (first_left, 96, 112),
        (first_right, 112, 128),
    )
    moved = mm(token_sort[...], tokens[...].reshape(128, D)).astype(bf16)
    for ref, lo, hi in outs:
        ref[:, 0:D] = moved[lo:hi]
    first = lax.axis_index("lat") == 0
    code = labels[...] + jnp.where(iota((8, 16), 1) < 4, jnp.where(first, 4, 0), 0)
    spread = mm(label_col[...], code.astype(f32).astype(bf16)) * label_row[...]
    column = jnp.sum(spread, axis=1, keepdims=True)
    wide = jnp.broadcast_to(column, (128, 128)).astype(bf16)
    for ref, lo, hi in outs:
        ref[:, 2 * D :] = wide[lo:hi]
    for r in range(8):
        cot_rows[4 * r : 4 * r + 4, :] = cot[r].astype(f32)
    stacked = jnp.concatenate(
        [cot_rows[:, s * D : (s + 1) * D].astype(bf16) for s in range(4)], axis=0
    )
    moved_cot = mm(cot_sort[...], stacked).astype(bf16)
    for ref, lo, hi in outs:
        ref[:, D : 2 * D] = moved_cot[lo:hi]


def pack(tokens, labels, cot, sorts):
    shapes = [jax.ShapeDtypeStruct((n, WIDE), bf16) for n in (48, 48, 32, 16, 16)]
    return pl.pallas_call(
        pack_kernel,
        out_shape=shapes,
        scratch_shapes=[pltpu.VMEM((32, 4 * D), f32)],
        compiler_params=pltpu.CompilerParams(vmem_limit_bytes=12 * MIB),
        cost_estimate=BUSY,
        name="pack",
    )(*sorts, tokens, labels, cot)


def relative_bias(table, natural, ebias):
    entry, place = iota((225, 256), 0), iota((225, 256), 1)
    table_spread = onehot((entry == 15 * (place // 16) + place % 16) & (place % 16 < 15))
    entry, place = iota((256, 512), 0), iota((256, 512), 1)
    row, col = window_place(place % 64)
    toeplitz = onehot(entry == 16 * (row - place // 64 + 7) + col)
    row, col = window_place(iota((64, 64), 0))
    row_order = onehot(iota((64, 64), 1) == row * 8 + col)
    gate = 16.0 / (1.0 + jnp.exp(-table))
    high, low = halves(gate)
    spread = mm(high, table_spread) + mm(low, table_spread)
    pieces = []
    for h in range(HEADS):
        line = jnp.broadcast_to(spread[h : h + 1, :], (8, 256))
        pieces.append(pltpu.roll(line, 249, 1, stride=1, stride_axis=0))
    high, low = halves(jnp.concatenate(pieces, axis=0))
    blocks = mm(high, toeplitz) + mm(low, toeplitz)
    left = iota((8, 128), 1) < 64
    for q in range(8):
        for p in range(4):
            even = blocks[16 * q : 16 * q + 8, 128 * p : 128 * p + 128]
            odd = blocks[16 * q + 8 : 16 * q + 16, 128 * p : 128 * p + 128]
            lanes = slice(128 * q, 128 * q + 128)
            natural[16 * p : 16 * p + 8, lanes] = jnp.where(left, even, pltpu.roll(odd, 64, 1))
            natural[16 * p + 8 : 16 * p + 16, lanes] = jnp.where(
                left, pltpu.roll(even, 64, 1), odd
            )
    high, low = halves(natural[...])
    ebias[...] = jnp.exp(mm(row_order, high) + mm(row_order, low))


def prep_kernel(table, scale, ebias, temper, natural):
    relative_bias(table[...], natural, ebias)
    per_head = jnp.exp(jnp.minimum(scale[...], math.log(100.0)))
    head_of = iota((1, ATT), 1) // 32
    line = jnp.zeros((1, ATT), f32)
    for h in range(HEADS):
        line = jnp.where(head_of == h, per_head[0:1, h : h + 1], line)
    temper[...] = line


def prep(table, scale):
    return pl.pallas_call(
        prep_kernel,
        out_shape=[
            jax.ShapeDtypeStruct((CELLS, HEADS * CELLS), f32),
            jax.ShapeDtypeStruct((1, ATT), f32),
        ],
        scratch_shapes=[pltpu.VMEM((CELLS, HEADS * CELLS), f32)],
        compiler_params=pltpu.CompilerParams(vmem_limit_bytes=12 * MIB),
        cost_estimate=pl.CostEstimate(
            flops=100_000_000, bytes_accessed=400_000, transcendentals=80_000
        ),
        name="prep",
    )(table, scale)


def group_total(column):
    pair = column[0:8] + column[8:16]
    pair = pair + pltpu.roll(pair, 4, 0)
    return jnp.concatenate([pair, pair], axis=0)


def row_total(value):
    return jnp.sum(value, axis=1, keepdims=True)


def col_total(value):
    return jnp.sum(value, axis=0, keepdims=True)


def windows(quads, kept, emit, params, scratch):
    ebias, temper, w_qkv, w_proj, gain, shift, merge = params
    (
        x_s,
        qkv_s,
        unit_s,
        inv_s,
        unit16_s,
        seg_s,
        qbd_s,
        prob_s,
        prob16_s,
        att_s,
        proj_s,
        mixed_s,
        gproj_s,
        ga_s,
        gpack_s,
        mgain,
    ) = scratch
    count = 16 * len(quads)
    pairs = [(w, b) for w in range(count // 64) for b in range(BLOCKS)]
    for n, (ref, lo) in enumerate(quads):
        x_s[16 * n : 16 * n + 16, :] = ref[lo : lo + 16, 0:D]
    for n in range(6):
        cols = slice(256 * n, 256 * n + 256)
        qkv_s[:, cols] = mm(x_s[...], w_qkv[:, cols]).astype(bf16)

    line, lane = iota((256, 128), 0), iota((256, 128), 1)
    seg = onehot((line % 128) // 32 == lane // 32)
    head_lane = iota((64, 128), 1) // 32
    head_mask = [onehot(head_lane == h) for h in range(4)]

    def store_halves(n, value):
        high, low = halves(value)
        seg_s[count * n : count * n + count, 0:128] = high
        seg_s[count * n : count * n + count, 128:256] = low

    def block_diagonal(value):
        return jnp.concatenate([value * head_mask[h] for h in range(4)], axis=0)

    def diagonal(value):
        out = value[192:256]
        for h in range(3):
            out = jnp.where(head_lane == h, value[64 * h : 64 * h + 64], out)
        return out

    for n in range(8):
        raw = qkv_s[:, 128 * n : 128 * n + 128].astype(f32)
        store_halves(n, raw * raw)
    squares = mm(seg_s[...], seg)
    for n in range(8):
        cols = slice(128 * n, 128 * n + 128)
        inv = lax.rsqrt(squares[count * n : count * n + count] + unit_eps)
        unit = qkv_s[:, cols].astype(f32) * inv
        inv_s[:, cols] = inv
        unit_s[:, cols] = unit
        if n < BLOCKS:
            unit = unit * temper[:, cols]
        unit16_s[:, cols] = unit.astype(bf16)

    code_lane = iota((16, 128), 1)
    allowed = []
    for w in range(count // 64):
        hot = jnp.concatenate(
            [
                onehot(ref[lo : lo + 16, 2 * D :].astype(f32).astype(jnp.int32) == code_lane)
                for ref, lo in quads[4 * w : 4 * w + 4]
            ],
            axis=0,
        )
        allowed.append(mm_nt(hot, jnp.concatenate([hot] * 4, axis=0)))
    for n, (w, b) in enumerate(pairs):
        rows = slice(64 * w, 64 * w + 64)
        wide = slice(256 * b, 256 * b + 256)
        qbd = block_diagonal(unit16_s[rows, 128 * b : 128 * b + 128])
        qbd_s[256 * n : 256 * n + 256, :] = qbd
        score = mm_nt(unit16_s[rows, ATT + 128 * b : ATT + 128 * b + 128], qbd)
        weight = jnp.exp(score) * ebias[:, wide] * allowed[w]
        prob = weight * (1.0 / col_total(weight))
        prob_s[rows, wide] = prob
        prob16_s[rows, wide] = prob.astype(bf16)
    for w, b in pairs:
        rows = slice(64 * w, 64 * w + 64)
        vals = qkv_s[rows, 2 * ATT + 128 * b : 2 * ATT + 128 * b + 128]
        att = diagonal(mm_tn(prob16_s[rows, 256 * b : 256 * b + 256], vals))
        att_s[rows, 128 * b : 128 * b + 128] = att.astype(bf16)

    for n in range(4):
        cols = slice(256 * n, 256 * n + 256)
        proj_s[:, cols] = mm(att_s[...], w_proj[:, cols])

    spans = [slice(16 * n, 16 * n + 16) for n in range(len(quads))]

    def ghat_of(n):
        ref, lo = quads[n]
        return ref[lo : lo + 16, D : 2 * D].astype(f32) * mgain[...]

    for s in range(4):
        mgain[4 * s : 4 * s + 4, :] = jnp.broadcast_to(merge[:, s * D : (s + 1) * D], (4, D))
    mean = [row_total(proj_s[rows, :]) * (1.0 / D) for rows in spans]
    inv_std = []
    for n, rows in enumerate(spans):
        centered = proj_s[rows, :] - mean[n]
        inv_std.append(lax.rsqrt(row_total(centered * centered) * (1.0 / D) + norm_eps))
    mean_m, mean_g = [], []
    for n, rows in enumerate(spans):
        normed = (proj_s[rows, :] - mean[n]) * inv_std[n]
        proj_s[rows, :] = normed
        mixed = x_s[rows, :].astype(f32) + normed * gain[...] + shift[...]
        mixed_s[rows, :] = mixed
        mean_m.append(group_total(row_total(mixed)) * (0.25 / D))
        mean_g.append(group_total(row_total(ghat_of(n))) * (0.25 / D))
    merge_inv, slope = [], []
    for n, rows in enumerate(spans):
        cent = mixed_s[rows, :] - mean_m[n]
        ghat = ghat_of(n)
        inv = lax.rsqrt(group_total(row_total(cent * cent)) * (0.25 / D) + norm_eps)
        merge_inv.append(inv)
        slope.append(group_total(row_total(ghat * cent)) * (0.25 / D) * inv * inv)
    mean_e, mean_en = [], []
    for n, rows in enumerate(spans):
        cent = mixed_s[rows, :] - mean_m[n]
        gmixed = merge_inv[n] * (ghat_of(n) - mean_g[n] - cent * slope[n])
        mixed_s[rows, :] = gmixed
        gnorm = gmixed * gain[...]
        mean_e.append(row_total(gnorm) * (1.0 / D))
        mean_en.append(row_total(gnorm * proj_s[rows, :]) * (1.0 / D))
    for n, rows in enumerate(spans):
        gnorm = mixed_s[rows, :] * gain[...]
        gproj = inv_std[n] * (gnorm - mean_e[n] - proj_s[rows, :] * mean_en[n])
        gproj_s[rows, :] = gproj.astype(bf16)

    for n in range(2):
        cols = slice(256 * n, 256 * n + 256)
        ga_s[:, cols] = mm_nt(gproj_s[...], w_proj[cols, :]).astype(bf16)

    grad_k, grad_q = [], []
    for n, (w, b) in enumerate(pairs):
        rows = slice(64 * w, 64 * w + 64)
        wide = slice(256 * b, 256 * b + 256)
        vcols = slice(2 * ATT + 128 * b, 2 * ATT + 128 * b + 128)
        gabd = block_diagonal(ga_s[rows, 128 * b : 128 * b + 128])
        gprob = mm_nt(qkv_s[rows, vcols], gabd)
        gpack_s[rows, vcols] = mm(prob16_s[rows, wide], gabd).astype(bf16)
        prob = prob_s[rows, wide]
        gscore = prob * (gprob - col_total(prob * gprob))
        prob16_s[rows, wide] = gscore.astype(bf16)
    for n, (w, b) in enumerate(pairs):
        rows = slice(64 * w, 64 * w + 64)
        gscore = prob16_s[rows, 256 * b : 256 * b + 256]
        qcols = slice(128 * b, 128 * b + 128)
        kcols = slice(ATT + 128 * b, ATT + 128 * b + 128)
        gk = mm(gscore, qbd_s[256 * n : 256 * n + 256, :])
        gq = diagonal(mm_tn(gscore, unit16_s[rows, kcols])) * temper[:, qcols]
        proj_s[rows, qcols] = gq
        proj_s[rows, kcols] = gk
    for n in range(8):
        cols = slice(128 * n, 128 * n + 128)
        store_halves(n, unit_s[:, cols] * proj_s[:, cols])
    along = mm(seg_s[...], seg)
    for n in range(8):
        cols = slice(128 * n, 128 * n + 128)
        grad = inv_s[:, cols] * (proj_s[:, cols] - unit_s[:, cols] * along[count * n : count * n + count])
        gpack_s[:, cols] = grad.astype(bf16)

    spans = [slice(16 * n, 16 * n + 16) for n in kept]
    gpack = jnp.concatenate([gpack_s[rows, :] for rows in spans], axis=0)
    for n in range(4):
        cols = slice(256 * n, 256 * n + 256)
        mixed = jnp.concatenate([mixed_s[rows, cols] for rows in spans], axis=0)
        emit(cols, (mixed + mm_nt(gpack, w_qkv[cols, :])).astype(bf16))


def scratch_for(count):
    return [
        pltpu.VMEM((count, D), bf16),
        pltpu.VMEM((count, 3 * ATT), bf16),
        pltpu.VMEM((count, 2 * ATT), f32),
        pltpu.VMEM((count, 2 * ATT), f32),
        pltpu.VMEM((count, 2 * ATT), bf16),
        pltpu.VMEM((8 * count, 256), bf16),
        pltpu.VMEM((16 * count, 128), bf16),
        pltpu.VMEM((count, HEADS * CELLS), f32),
        pltpu.VMEM((count, HEADS * CELLS), bf16),
        pltpu.VMEM((count, ATT), bf16),
        pltpu.VMEM((count, D), f32),
        pltpu.VMEM((count, D), f32),
        pltpu.VMEM((count, D), bf16),
        pltpu.VMEM((count, ATT), bf16),
        pltpu.VMEM((count, 3 * ATT), bf16),
        pltpu.VMEM((16, D), f32),
    ]


def main_kernel(right, left, east, west, below, below_east, below_west, *refs):
    params, (out_own, out_below), scratch = refs[:7], refs[7:9], refs[9:]
    quads = (
        (east, 0),
        (left, 0),
        (east, 16),
        (left, 16),
        (east, 32),
        (left, 32),
        (below_east, 0),
        (below, 0),
        (right, 0),
        (west, 0),
        (right, 16),
        (west, 16),
        (right, 32),
        (west, 32),
        (below, 16),
        (below_west, 0),
    )
    kept = (8, 10, 12, 1, 3, 5, 7, 14)

    def emit(cols, total):
        out_own[:, cols] = total[0:96]
        out_below[:, cols] = total[96:128]

    windows(quads, kept, emit, params, scratch)


def main(blocks, params):
    return pl.pallas_call(
        main_kernel,
        out_shape=[jax.ShapeDtypeStruct((n, D), bf16) for n in (96, 32)],
        scratch_shapes=scratch_for(256),
        compiler_params=pltpu.CompilerParams(vmem_limit_bytes=32 * MIB),
        cost_estimate=pl.CostEstimate(
            flops=3_000_000_000, bytes_accessed=6_000_000, transcendentals=150_000
        ),
        name="main",
    )(*blocks, *params)


def final_kernel(own, first_row, out):
    rows = jnp.concatenate([own[...], first_row[...]], axis=0)
    row, col, _ = sorted_place(iota((128, 128), 1))
    token_place = onehot(iota((128, 128), 0) == row * 8 + col)
    out[...] = mm(token_place, rows).reshape(16, 8, D).astype(bf16)


def final(own, first_row):
    return pl.pallas_call(
        final_kernel,
        out_shape=jax.ShapeDtypeStruct((16, 8, D), bf16),
        compiler_params=pltpu.CompilerParams(vmem_limit_bytes=8 * MIB),
        name="final",
    )(own, first_row)


def shift_by(block, lat_step, lon_step):
    lats, lons = lax.axis_size("lat"), lax.axis_size("lon")
    route = [
        (j * lats + i, ((j + lon_step) % lons) * lats + (i + lat_step) % lats)
        for j in range(lons)
        for i in range(lats)
    ]
    return lax.ppermute(block, ("lon", "lat"), route)


def shards(
    tokens,
    labels,
    w_qkv,
    w_proj,
    logit_scale,
    bias_table,
    norm_gain,
    norm_shift,
    merge_gain,
    cotangent,
):
    right, left, first_row, first_left, first_right = pack(
        tokens, labels.T, cotangent, places()
    )
    east = shift_by(right, 0, 1)
    west = shift_by(left, 0, -1)
    below = shift_by(first_row, -1, 0)
    below_east = shift_by(first_right, -1, 1)
    below_west = shift_by(first_left, -1, -1)
    ebias, temper = prep(bias_table, logit_scale.reshape(1, HEADS))
    params = (
        ebias,
        temper,
        w_qkv,
        w_proj,
        norm_gain.reshape(1, D),
        norm_shift.reshape(1, D),
        merge_gain.reshape(1, 4 * D),
    )
    blocks = (right, left, east, west, below, below_east, below_west)
    own, below = main(blocks, params)
    return final(own, shift_by(below, 1, 0))


def solution(mesh):
    placed = (
        P("lat", "lon", None),
        P("lat", "lon"),
        P(),
        P(),
        P(),
        P(),
        P(),
        P(),
        P(),
        P("lat", "lon", None),
    )
    return jax.shard_map(
        shards, mesh=mesh, in_specs=placed, out_specs=P("lat", "lon", None), check_vma=False
    )
```

```python
import math

import jax
import jax.numpy as jnp
from jax import lax
from jax.experimental import pallas as pl
from jax.experimental.pallas import tpu as pltpu
from jax.sharding import PartitionSpec as P

WIN = 8
D = 1024
HEADS = 16
ATT = 512
QUAD = 16
CELLS = 64
BLOCKS = 4
WIDE = 2 * D + 128

norm_eps = 1e-05
unit_eps = 1e-06
f32 = jnp.float32
bf16 = jnp.bfloat16
MIB = 1024 * 1024
BUSY = pl.CostEstimate(flops=10_000_000_000, bytes_accessed=30_000_000, transcendentals=0)


def sorted_place(n):
    quad = n // 16
    s = (n // 4) % 4
    g = n % 4
    row = jnp.where(quad < 6, 4 + 4 * (quad % 3), 0) + 2 * (g // 2) + s % 2
    col = jnp.where((quad // 3 == 1) | (quad == 7), 4, 0) + 2 * (g % 2) + s // 2
    return row, col, s


def window_place(n):
    row = 4 * (n // 32) + 2 * ((n // 2) % 2) + (n // 4) % 2
    col = 4 * ((n // 16) % 2) + 2 * (n % 2) + (n // 8) % 2
    return row, col


def iota(shape, axis):
    return lax.broadcasted_iota(jnp.int32, shape, axis)


def onehot(match):
    return match.astype(f32).astype(bf16)


def halves(value):
    high = value.astype(bf16)
    low = (value - high.astype(f32)).astype(bf16)
    return high, low


def mm(a, b):
    return jnp.dot(a, b, preferred_element_type=f32)


def mm_nt(a, b):
    return lax.dot_general(a, b, (((1,), (1,)), ((), ())), preferred_element_type=f32)


def mm_tn(a, b):
    return lax.dot_general(a, b, (((0,), (0,)), ((), ())), preferred_element_type=f32)


def places_kernel(token_sort, cot_sort, label_row, label_col):
    row, col, s = sorted_place(iota((128, 128), 0))
    lane = iota((128, 128), 1)
    token_sort[...] = onehot(lane == row * 8 + col)
    cot_sort[...] = onehot(lane == s * 32 + (row // 2) * 4 + col // 2)
    row, _, _ = sorted_place(iota((128, 16), 0))
    label_row[...] = (iota((128, 16), 1) == row).astype(f32)
    _, col, _ = sorted_place(iota((128, 8), 0))
    label_col[...] = onehot(iota((128, 8), 1) == col)


def places():
    return pl.pallas_call(
        places_kernel,
        out_shape=[
            jax.ShapeDtypeStruct((128, 128), bf16),
            jax.ShapeDtypeStruct((128, 128), bf16),
            jax.ShapeDtypeStruct((128, 16), f32),
            jax.ShapeDtypeStruct((128, 8), bf16),
        ],
        compiler_params=pltpu.CompilerParams(vmem_limit_bytes=8 * MIB),
        cost_estimate=BUSY,
        name="places",
    )()


def pack_kernel(
    token_sort, cot_sort, label_row, label_col, tokens, labels, cot, own, lon, lat, dia, cot_rows
):
    outs = ((own, 0, 48), (lon, 48, 96), (lat, 96, 112), (dia, 112, 128))
    moved = mm(token_sort[...], tokens[...].reshape(128, D)).astype(bf16)
    for ref, lo, hi in outs:
        ref[:, 0:D] = moved[lo:hi]
    first = lax.axis_index("lat") == 0
    code = labels[...] + jnp.where(iota((8, 16), 1) < 4, jnp.where(first, 4, 0), 0)
    spread = mm(label_col[...], code.astype(f32).astype(bf16)) * label_row[...]
    column = jnp.sum(spread, axis=1, keepdims=True)
    wide = jnp.broadcast_to(column, (128, 128)).astype(bf16)
    for ref, lo, hi in outs:
        ref[:, 2 * D :] = wide[lo:hi]
    for r in range(8):
        cot_rows[4 * r : 4 * r + 4, :] = cot[r].astype(f32)
    stacked = jnp.concatenate(
        [cot_rows[:, s * D : (s + 1) * D].astype(bf16) for s in range(4)], axis=0
    )
    moved_cot = mm(cot_sort[...], stacked).astype(bf16)
    for ref, lo, hi in outs:
        ref[:, D : 2 * D] = moved_cot[lo:hi]


def pack(tokens, labels, cot, sorts):
    shapes = [jax.ShapeDtypeStruct((n, WIDE), bf16) for n in (48, 48, 16, 16)]
    return pl.pallas_call(
        pack_kernel,
        out_shape=shapes,
        scratch_shapes=[pltpu.VMEM((32, 4 * D), f32)],
        compiler_params=pltpu.CompilerParams(vmem_limit_bytes=12 * MIB),
        cost_estimate=BUSY,
        name="pack",
    )(*sorts, tokens, labels, cot)


def relative_bias(table, natural, ebias):
    entry, place = iota((225, 256), 0), iota((225, 256), 1)
    table_spread = onehot((entry == 15 * (place // 16) + place % 16) & (place % 16 < 15))
    entry, place = iota((256, 512), 0), iota((256, 512), 1)
    row, col = window_place(place % 64)
    toeplitz = onehot(entry == 16 * (row - place // 64 + 7) + col)
    row, col = window_place(iota((64, 64), 0))
    row_order = onehot(iota((64, 64), 1) == row * 8 + col)
    gate = 16.0 / (1.0 + jnp.exp(-table))
    high, low = halves(gate)
    spread = mm(high, table_spread) + mm(low, table_spread)
    pieces = []
    for h in range(HEADS):
        line = jnp.broadcast_to(spread[h : h + 1, :], (8, 256))
        pieces.append(pltpu.roll(line, 249, 1, stride=1, stride_axis=0))
    high, low = halves(jnp.concatenate(pieces, axis=0))
    blocks = mm(high, toeplitz) + mm(low, toeplitz)
    left = iota((8, 128), 1) < 64
    for q in range(8):
        for p in range(4):
            even = blocks[16 * q : 16 * q + 8, 128 * p : 128 * p + 128]
            odd = blocks[16 * q + 8 : 16 * q + 16, 128 * p : 128 * p + 128]
            lanes = slice(128 * q, 128 * q + 128)
            natural[16 * p : 16 * p + 8, lanes] = jnp.where(left, even, pltpu.roll(odd, 64, 1))
            natural[16 * p + 8 : 16 * p + 16, lanes] = jnp.where(
                left, pltpu.roll(even, 64, 1), odd
            )
    high, low = halves(natural[...])
    ebias[...] = jnp.exp(mm(row_order, high) + mm(row_order, low))


def prep_kernel(table, scale, ebias, temper, natural):
    relative_bias(table[...], natural, ebias)
    per_head = jnp.exp(jnp.minimum(scale[...], math.log(100.0)))
    head_of = iota((1, ATT), 1) // 32
    line = jnp.zeros((1, ATT), f32)
    for h in range(HEADS):
        line = jnp.where(head_of == h, per_head[0:1, h : h + 1], line)
    temper[...] = line


def prep(table, scale):
    return pl.pallas_call(
        prep_kernel,
        out_shape=[
            jax.ShapeDtypeStruct((CELLS, HEADS * CELLS), f32),
            jax.ShapeDtypeStruct((1, ATT), f32),
        ],
        scratch_shapes=[pltpu.VMEM((CELLS, HEADS * CELLS), f32)],
        compiler_params=pltpu.CompilerParams(vmem_limit_bytes=12 * MIB),
        cost_estimate=pl.CostEstimate(
            flops=100_000_000, bytes_accessed=400_000, transcendentals=80_000
        ),
        name="prep",
    )(table, scale)


def group_total(column):
    pair = column[0:8] + column[8:16]
    pair = pair + pltpu.roll(pair, 4, 0)
    return jnp.concatenate([pair, pair], axis=0)


def row_total(value):
    return jnp.sum(value, axis=1, keepdims=True)


def col_total(value):
    return jnp.sum(value, axis=0, keepdims=True)


def main_kernel(
    own,
    lon,
    dia,
    lat,
    ebias,
    temper,
    w_qkv,
    w_proj,
    gain,
    shift,
    merge,
    out_own,
    out_lon,
    out_lat,
    out_dia,
    x_s,
    qkv_s,
    unit_s,
    inv_s,
    unit16_s,
    seg_s,
    qbd_s,
    prob_s,
    prob16_s,
    att_s,
    proj_s,
    mixed_s,
    gproj_s,
    ga_s,
    gpack_s,
    mgain,
):
    quads = (
        (lon, out_lon, 0),
        (own, out_own, 0),
        (lon, out_lon, 16),
        (own, out_own, 16),
        (lon, out_lon, 32),
        (own, out_own, 32),
        (dia, out_dia, 0),
        (lat, out_lat, 0),
    )
    pairs = [(w, b) for w in range(2) for b in range(BLOCKS)]
    for n, (ref, _, lo) in enumerate(quads):
        x_s[16 * n : 16 * n + 16, :] = ref[lo : lo + 16, 0:D]
    for n in range(6):
        cols = slice(256 * n, 256 * n + 256)
        qkv_s[:, cols] = mm(x_s[...], w_qkv[:, cols]).astype(bf16)

    line, lane = iota((256, 128), 0), iota((256, 128), 1)
    seg = onehot((line % 128) // 32 == lane // 32)
    head_lane = iota((64, 128), 1) // 32
    head_mask = [onehot(head_lane == h) for h in range(4)]

    def store_halves(n, value):
        high, low = halves(value)
        seg_s[128 * n : 128 * n + 128, 0:128] = high
        seg_s[128 * n : 128 * n + 128, 128:256] = low

    def block_diagonal(value):
        return jnp.concatenate([value * head_mask[h] for h in range(4)], axis=0)

    def diagonal(value):
        out = value[192:256]
        for h in range(3):
            out = jnp.where(head_lane == h, value[64 * h : 64 * h + 64], out)
        return out

    for n in range(8):
        raw = qkv_s[:, 128 * n : 128 * n + 128].astype(f32)
        store_halves(n, raw * raw)
    squares = mm(seg_s[...], seg)
    for n in range(8):
        cols = slice(128 * n, 128 * n + 128)
        inv = lax.rsqrt(squares[cols] + unit_eps)
        unit = qkv_s[:, cols].astype(f32) * inv
        inv_s[:, cols] = inv
        unit_s[:, cols] = unit
        if n < BLOCKS:
            unit = unit * temper[:, cols]
        unit16_s[:, cols] = unit.astype(bf16)

    code_lane = iota((16, 128), 1)
    allowed = []
    for w in range(2):
        hot = jnp.concatenate(
            [
                onehot(ref[lo : lo + 16, 2 * D :].astype(f32).astype(jnp.int32) == code_lane)
                for ref, _, lo in quads[4 * w : 4 * w + 4]
            ],
            axis=0,
        )
        allowed.append(mm_nt(hot, jnp.concatenate([hot] * 4, axis=0)))
    for n, (w, b) in enumerate(pairs):
        rows = slice(64 * w, 64 * w + 64)
        wide = slice(256 * b, 256 * b + 256)
        qbd = block_diagonal(unit16_s[rows, 128 * b : 128 * b + 128])
        qbd_s[256 * n : 256 * n + 256, :] = qbd
        score = mm_nt(unit16_s[rows, ATT + 128 * b : ATT + 128 * b + 128], qbd)
        weight = jnp.exp(score) * ebias[:, wide] * allowed[w]
        prob = weight * (1.0 / col_total(weight))
        prob_s[rows, wide] = prob
        prob16_s[rows, wide] = prob.astype(bf16)
    for w, b in pairs:
        rows = slice(64 * w, 64 * w + 64)
        vals = qkv_s[rows, 2 * ATT + 128 * b : 2 * ATT + 128 * b + 128]
        att = diagonal(mm_tn(prob16_s[rows, 256 * b : 256 * b + 256], vals))
        att_s[rows, 128 * b : 128 * b + 128] = att.astype(bf16)

    for n in range(4):
        cols = slice(256 * n, 256 * n + 256)
        proj_s[:, cols] = mm(att_s[...], w_proj[:, cols])

    spans = [slice(16 * n, 16 * n + 16) for n in range(8)]

    def ghat_of(n):
        ref, _, lo = quads[n]
        return ref[lo : lo + 16, D : 2 * D].astype(f32) * mgain[...]

    for s in range(4):
        mgain[4 * s : 4 * s + 4, :] = jnp.broadcast_to(merge[:, s * D : (s + 1) * D], (4, D))
    mean = [row_total(proj_s[rows, :]) * (1.0 / D) for rows in spans]
    inv_std = []
    for n, rows in enumerate(spans):
        centered = proj_s[rows, :] - mean[n]
        inv_std.append(lax.rsqrt(row_total(centered * centered) * (1.0 / D) + norm_eps))
    mean_m, mean_g = [], []
    for n, rows in enumerate(spans):
        normed = (proj_s[rows, :] - mean[n]) * inv_std[n]
        proj_s[rows, :] = normed
        mixed = x_s[rows, :].astype(f32) + normed * gain[...] + shift[...]
        mixed_s[rows, :] = mixed
        mean_m.append(group_total(row_total(mixed)) * (0.25 / D))
        mean_g.append(group_total(row_total(ghat_of(n))) * (0.25 / D))
    merge_inv, slope = [], []
    for n, rows in enumerate(spans):
        cent = mixed_s[rows, :] - mean_m[n]
        ghat = ghat_of(n)
        inv = lax.rsqrt(group_total(row_total(cent * cent)) * (0.25 / D) + norm_eps)
        merge_inv.append(inv)
        slope.append(group_total(row_total(ghat * cent)) * (0.25 / D) * inv * inv)
    mean_e, mean_en = [], []
    for n, rows in enumerate(spans):
        cent = mixed_s[rows, :] - mean_m[n]
        gmixed = merge_inv[n] * (ghat_of(n) - mean_g[n] - cent * slope[n])
        mixed_s[rows, :] = gmixed
        gnorm = gmixed * gain[...]
        mean_e.append(row_total(gnorm) * (1.0 / D))
        mean_en.append(row_total(gnorm * proj_s[rows, :]) * (1.0 / D))
    for n, rows in enumerate(spans):
        gnorm = mixed_s[rows, :] * gain[...]
        gproj = inv_std[n] * (gnorm - mean_e[n] - proj_s[rows, :] * mean_en[n])
        gproj_s[rows, :] = gproj.astype(bf16)

    for n in range(2):
        cols = slice(256 * n, 256 * n + 256)
        ga_s[:, cols] = mm_nt(gproj_s[...], w_proj[cols, :]).astype(bf16)

    grad_k, grad_q = [], []
    for n, (w, b) in enumerate(pairs):
        rows = slice(64 * w, 64 * w + 64)
        wide = slice(256 * b, 256 * b + 256)
        vcols = slice(2 * ATT + 128 * b, 2 * ATT + 128 * b + 128)
        gabd = block_diagonal(ga_s[rows, 128 * b : 128 * b + 128])
        gprob = mm_nt(qkv_s[rows, vcols], gabd)
        gpack_s[rows, vcols] = mm(prob16_s[rows, wide], gabd).astype(bf16)
        prob = prob_s[rows, wide]
        gscore = prob * (gprob - col_total(prob * gprob))
        prob16_s[rows, wide] = gscore.astype(bf16)
    for n, (w, b) in enumerate(pairs):
        rows = slice(64 * w, 64 * w + 64)
        gscore = prob16_s[rows, 256 * b : 256 * b + 256]
        qcols = slice(128 * b, 128 * b + 128)
        kcols = slice(ATT + 128 * b, ATT + 128 * b + 128)
        gk = mm(gscore, qbd_s[256 * n : 256 * n + 256, :])
        gq = diagonal(mm_tn(gscore, unit16_s[rows, kcols])) * temper[:, qcols]
        proj_s[rows, qcols] = gq
        proj_s[rows, kcols] = gk
    for n in range(8):
        cols = slice(128 * n, 128 * n + 128)
        store_halves(n, unit_s[:, cols] * proj_s[:, cols])
    along = mm(seg_s[...], seg)
    for n in range(8):
        cols = slice(128 * n, 128 * n + 128)
        grad = inv_s[:, cols] * (proj_s[:, cols] - unit_s[:, cols] * along[cols])
        gpack_s[:, cols] = grad.astype(bf16)

    out_lat[16:64, :] = jnp.zeros((48, D), bf16)
    for n in range(4):
        cols = slice(256 * n, 256 * n + 256)
        total = (mixed_s[:, cols] + mm_nt(gpack_s[...], w_qkv[cols, :])).astype(bf16)
        for m, (_, ref, lo) in enumerate(quads):
            ref[lo : lo + 16, cols] = total[16 * m : 16 * m + 16]


def main(own, lon, dia, lat, *params):
    return pl.pallas_call(
        main_kernel,
        out_shape=[jax.ShapeDtypeStruct((n, D), bf16) for n in (48, 48, 64, 16)],
        scratch_shapes=[
            pltpu.VMEM((128, D), bf16),
            pltpu.VMEM((128, 3 * ATT), bf16),
            pltpu.VMEM((128, 2 * ATT), f32),
            pltpu.VMEM((128, 2 * ATT), f32),
            pltpu.VMEM((128, 2 * ATT), bf16),
            pltpu.VMEM((1024, 256), bf16),
            pltpu.VMEM((2048, 128), bf16),
            pltpu.VMEM((128, HEADS * CELLS), f32),
            pltpu.VMEM((128, HEADS * CELLS), bf16),
            pltpu.VMEM((128, ATT), bf16),
            pltpu.VMEM((128, D), f32),
            pltpu.VMEM((128, D), f32),
            pltpu.VMEM((128, D), bf16),
            pltpu.VMEM((128, ATT), bf16),
            pltpu.VMEM((128, 3 * ATT), bf16),
            pltpu.VMEM((16, D), f32),
        ],
        compiler_params=pltpu.CompilerParams(vmem_limit_bytes=24 * MIB),
        cost_estimate=pl.CostEstimate(
            flops=1_500_000_000, bytes_accessed=6_000_000, transcendentals=150_000
        ),
        name="main",
    )(own, lon, dia, lat, *params)


def final_kernel(own, lat, lon, dia, out):
    rows = jnp.concatenate([own[...], lon[...], lat[0:16, :], dia[...]], axis=0)
    row, col, _ = sorted_place(iota((128, 128), 1))
    token_place = onehot(iota((128, 128), 0) == row * 8 + col)
    out[...] = mm(token_place, rows).reshape(16, 8, D).astype(bf16)


def final(own, lon, lat, dia):
    return pl.pallas_call(
        final_kernel,
        out_shape=jax.ShapeDtypeStruct((16, 8, D), bf16),
        compiler_params=pltpu.CompilerParams(vmem_limit_bytes=8 * MIB),
        name="final",
    )(own, lat, lon, dia)


def shift_by(block, lat_step, lon_step):
    lats, lons = lax.axis_size("lat"), lax.axis_size("lon")
    route = [
        (j * lats + i, ((j + lon_step) % lons) * lats + (i + lat_step) % lats)
        for j in range(lons)
        for i in range(lats)
    ]
    return lax.ppermute(block, ("lon", "lat"), route)


def shards(
    tokens,
    labels,
    w_qkv,
    w_proj,
    logit_scale,
    bias_table,
    norm_gain,
    norm_shift,
    merge_gain,
    cotangent,
):
    own, lon, lat, dia = pack(tokens, labels.T, cotangent, places())
    lon = shift_by(lon, 0, 1)
    dia = shift_by(dia, -1, 1)
    lat = shift_by(lat, -1, 0)
    ebias, temper = prep(bias_table, logit_scale.reshape(1, HEADS))
    own, lon, lat, dia = main(
        own,
        lon,
        dia,
        lat,
        ebias,
        temper,
        w_qkv,
        w_proj,
        norm_gain.reshape(1, D),
        norm_shift.reshape(1, D),
        merge_gain.reshape(1, 4 * D),
    )
    lon = shift_by(lon, 0, -1)
    dia = shift_by(dia, 1, -1)
    lat = shift_by(lat, 1, 0)
    return final(own, lon, lat, dia)


def solution(mesh):
    placed = (
        P("lat", "lon", None),
        P("lat", "lon"),
        P(),
        P(),
        P(),
        P(),
        P(),
        P(),
        P(),
        P("lat", "lon", None),
    )
    return jax.shard_map(
        shards, mesh=mesh, in_specs=placed, out_specs=P("lat", "lon", None), check_vma=False
    )
```

```python
import math

import jax
import jax.numpy as jnp
from jax import lax
from jax.experimental import pallas as pl
from jax.experimental.pallas import tpu as pltpu
from jax.sharding import PartitionSpec as P

WIN = 8
D = 1024
HEADS = 16
ATT = 512
QUAD = 16
CELLS = 64
BLOCKS = 4
WIDE = 2 * D + 128

norm_eps = 1e-05
unit_eps = 1e-06
f32 = jnp.float32
bf16 = jnp.bfloat16
MIB = 1024 * 1024
BUSY = pl.CostEstimate(flops=10_000_000_000, bytes_accessed=30_000_000, transcendentals=0)


def sorted_place(n):
    quad = n // 16
    s = (n // 4) % 4
    g = n % 4
    row = jnp.where(quad < 6, 4 + 4 * (quad % 3), 0) + 2 * (g // 2) + s % 2
    col = jnp.where((quad // 3 == 1) | (quad == 7), 4, 0) + 2 * (g % 2) + s // 2
    return row, col, s


def window_place(n):
    row = 4 * (n // 32) + 2 * ((n // 2) % 2) + (n // 4) % 2
    col = 4 * ((n // 16) % 2) + 2 * (n % 2) + (n // 8) % 2
    return row, col


def iota(shape, axis):
    return lax.broadcasted_iota(jnp.int32, shape, axis)


def onehot(match):
    return match.astype(f32).astype(bf16)


def halves(value):
    high = value.astype(bf16)
    low = (value - high.astype(f32)).astype(bf16)
    return high, low


def mm(a, b):
    return jnp.dot(a, b, preferred_element_type=f32)


def mm_nt(a, b):
    return lax.dot_general(a, b, (((1,), (1,)), ((), ())), preferred_element_type=f32)


def mm_tn(a, b):
    return lax.dot_general(a, b, (((0,), (0,)), ((), ())), preferred_element_type=f32)


def places_kernel(token_sort, cot_sort, label_row, label_col):
    row, col, s = sorted_place(iota((128, 128), 0))
    lane = iota((128, 128), 1)
    token_sort[...] = onehot(lane == row * 8 + col)
    cot_sort[...] = onehot(lane == s * 32 + (row // 2) * 4 + col // 2)
    row, _, _ = sorted_place(iota((128, 16), 0))
    label_row[...] = (iota((128, 16), 1) == row).astype(f32)
    _, col, _ = sorted_place(iota((128, 8), 0))
    label_col[...] = onehot(iota((128, 8), 1) == col)


def places():
    return pl.pallas_call(
        places_kernel,
        out_shape=[
            jax.ShapeDtypeStruct((128, 128), bf16),
            jax.ShapeDtypeStruct((128, 128), bf16),
            jax.ShapeDtypeStruct((128, 16), f32),
            jax.ShapeDtypeStruct((128, 8), bf16),
        ],
        compiler_params=pltpu.CompilerParams(vmem_limit_bytes=8 * MIB),
        cost_estimate=BUSY,
        name="places",
    )()


def pack_kernel(
    token_sort, cot_sort, label_row, label_col, tokens, labels, cot, own, lon, lat, dia, cot_rows
):
    outs = ((own, 0, 48), (lon, 48, 96), (lat, 96, 112), (dia, 112, 128))
    moved = mm(token_sort[...], tokens[...].reshape(128, D)).astype(bf16)
    for ref, lo, hi in outs:
        ref[:, 0:D] = moved[lo:hi]
    first = lax.axis_index("lat") == 0
    code = labels[...] + jnp.where(iota((8, 16), 1) < 4, jnp.where(first, 4, 0), 0)
    spread = mm(label_col[...], code.astype(f32).astype(bf16)) * label_row[...]
    column = jnp.sum(spread, axis=1, keepdims=True)
    wide = jnp.broadcast_to(column, (128, 128)).astype(bf16)
    for ref, lo, hi in outs:
        ref[:, 2 * D :] = wide[lo:hi]
    for r in range(8):
        cot_rows[4 * r : 4 * r + 4, :] = cot[r].astype(f32)
    stacked = jnp.concatenate(
        [cot_rows[:, s * D : (s + 1) * D].astype(bf16) for s in range(4)], axis=0
    )
    moved_cot = mm(cot_sort[...], stacked).astype(bf16)
    for ref, lo, hi in outs:
        ref[:, D : 2 * D] = moved_cot[lo:hi]


def pack(tokens, labels, cot, sorts):
    shapes = [jax.ShapeDtypeStruct((n, WIDE), bf16) for n in (48, 48, 16, 16)]
    return pl.pallas_call(
        pack_kernel,
        out_shape=shapes,
        scratch_shapes=[pltpu.VMEM((32, 4 * D), f32)],
        compiler_params=pltpu.CompilerParams(vmem_limit_bytes=12 * MIB),
        cost_estimate=BUSY,
        name="pack",
    )(*sorts, tokens, labels, cot)


def relative_bias(table, natural, ebias):
    entry, place = iota((225, 256), 0), iota((225, 256), 1)
    table_spread = onehot((entry == 15 * (place // 16) + place % 16) & (place % 16 < 15))
    entry, place = iota((256, 512), 0), iota((256, 512), 1)
    row, col = window_place(place % 64)
    toeplitz = onehot(entry == 16 * (row - place // 64 + 7) + col)
    row, col = window_place(iota((64, 64), 0))
    row_order = onehot(iota((64, 64), 1) == row * 8 + col)
    gate = 16.0 / (1.0 + jnp.exp(-table))
    high, low = halves(gate)
    spread = mm(high, table_spread) + mm(low, table_spread)
    pieces = []
    for h in range(HEADS):
        line = jnp.broadcast_to(spread[h : h + 1, :], (8, 256))
        pieces.append(pltpu.roll(line, 249, 1, stride=1, stride_axis=0))
    high, low = halves(jnp.concatenate(pieces, axis=0))
    blocks = mm(high, toeplitz) + mm(low, toeplitz)
    left = iota((8, 128), 1) < 64
    for q in range(8):
        for p in range(4):
            even = blocks[16 * q : 16 * q + 8, 128 * p : 128 * p + 128]
            odd = blocks[16 * q + 8 : 16 * q + 16, 128 * p : 128 * p + 128]
            lanes = slice(128 * q, 128 * q + 128)
            natural[16 * p : 16 * p + 8, lanes] = jnp.where(left, even, pltpu.roll(odd, 64, 1))
            natural[16 * p + 8 : 16 * p + 16, lanes] = jnp.where(
                left, pltpu.roll(even, 64, 1), odd
            )
    high, low = halves(natural[...])
    ebias[...] = jnp.exp(mm(row_order, high) + mm(row_order, low))


def prep_kernel(table, scale, ebias, temper, natural):
    relative_bias(table[...], natural, ebias)
    per_head = jnp.exp(jnp.minimum(scale[...], math.log(100.0)))
    head_of = iota((1, ATT), 1) // 32
    line = jnp.zeros((1, ATT), f32)
    for h in range(HEADS):
        line = jnp.where(head_of == h, per_head[0:1, h : h + 1], line)
    temper[...] = line


def prep(table, scale):
    return pl.pallas_call(
        prep_kernel,
        out_shape=[
            jax.ShapeDtypeStruct((CELLS, HEADS * CELLS), f32),
            jax.ShapeDtypeStruct((1, ATT), f32),
        ],
        scratch_shapes=[pltpu.VMEM((CELLS, HEADS * CELLS), f32)],
        compiler_params=pltpu.CompilerParams(vmem_limit_bytes=12 * MIB),
        cost_estimate=pl.CostEstimate(
            flops=100_000_000, bytes_accessed=400_000, transcendentals=80_000
        ),
        name="prep",
    )(table, scale)


def group_total(column):
    pair = column[0:8] + column[8:16]
    pair = pair + pltpu.roll(pair, 4, 0)
    return jnp.concatenate([pair, pair], axis=0)


def row_total(value):
    return jnp.sum(value, axis=1, keepdims=True)


def col_total(value):
    return jnp.sum(value, axis=0, keepdims=True)


def main_kernel(
    own,
    lon,
    dia,
    lat,
    ebias,
    temper,
    w_qkv,
    w_proj,
    gain,
    shift,
    merge,
    out_own,
    out_lon,
    out_lat,
    out_dia,
    x_s,
    qkv_s,
    unit_s,
    inv_s,
    unit16_s,
    seg_s,
    qbd_s,
    prob_s,
    prob16_s,
    att_s,
    proj_s,
    mixed_s,
    gproj_s,
    ga_s,
    gpack_s,
    mgain,
):
    quads = (
        (lon, out_lon, 0),
        (own, out_own, 0),
        (lon, out_lon, 16),
        (own, out_own, 16),
        (lon, out_lon, 32),
        (own, out_own, 32),
        (dia, out_dia, 0),
        (lat, out_lat, 0),
    )
    pairs = [(w, b) for w in range(2) for b in range(BLOCKS)]
    for n, (ref, _, lo) in enumerate(quads):
        x_s[16 * n : 16 * n + 16, :] = ref[lo : lo + 16, 0:D]
    for n in range(6):
        cols = slice(256 * n, 256 * n + 256)
        qkv_s[:, cols] = mm(x_s[...], w_qkv[:, cols]).astype(bf16)

    line, lane = iota((256, 128), 0), iota((256, 128), 1)
    seg = onehot((line % 128) // 32 == lane // 32)
    head_lane = iota((64, 128), 1) // 32
    head_mask = [onehot(head_lane == h) for h in range(4)]

    def store_halves(n, value):
        high, low = halves(value)
        seg_s[128 * n : 128 * n + 128, 0:128] = high
        seg_s[128 * n : 128 * n + 128, 128:256] = low

    def block_diagonal(value):
        return jnp.concatenate([value * head_mask[h] for h in range(4)], axis=0)

    def diagonal(value):
        out = value[192:256]
        for h in range(3):
            out = jnp.where(head_lane == h, value[64 * h : 64 * h + 64], out)
        return out

    for n in range(8):
        raw = qkv_s[:, 128 * n : 128 * n + 128].astype(f32)
        store_halves(n, raw * raw)
    squares = mm(seg_s[...], seg)
    for n in range(8):
        cols = slice(128 * n, 128 * n + 128)
        inv = lax.rsqrt(squares[cols] + unit_eps)
        unit = qkv_s[:, cols].astype(f32) * inv
        inv_s[:, cols] = inv
        unit_s[:, cols] = unit
        if n < BLOCKS:
            unit = unit * temper[:, cols]
        unit16_s[:, cols] = unit.astype(bf16)

    code_lane = iota((16, 128), 1)
    allowed = []
    for w in range(2):
        hot = jnp.concatenate(
            [
                onehot(ref[lo : lo + 16, 2 * D :].astype(f32).astype(jnp.int32) == code_lane)
                for ref, _, lo in quads[4 * w : 4 * w + 4]
            ],
            axis=0,
        )
        allowed.append(mm_nt(hot, jnp.concatenate([hot] * 4, axis=0)))
    for n, (w, b) in enumerate(pairs):
        rows = slice(64 * w, 64 * w + 64)
        wide = slice(256 * b, 256 * b + 256)
        qbd = block_diagonal(unit16_s[rows, 128 * b : 128 * b + 128])
        qbd_s[256 * n : 256 * n + 256, :] = qbd
        score = mm_nt(unit16_s[rows, ATT + 128 * b : ATT + 128 * b + 128], qbd)
        weight = jnp.exp(score) * ebias[:, wide] * allowed[w]
        prob = weight * (1.0 / col_total(weight))
        prob_s[rows, wide] = prob
        prob16_s[rows, wide] = prob.astype(bf16)
    for w, b in pairs:
        rows = slice(64 * w, 64 * w + 64)
        vals = qkv_s[rows, 2 * ATT + 128 * b : 2 * ATT + 128 * b + 128]
        att = diagonal(mm_tn(prob16_s[rows, 256 * b : 256 * b + 256], vals))
        att_s[rows, 128 * b : 128 * b + 128] = att.astype(bf16)

    for n in range(4):
        cols = slice(256 * n, 256 * n + 256)
        proj_s[:, cols] = mm(att_s[...], w_proj[:, cols])

    spans = [slice(16 * n, 16 * n + 16) for n in range(8)]

    def ghat_of(n):
        ref, _, lo = quads[n]
        return ref[lo : lo + 16, D : 2 * D].astype(f32) * mgain[...]

    for s in range(4):
        mgain[4 * s : 4 * s + 4, :] = jnp.broadcast_to(merge[:, s * D : (s + 1) * D], (4, D))
    mean = [row_total(proj_s[rows, :]) * (1.0 / D) for rows in spans]
    inv_std = []
    for n, rows in enumerate(spans):
        centered = proj_s[rows, :] - mean[n]
        inv_std.append(lax.rsqrt(row_total(centered * centered) * (1.0 / D) + norm_eps))
    mean_m, mean_g = [], []
    for n, rows in enumerate(spans):
        normed = (proj_s[rows, :] - mean[n]) * inv_std[n]
        proj_s[rows, :] = normed
        mixed = x_s[rows, :].astype(f32) + normed * gain[...] + shift[...]
        mixed_s[rows, :] = mixed
        mean_m.append(group_total(row_total(mixed)) * (0.25 / D))
        mean_g.append(group_total(row_total(ghat_of(n))) * (0.25 / D))
    merge_inv, slope = [], []
    for n, rows in enumerate(spans):
        cent = mixed_s[rows, :] - mean_m[n]
        ghat = ghat_of(n)
        inv = lax.rsqrt(group_total(row_total(cent * cent)) * (0.25 / D) + norm_eps)
        merge_inv.append(inv)
        slope.append(group_total(row_total(ghat * cent)) * (0.25 / D) * inv * inv)
    mean_e, mean_en = [], []
    for n, rows in enumerate(spans):
        cent = mixed_s[rows, :] - mean_m[n]
        gmixed = merge_inv[n] * (ghat_of(n) - mean_g[n] - cent * slope[n])
        mixed_s[rows, :] = gmixed
        gnorm = gmixed * gain[...]
        mean_e.append(row_total(gnorm) * (1.0 / D))
        mean_en.append(row_total(gnorm * proj_s[rows, :]) * (1.0 / D))
    for n, rows in enumerate(spans):
        gnorm = mixed_s[rows, :] * gain[...]
        gproj = inv_std[n] * (gnorm - mean_e[n] - proj_s[rows, :] * mean_en[n])
        gproj_s[rows, :] = gproj.astype(bf16)

    for n in range(2):
        cols = slice(256 * n, 256 * n + 256)
        ga_s[:, cols] = mm_nt(gproj_s[...], w_proj[cols, :]).astype(bf16)

    grad_k, grad_q = [], []
    for n, (w, b) in enumerate(pairs):
        rows = slice(64 * w, 64 * w + 64)
        wide = slice(256 * b, 256 * b + 256)
        vcols = slice(2 * ATT + 128 * b, 2 * ATT + 128 * b + 128)
        gabd = block_diagonal(ga_s[rows, 128 * b : 128 * b + 128])
        gprob = mm_nt(qkv_s[rows, vcols], gabd)
        gpack_s[rows, vcols] = mm(prob16_s[rows, wide], gabd).astype(bf16)
        prob = prob_s[rows, wide]
        gscore = prob * (gprob - col_total(prob * gprob))
        prob16_s[rows, wide] = gscore.astype(bf16)
    for n, (w, b) in enumerate(pairs):
        rows = slice(64 * w, 64 * w + 64)
        gscore = prob16_s[rows, 256 * b : 256 * b + 256]
        qcols = slice(128 * b, 128 * b + 128)
        kcols = slice(ATT + 128 * b, ATT + 128 * b + 128)
        gk = mm(gscore, qbd_s[256 * n : 256 * n + 256, :])
        gq = diagonal(mm_tn(gscore, unit16_s[rows, kcols])) * temper[:, qcols]
        proj_s[rows, qcols] = gq
        proj_s[rows, kcols] = gk
    for n in range(8):
        cols = slice(128 * n, 128 * n + 128)
        store_halves(n, unit_s[:, cols] * proj_s[:, cols])
    along = mm(seg_s[...], seg)
    for n in range(8):
        cols = slice(128 * n, 128 * n + 128)
        grad = inv_s[:, cols] * (proj_s[:, cols] - unit_s[:, cols] * along[cols])
        gpack_s[:, cols] = grad.astype(bf16)

    for n in range(4):
        cols = slice(256 * n, 256 * n + 256)
        total = (mixed_s[:, cols] + mm_nt(gpack_s[...], w_qkv[cols, :])).astype(bf16)
        for m, (_, ref, lo) in enumerate(quads):
            ref[lo : lo + 16, cols] = total[16 * m : 16 * m + 16]


def main(own, lon, dia, lat, *params):
    return pl.pallas_call(
        main_kernel,
        out_shape=[jax.ShapeDtypeStruct((n, D), bf16) for n in (48, 48, 16, 16)],
        scratch_shapes=[
            pltpu.VMEM((128, D), bf16),
            pltpu.VMEM((128, 3 * ATT), bf16),
            pltpu.VMEM((128, 2 * ATT), f32),
            pltpu.VMEM((128, 2 * ATT), f32),
            pltpu.VMEM((128, 2 * ATT), bf16),
            pltpu.VMEM((1024, 256), bf16),
            pltpu.VMEM((2048, 128), bf16),
            pltpu.VMEM((128, HEADS * CELLS), f32),
            pltpu.VMEM((128, HEADS * CELLS), bf16),
            pltpu.VMEM((128, ATT), bf16),
            pltpu.VMEM((128, D), f32),
            pltpu.VMEM((128, D), f32),
            pltpu.VMEM((128, D), bf16),
            pltpu.VMEM((128, ATT), bf16),
            pltpu.VMEM((128, 3 * ATT), bf16),
            pltpu.VMEM((16, D), f32),
        ],
        compiler_params=pltpu.CompilerParams(vmem_limit_bytes=24 * MIB),
        cost_estimate=pl.CostEstimate(
            flops=1_500_000_000, bytes_accessed=6_000_000, transcendentals=150_000
        ),
        name="main",
    )(own, lon, dia, lat, *params)


def final_kernel(own, lon, dia, lat, out):
    rows = jnp.concatenate([own[...], lon[...], lat[...], dia[...]], axis=0)
    row, col, _ = sorted_place(iota((128, 128), 1))
    token_place = onehot(iota((128, 128), 0) == row * 8 + col)
    out[...] = mm(token_place, rows).reshape(16, 8, D).astype(bf16)


def final(own, lon, lat, dia):
    return pl.pallas_call(
        final_kernel,
        out_shape=jax.ShapeDtypeStruct((16, 8, D), bf16),
        compiler_params=pltpu.CompilerParams(vmem_limit_bytes=8 * MIB),
        name="final",
    )(own, lon, dia, lat)


def shift_by(block, lat_step, lon_step):
    lats, lons = lax.axis_size("lat"), lax.axis_size("lon")
    route = [
        (j * lats + i, ((j + lon_step) % lons) * lats + (i + lat_step) % lats)
        for j in range(lons)
        for i in range(lats)
    ]
    return lax.ppermute(block, ("lon", "lat"), route)


def shards(
    tokens,
    labels,
    w_qkv,
    w_proj,
    logit_scale,
    bias_table,
    norm_gain,
    norm_shift,
    merge_gain,
    cotangent,
):
    own, lon, lat, dia = pack(tokens, labels.T, cotangent, places())
    lon = shift_by(lon, 0, 1)
    dia = shift_by(dia, -1, 1)
    lat = shift_by(lat, -1, 0)
    ebias, temper = prep(bias_table, logit_scale.reshape(1, HEADS))
    own, lon, lat, dia = main(
        own,
        lon,
        dia,
        lat,
        ebias,
        temper,
        w_qkv,
        w_proj,
        norm_gain.reshape(1, D),
        norm_shift.reshape(1, D),
        merge_gain.reshape(1, 4 * D),
    )
    lon = shift_by(lon, 0, -1)
    dia = shift_by(dia, 1, -1)
    lat = shift_by(lat, 1, 0)
    return final(own, lon, lat, dia)


def solution(mesh):
    placed = (
        P("lat", "lon", None),
        P("lat", "lon"),
        P(),
        P(),
        P(),
        P(),
        P(),
        P(),
        P(),
        P("lat", "lon", None),
    )
    return jax.shard_map(
        shards, mesh=mesh, in_specs=placed, out_specs=P("lat", "lon", None), check_vma=False
    )
```

```python
import math

import jax
import jax.numpy as jnp
from jax import lax
from jax.experimental import pallas as pl
from jax.experimental.pallas import tpu as pltpu
from jax.sharding import PartitionSpec as P

WIN = 8
D = 1024
HEADS = 16
ATT = 512
QUAD = 16
CELLS = 64
BLOCKS = 4
WIDE = 2 * D + 128

norm_eps = 1e-05
unit_eps = 1e-06
f32 = jnp.float32
bf16 = jnp.bfloat16
MIB = 1024 * 1024
BUSY = pl.CostEstimate(flops=10_000_000_000, bytes_accessed=30_000_000, transcendentals=0)


def sorted_place(n):
    quad = n // 16
    s = (n // 4) % 4
    g = n % 4
    row = jnp.where(quad < 6, 4 + 4 * (quad % 3), 0) + 2 * (g // 2) + s % 2
    col = jnp.where((quad // 3 == 1) | (quad == 7), 4, 0) + 2 * (g % 2) + s // 2
    return row, col, s


def window_place(n):
    row = 4 * (n // 32) + 2 * ((n // 2) % 2) + (n // 4) % 2
    col = 4 * ((n // 16) % 2) + 2 * (n % 2) + (n // 8) % 2
    return row, col


def iota(shape, axis):
    return lax.broadcasted_iota(jnp.int32, shape, axis)


def onehot(match):
    return match.astype(f32).astype(bf16)


def halves(value):
    high = value.astype(bf16)
    low = (value - high.astype(f32)).astype(bf16)
    return high, low


def mm(a, b):
    return jnp.dot(a, b, preferred_element_type=f32)


def mm_nt(a, b):
    return lax.dot_general(a, b, (((1,), (1,)), ((), ())), preferred_element_type=f32)


def mm_tn(a, b):
    return lax.dot_general(a, b, (((0,), (0,)), ((), ())), preferred_element_type=f32)


def places_kernel(token_sort, cot_sort, label_row, label_col):
    row, col, s = sorted_place(iota((128, 128), 0))
    lane = iota((128, 128), 1)
    token_sort[...] = onehot(lane == row * 8 + col)
    cot_sort[...] = onehot(lane == s * 32 + (row // 2) * 4 + col // 2)
    row, _, _ = sorted_place(iota((128, 16), 0))
    label_row[...] = (iota((128, 16), 1) == row).astype(f32)
    _, col, _ = sorted_place(iota((128, 8), 0))
    label_col[...] = onehot(iota((128, 8), 1) == col)


def places():
    return pl.pallas_call(
        places_kernel,
        out_shape=[
            jax.ShapeDtypeStruct((128, 128), bf16),
            jax.ShapeDtypeStruct((128, 128), bf16),
            jax.ShapeDtypeStruct((128, 16), f32),
            jax.ShapeDtypeStruct((128, 8), bf16),
        ],
        compiler_params=pltpu.CompilerParams(vmem_limit_bytes=8 * MIB),
        cost_estimate=BUSY,
        name="places",
    )()


def pack_kernel(
    token_sort, cot_sort, label_row, label_col, tokens, labels, cot, own, lon, lat, dia, cot_rows
):
    outs = ((own, 0, 48), (lon, 48, 96), (lat, 96, 112), (dia, 112, 128))
    moved = mm(token_sort[...], tokens[...].reshape(128, D)).astype(bf16)
    for ref, lo, hi in outs:
        ref[:, 0:D] = moved[lo:hi]
    first = lax.axis_index("lat") == 0
    code = labels[...] + jnp.where(iota((8, 16), 1) < 4, jnp.where(first, 4, 0), 0)
    spread = mm(label_col[...], code.astype(f32).astype(bf16)) * label_row[...]
    column = jnp.sum(spread, axis=1, keepdims=True)
    wide = jnp.broadcast_to(column, (128, 128)).astype(bf16)
    for ref, lo, hi in outs:
        ref[:, 2 * D :] = wide[lo:hi]
    for r in range(8):
        cot_rows[4 * r : 4 * r + 4, :] = cot[r].astype(f32)
    stacked = jnp.concatenate(
        [cot_rows[:, s * D : (s + 1) * D].astype(bf16) for s in range(4)], axis=0
    )
    moved_cot = mm(cot_sort[...], stacked).astype(bf16)
    for ref, lo, hi in outs:
        ref[:, D : 2 * D] = moved_cot[lo:hi]


def pack(tokens, labels, cot, sorts):
    shapes = [jax.ShapeDtypeStruct((n, WIDE), bf16) for n in (48, 48, 16, 16)]
    return pl.pallas_call(
        pack_kernel,
        out_shape=shapes,
        scratch_shapes=[pltpu.VMEM((32, 4 * D), f32)],
        compiler_params=pltpu.CompilerParams(vmem_limit_bytes=12 * MIB),
        cost_estimate=BUSY,
        name="pack",
    )(*sorts, tokens, labels, cot)


def relative_bias(table, natural, ebias):
    entry, place = iota((225, 256), 0), iota((225, 256), 1)
    table_spread = onehot((entry == 15 * (place // 16) + place % 16) & (place % 16 < 15))
    entry, place = iota((256, 512), 0), iota((256, 512), 1)
    row, col = window_place(place % 64)
    toeplitz = onehot(entry == 16 * (row - place // 64 + 7) + col)
    row, col = window_place(iota((64, 64), 0))
    row_order = onehot(iota((64, 64), 1) == row * 8 + col)
    gate = 16.0 / (1.0 + jnp.exp(-table))
    high, low = halves(gate)
    spread = mm(high, table_spread) + mm(low, table_spread)
    pieces = []
    for h in range(HEADS):
        line = jnp.broadcast_to(spread[h : h + 1, :], (8, 256))
        pieces.append(pltpu.roll(line, 249, 1, stride=1, stride_axis=0))
    high, low = halves(jnp.concatenate(pieces, axis=0))
    blocks = mm(high, toeplitz) + mm(low, toeplitz)
    left = iota((8, 128), 1) < 64
    for q in range(8):
        for p in range(4):
            even = blocks[16 * q : 16 * q + 8, 128 * p : 128 * p + 128]
            odd = blocks[16 * q + 8 : 16 * q + 16, 128 * p : 128 * p + 128]
            lanes = slice(128 * q, 128 * q + 128)
            natural[16 * p : 16 * p + 8, lanes] = jnp.where(left, even, pltpu.roll(odd, 64, 1))
            natural[16 * p + 8 : 16 * p + 16, lanes] = jnp.where(
                left, pltpu.roll(even, 64, 1), odd
            )
    high, low = halves(natural[...])
    ebias[...] = jnp.exp(mm(row_order, high) + mm(row_order, low))


def prep_kernel(table, scale, ebias, temper, natural):
    relative_bias(table[...], natural, ebias)
    per_head = jnp.exp(jnp.minimum(scale[...], math.log(100.0)))
    head_of = iota((1, ATT), 1) // 32
    line = jnp.zeros((1, ATT), f32)
    for h in range(HEADS):
        line = jnp.where(head_of == h, per_head[0:1, h : h + 1], line)
    temper[...] = line


def prep(table, scale):
    return pl.pallas_call(
        prep_kernel,
        out_shape=[
            jax.ShapeDtypeStruct((CELLS, HEADS * CELLS), f32),
            jax.ShapeDtypeStruct((1, ATT), f32),
        ],
        scratch_shapes=[pltpu.VMEM((CELLS, HEADS * CELLS), f32)],
        compiler_params=pltpu.CompilerParams(vmem_limit_bytes=12 * MIB),
        cost_estimate=pl.CostEstimate(
            flops=100_000_000, bytes_accessed=400_000, transcendentals=80_000
        ),
        name="prep",
    )(table, scale)


def group_total(column):
    pair = column[0:8] + column[8:16]
    pair = pair + pltpu.roll(pair, 4, 0)
    return jnp.concatenate([pair, pair], axis=0)


def row_total(value):
    return jnp.sum(value, axis=1, keepdims=True)


def col_total(value):
    return jnp.sum(value, axis=0, keepdims=True)


def main_kernel(
    own,
    lon,
    dia,
    lat,
    ebias,
    temper,
    w_qkv,
    w_proj,
    gain,
    shift,
    merge,
    out_own,
    out_lon,
    out_lat,
    out_dia,
    x_s,
    qkv_s,
    unit_s,
    inv_s,
    unit16_s,
    seg_s,
    qbd_s,
    prob_s,
    prob16_s,
    att_s,
    proj_s,
    mixed_s,
    gproj_s,
    ga_s,
    gpack_s,
    mgain,
):
    quads = (
        (lon, out_lon, 0),
        (own, out_own, 0),
        (lon, out_lon, 16),
        (own, out_own, 16),
        (lon, out_lon, 32),
        (own, out_own, 32),
        (dia, out_dia, 0),
        (lat, out_lat, 0),
    )
    pairs = [(w, b) for w in range(2) for b in range(BLOCKS)]
    for n, (ref, _, lo) in enumerate(quads):
        x_s[16 * n : 16 * n + 16, :] = ref[lo : lo + 16, 0:D]
    for n in range(6):
        cols = slice(256 * n, 256 * n + 256)
        qkv_s[:, cols] = mm(x_s[...], w_qkv[:, cols]).astype(bf16)

    seg = onehot(iota((128, 128), 0) // 32 == iota((128, 128), 1) // 32)
    head_lane = iota((64, 128), 1) // 32
    head_mask = [onehot(head_lane == h) for h in range(4)]

    def store_terms(n, value):
        seg_s[128 * n : 128 * n + 128, :] = value.astype(bf16)

    def block_diagonal(value):
        return jnp.concatenate([value * head_mask[h] for h in range(4)], axis=0)

    def diagonal(value):
        out = value[192:256]
        for h in range(3):
            out = jnp.where(head_lane == h, value[64 * h : 64 * h + 64], out)
        return out

    for n in range(8):
        raw = qkv_s[:, 128 * n : 128 * n + 128].astype(f32)
        store_terms(n, raw * raw)
    squares = mm(seg_s[...], seg)
    for n in range(8):
        cols = slice(128 * n, 128 * n + 128)
        inv = lax.rsqrt(squares[cols] + unit_eps)
        unit = qkv_s[:, cols].astype(f32) * inv
        inv_s[:, cols] = inv
        unit_s[:, cols] = unit
        if n < BLOCKS:
            unit = unit * temper[:, cols]
        unit16_s[:, cols] = unit.astype(bf16)

    code_lane = iota((16, 128), 1)
    allowed = []
    for w in range(2):
        hot = jnp.concatenate(
            [
                onehot(ref[lo : lo + 16, 2 * D :].astype(f32).astype(jnp.int32) == code_lane)
                for ref, _, lo in quads[4 * w : 4 * w + 4]
            ],
            axis=0,
        )
        allowed.append(mm_nt(hot, jnp.concatenate([hot] * 4, axis=0)))
    for n, (w, b) in enumerate(pairs):
        rows = slice(64 * w, 64 * w + 64)
        wide = slice(256 * b, 256 * b + 256)
        qbd = block_diagonal(unit16_s[rows, 128 * b : 128 * b + 128])
        qbd_s[256 * n : 256 * n + 256, :] = qbd
        score = mm_nt(unit16_s[rows, ATT + 128 * b : ATT + 128 * b + 128], qbd)
        weight = jnp.exp(score) * ebias[:, wide] * allowed[w]
        prob = weight * (1.0 / col_total(weight))
        prob_s[rows, wide] = prob
        prob16_s[rows, wide] = prob.astype(bf16)
    for w, b in pairs:
        rows = slice(64 * w, 64 * w + 64)
        vals = qkv_s[rows, 2 * ATT + 128 * b : 2 * ATT + 128 * b + 128]
        att = diagonal(mm_tn(prob16_s[rows, 256 * b : 256 * b + 256], vals))
        att_s[rows, 128 * b : 128 * b + 128] = att.astype(bf16)

    total = jnp.zeros((128, 128), f32)
    square = jnp.zeros((128, 128), f32)
    for n in range(4):
        cols = slice(256 * n, 256 * n + 256)
        part = mm(att_s[...], w_proj[:, cols])
        proj_s[:, cols] = part
        left, right = part[:, 0:128], part[:, 128:256]
        total = total + left + right
        square = square + left * left + right * right

    spans = [slice(16 * n, 16 * n + 16) for n in range(8)]

    def ghat_of(n):
        ref, _, lo = quads[n]
        return ref[lo : lo + 16, D : 2 * D].astype(f32) * mgain[...]

    for s in range(4):
        mgain[4 * s : 4 * s + 4, :] = jnp.broadcast_to(merge[:, s * D : (s + 1) * D], (4, D))
    mean_p = row_total(total) * (1.0 / D)
    var_p = row_total(square) * (1.0 / D) - mean_p * mean_p
    inv_p = lax.rsqrt(jnp.maximum(var_p, 0.0) + norm_eps)
    mean = [mean_p[rows] for rows in spans]
    inv_std = [inv_p[rows] for rows in spans]
    mean_m, mean_g, merge_inv, slope = [], [], [], []
    for n, rows in enumerate(spans):
        normed = (proj_s[rows, :] - mean[n]) * inv_std[n]
        proj_s[rows, :] = normed
        mixed = x_s[rows, :].astype(f32) + normed * gain[...] + shift[...]
        mixed_s[rows, :] = mixed
        ghat = ghat_of(n)
        mu = group_total(row_total(mixed)) * (0.25 / D)
        mg = group_total(row_total(ghat)) * (0.25 / D)
        mm2 = group_total(row_total(mixed * mixed)) * (0.25 / D)
        mgm = group_total(row_total(ghat * mixed)) * (0.25 / D)
        inv = lax.rsqrt(jnp.maximum(mm2 - mu * mu, 0.0) + norm_eps)
        mean_m.append(mu)
        mean_g.append(mg)
        merge_inv.append(inv)
        slope.append((mgm - mg * mu) * inv * inv)
    mean_e, mean_en = [], []
    for n, rows in enumerate(spans):
        cent = mixed_s[rows, :] - mean_m[n]
        gmixed = merge_inv[n] * (ghat_of(n) - mean_g[n] - cent * slope[n])
        mixed_s[rows, :] = gmixed
        gnorm = gmixed * gain[...]
        mean_e.append(row_total(gnorm) * (1.0 / D))
        mean_en.append(row_total(gnorm * proj_s[rows, :]) * (1.0 / D))
    for n, rows in enumerate(spans):
        gnorm = mixed_s[rows, :] * gain[...]
        gproj = inv_std[n] * (gnorm - mean_e[n] - proj_s[rows, :] * mean_en[n])
        gproj_s[rows, :] = gproj.astype(bf16)

    for n in range(2):
        cols = slice(256 * n, 256 * n + 256)
        ga_s[:, cols] = mm_nt(gproj_s[...], w_proj[cols, :]).astype(bf16)

    grad_k, grad_q = [], []
    for n, (w, b) in enumerate(pairs):
        rows = slice(64 * w, 64 * w + 64)
        wide = slice(256 * b, 256 * b + 256)
        vcols = slice(2 * ATT + 128 * b, 2 * ATT + 128 * b + 128)
        gabd = block_diagonal(ga_s[rows, 128 * b : 128 * b + 128])
        gprob = mm_nt(qkv_s[rows, vcols], gabd)
        gpack_s[rows, vcols] = mm(prob16_s[rows, wide], gabd).astype(bf16)
        prob = prob_s[rows, wide]
        gscore = prob * (gprob - col_total(prob * gprob))
        prob16_s[rows, wide] = gscore.astype(bf16)
    for n, (w, b) in enumerate(pairs):
        rows = slice(64 * w, 64 * w + 64)
        gscore = prob16_s[rows, 256 * b : 256 * b + 256]
        qcols = slice(128 * b, 128 * b + 128)
        kcols = slice(ATT + 128 * b, ATT + 128 * b + 128)
        gk = mm(gscore, qbd_s[256 * n : 256 * n + 256, :])
        gq = diagonal(mm_tn(gscore, unit16_s[rows, kcols])) * temper[:, qcols]
        proj_s[rows, qcols] = gq
        proj_s[rows, kcols] = gk
    for n in range(8):
        cols = slice(128 * n, 128 * n + 128)
        store_terms(n, unit_s[:, cols] * proj_s[:, cols])
    along = mm(seg_s[...], seg)
    for n in range(8):
        cols = slice(128 * n, 128 * n + 128)
        grad = inv_s[:, cols] * (proj_s[:, cols] - unit_s[:, cols] * along[cols])
        gpack_s[:, cols] = grad.astype(bf16)

    for n in range(4):
        cols = slice(256 * n, 256 * n + 256)
        total = (mixed_s[:, cols] + mm_nt(gpack_s[...], w_qkv[cols, :])).astype(bf16)
        for m, (_, ref, lo) in enumerate(quads):
            ref[lo : lo + 16, cols] = total[16 * m : 16 * m + 16]


def main(own, lon, dia, lat, *params):
    return pl.pallas_call(
        main_kernel,
        out_shape=[jax.ShapeDtypeStruct((n, D), bf16) for n in (48, 48, 16, 16)],
        scratch_shapes=[
            pltpu.VMEM((128, D), bf16),
            pltpu.VMEM((128, 3 * ATT), bf16),
            pltpu.VMEM((128, 2 * ATT), f32),
            pltpu.VMEM((128, 2 * ATT), f32),
            pltpu.VMEM((128, 2 * ATT), bf16),
            pltpu.VMEM((1024, 128), bf16),
            pltpu.VMEM((2048, 128), bf16),
            pltpu.VMEM((128, HEADS * CELLS), f32),
            pltpu.VMEM((128, HEADS * CELLS), bf16),
            pltpu.VMEM((128, ATT), bf16),
            pltpu.VMEM((128, D), f32),
            pltpu.VMEM((128, D), f32),
            pltpu.VMEM((128, D), bf16),
            pltpu.VMEM((128, ATT), bf16),
            pltpu.VMEM((128, 3 * ATT), bf16),
            pltpu.VMEM((16, D), f32),
        ],
        compiler_params=pltpu.CompilerParams(vmem_limit_bytes=24 * MIB),
        cost_estimate=pl.CostEstimate(
            flops=1_500_000_000, bytes_accessed=6_000_000, transcendentals=150_000
        ),
        name="main",
    )(own, lon, dia, lat, *params)


def final_kernel(own, lat, lon, dia, out):
    rows = jnp.concatenate([own[...], lon[...], lat[...], dia[...]], axis=0)
    row, col, _ = sorted_place(iota((128, 128), 1))
    token_place = onehot(iota((128, 128), 0) == row * 8 + col)
    out[...] = mm(token_place, rows).reshape(16, 8, D).astype(bf16)


def final(own, lon, lat, dia):
    return pl.pallas_call(
        final_kernel,
        out_shape=jax.ShapeDtypeStruct((16, 8, D), bf16),
        compiler_params=pltpu.CompilerParams(vmem_limit_bytes=8 * MIB),
        name="final",
    )(own, lat, lon, dia)


def shift_by(block, lat_step, lon_step):
    lats, lons = lax.axis_size("lat"), lax.axis_size("lon")
    route = [
        (j * lats + i, ((j + lon_step) % lons) * lats + (i + lat_step) % lats)
        for j in range(lons)
        for i in range(lats)
    ]
    return lax.ppermute(block, ("lon", "lat"), route)


def shards(
    tokens,
    labels,
    w_qkv,
    w_proj,
    logit_scale,
    bias_table,
    norm_gain,
    norm_shift,
    merge_gain,
    cotangent,
):
    own, lon, lat, dia = pack(tokens, labels.T, cotangent, places())
    lon = shift_by(lon, 0, 1)
    dia = shift_by(dia, -1, 1)
    lat = shift_by(lat, -1, 0)
    ebias, temper = prep(bias_table, logit_scale.reshape(1, HEADS))
    own, lon, lat, dia = main(
        own,
        lon,
        dia,
        lat,
        ebias,
        temper,
        w_qkv,
        w_proj,
        norm_gain.reshape(1, D),
        norm_shift.reshape(1, D),
        merge_gain.reshape(1, 4 * D),
    )
    lon = shift_by(lon, 0, -1)
    dia = shift_by(dia, 1, -1)
    lat = shift_by(lat, 1, 0)
    return final(own, lon, lat, dia)


def solution(mesh):
    placed = (
        P("lat", "lon", None),
        P("lat", "lon"),
        P(),
        P(),
        P(),
        P(),
        P(),
        P(),
        P(),
        P("lat", "lon", None),
    )
    return jax.shard_map(
        shards, mesh=mesh, in_specs=placed, out_specs=P("lat", "lon", None), check_vma=False
    )
```

```python
import math

import jax
import jax.numpy as jnp
from jax import lax
from jax.experimental import pallas as pl
from jax.experimental.pallas import tpu as pltpu
from jax.sharding import PartitionSpec as P

WIN = 8
D = 1024
HEADS = 16
ATT = 512
QUAD = 16
CELLS = 64
BLOCKS = 4
WIDE = 2 * D + 128

norm_eps = 1e-05
unit_eps = 1e-06
f32 = jnp.float32
bf16 = jnp.bfloat16
MIB = 1024 * 1024
BUSY = pl.CostEstimate(flops=10_000_000_000, bytes_accessed=30_000_000, transcendentals=0)


def sorted_place(n):
    quad = n // 16
    s = (n // 4) % 4
    g = n % 4
    row = jnp.where(quad < 6, 4 * (quad % 3), 12) + 2 * (g // 2) + s % 2
    col = jnp.where((quad // 3 == 1) | (quad == 7), 4, 0) + 2 * (g % 2) + s // 2
    return row, col, s


def window_place(n):
    row = 4 * (n // 32) + 2 * ((n // 2) % 2) + (n // 4) % 2
    col = 4 * ((n // 16) % 2) + 2 * (n % 2) + (n // 8) % 2
    return row, col


def iota(shape, axis):
    return lax.broadcasted_iota(jnp.int32, shape, axis)


def onehot(match):
    return match.astype(f32).astype(bf16)


def halves(value):
    high = value.astype(bf16)
    low = (value - high.astype(f32)).astype(bf16)
    return high, low


def mm(a, b):
    return jnp.dot(a, b, preferred_element_type=f32)


def mm_nt(a, b):
    return lax.dot_general(a, b, (((1,), (1,)), ((), ())), preferred_element_type=f32)


def mm_tn(a, b):
    return lax.dot_general(a, b, (((0,), (0,)), ((), ())), preferred_element_type=f32)


def places_kernel(token_sort, cot_sort, label_row, label_col):
    row, col, s = sorted_place(iota((128, 128), 0))
    lane = iota((128, 128), 1)
    token_sort[...] = onehot(lane == row * 8 + col)
    cot_sort[...] = onehot(lane == s * 32 + (row // 2) * 4 + col // 2)
    row, _, _ = sorted_place(iota((128, 16), 0))
    label_row[...] = (iota((128, 16), 1) == row).astype(f32)
    _, col, _ = sorted_place(iota((128, 8), 0))
    label_col[...] = onehot(iota((128, 8), 1) == col)


def places():
    return pl.pallas_call(
        places_kernel,
        out_shape=[
            jax.ShapeDtypeStruct((128, 128), bf16),
            jax.ShapeDtypeStruct((128, 128), bf16),
            jax.ShapeDtypeStruct((128, 16), f32),
            jax.ShapeDtypeStruct((128, 8), bf16),
        ],
        compiler_params=pltpu.CompilerParams(vmem_limit_bytes=8 * MIB),
        cost_estimate=BUSY,
        name="places",
    )()


def pack_kernel(
    token_sort, cot_sort, label_row, label_col, tokens, labels, cot, own, lon, lat, dia, cot_rows
):
    outs = ((own, 0, 48), (lon, 48, 96), (lat, 96, 112), (dia, 112, 128))
    moved = mm(token_sort[...], tokens[...].reshape(128, D)).astype(bf16)
    for ref, lo, hi in outs:
        ref[:, 0:D] = moved[lo:hi]
    first = lax.axis_index("lat") == 0
    code = labels[...] + jnp.where(iota((8, 16), 1) < 4, jnp.where(first, 4, 0), 0)
    spread = mm(label_col[...], code.astype(f32).astype(bf16)) * label_row[...]
    column = jnp.sum(spread, axis=1, keepdims=True)
    wide = jnp.broadcast_to(column, (128, 128)).astype(bf16)
    for ref, lo, hi in outs:
        ref[:, 2 * D :] = wide[lo:hi]
    for r in range(8):
        cot_rows[4 * r : 4 * r + 4, :] = cot[r].astype(f32)
    stacked = jnp.concatenate(
        [cot_rows[:, s * D : (s + 1) * D].astype(bf16) for s in range(4)], axis=0
    )
    moved_cot = mm(cot_sort[...], stacked).astype(bf16)
    for ref, lo, hi in outs:
        ref[:, D : 2 * D] = moved_cot[lo:hi]


def pack(tokens, labels, cot, sorts):
    shapes = [jax.ShapeDtypeStruct((n, WIDE), bf16) for n in (48, 48, 16, 16)]
    return pl.pallas_call(
        pack_kernel,
        out_shape=shapes,
        scratch_shapes=[pltpu.VMEM((32, 4 * D), f32)],
        compiler_params=pltpu.CompilerParams(vmem_limit_bytes=12 * MIB),
        cost_estimate=BUSY,
        name="pack",
    )(*sorts, tokens, labels, cot)


def relative_bias(table, natural, ebias):
    entry, place = iota((225, 256), 0), iota((225, 256), 1)
    table_spread = onehot((entry == 15 * (place // 16) + place % 16) & (place % 16 < 15))
    entry, place = iota((256, 512), 0), iota((256, 512), 1)
    row, col = window_place(place % 64)
    toeplitz = onehot(entry == 16 * (row - place // 64 + 7) + col)
    row, col = window_place(iota((64, 64), 0))
    row_order = onehot(iota((64, 64), 1) == row * 8 + col)
    gate = 16.0 / (1.0 + jnp.exp(-table))
    high, low = halves(gate)
    spread = mm(high, table_spread) + mm(low, table_spread)
    pieces = []
    for h in range(HEADS):
        line = jnp.broadcast_to(spread[h : h + 1, :], (8, 256))
        pieces.append(pltpu.roll(line, 249, 1, stride=1, stride_axis=0))
    high, low = halves(jnp.concatenate(pieces, axis=0))
    blocks = mm(high, toeplitz) + mm(low, toeplitz)
    left = iota((8, 128), 1) < 64
    for q in range(8):
        for p in range(4):
            even = blocks[16 * q : 16 * q + 8, 128 * p : 128 * p + 128]
            odd = blocks[16 * q + 8 : 16 * q + 16, 128 * p : 128 * p + 128]
            lanes = slice(128 * q, 128 * q + 128)
            natural[16 * p : 16 * p + 8, lanes] = jnp.where(left, even, pltpu.roll(odd, 64, 1))
            natural[16 * p + 8 : 16 * p + 16, lanes] = jnp.where(
                left, pltpu.roll(even, 64, 1), odd
            )
    high, low = halves(natural[...])
    ebias[...] = jnp.exp(mm(row_order, high) + mm(row_order, low))


def prep_kernel(table, scale, ebias, temper, natural):
    relative_bias(table[...], natural, ebias)
    per_head = jnp.exp(jnp.minimum(scale[...], math.log(100.0)))
    head_of = iota((1, ATT), 1) // 32
    line = jnp.zeros((1, ATT), f32)
    for h in range(HEADS):
        line = jnp.where(head_of == h, per_head[0:1, h : h + 1], line)
    temper[...] = line


def prep(table, scale):
    return pl.pallas_call(
        prep_kernel,
        out_shape=[
            jax.ShapeDtypeStruct((CELLS, HEADS * CELLS), f32),
            jax.ShapeDtypeStruct((1, ATT), f32),
        ],
        scratch_shapes=[pltpu.VMEM((CELLS, HEADS * CELLS), f32)],
        compiler_params=pltpu.CompilerParams(vmem_limit_bytes=12 * MIB),
        cost_estimate=pl.CostEstimate(
            flops=100_000_000, bytes_accessed=400_000, transcendentals=80_000
        ),
        name="prep",
    )(table, scale)


def group_total(column):
    pair = column[0:8] + column[8:16]
    pair = pair + pltpu.roll(pair, 4, 0)
    return jnp.concatenate([pair, pair], axis=0)


def row_total(value):
    return jnp.sum(value, axis=1, keepdims=True)


def col_total(value):
    return jnp.sum(value, axis=0, keepdims=True)


def main_kernel(
    own,
    lon,
    dia,
    lat,
    ebias,
    temper,
    w_qkv,
    w_proj,
    gain,
    shift,
    merge,
    out_own,
    out_lon,
    out_lat,
    out_dia,
    x_s,
    qkv_s,
    unit_s,
    inv_s,
    unit16_s,
    seg_s,
    qbd_s,
    prob_s,
    prob16_s,
    att_s,
    proj_s,
    mixed_s,
    gproj_s,
    ga_s,
    gpack_s,
    mgain,
):
    quads = (
        (dia, out_dia, 0),
        (lat, out_lat, 0),
        (lon, out_lon, 0),
        (own, out_own, 0),
        (lon, out_lon, 16),
        (own, out_own, 16),
        (lon, out_lon, 32),
        (own, out_own, 32),
    )
    pairs = [(w, b) for w in range(2) for b in range(BLOCKS)]
    for n, (ref, _, lo) in enumerate(quads):
        x_s[16 * n : 16 * n + 16, :] = ref[lo : lo + 16, 0:D]
    for n in range(6):
        cols = slice(256 * n, 256 * n + 256)
        qkv_s[:, cols] = mm(x_s[...], w_qkv[:, cols]).astype(bf16)

    seg = onehot(iota((128, 128), 0) // 32 == iota((128, 128), 1) // 32)
    head_lane = iota((64, 128), 1) // 32
    head_mask = [onehot(head_lane == h) for h in range(4)]

    def store_terms(n, value):
        seg_s[128 * n : 128 * n + 128, :] = value.astype(bf16)

    def block_diagonal(value):
        return jnp.concatenate([value * head_mask[h] for h in range(4)], axis=0)

    def diagonal(value):
        out = value[192:256]
        for h in range(3):
            out = jnp.where(head_lane == h, value[64 * h : 64 * h + 64], out)
        return out

    for n in range(8):
        raw = qkv_s[:, 128 * n : 128 * n + 128].astype(f32)
        store_terms(n, raw * raw)
    squares = mm(seg_s[...], seg)
    for n in range(8):
        cols = slice(128 * n, 128 * n + 128)
        inv = lax.rsqrt(squares[cols] + unit_eps)
        unit = qkv_s[:, cols].astype(f32) * inv
        inv_s[:, cols] = inv
        unit_s[:, cols] = unit
        if n < BLOCKS:
            unit = unit * temper[:, cols]
        unit16_s[:, cols] = unit.astype(bf16)

    code_lane = iota((16, 128), 1)
    allowed = []
    for w in range(2):
        hot = jnp.concatenate(
            [
                onehot(ref[lo : lo + 16, 2 * D :].astype(f32).astype(jnp.int32) == code_lane)
                for ref, _, lo in quads[4 * w : 4 * w + 4]
            ],
            axis=0,
        )
        allowed.append(mm_nt(hot, jnp.concatenate([hot] * 4, axis=0)))
    for n, (w, b) in enumerate(pairs):
        rows = slice(64 * w, 64 * w + 64)
        wide = slice(256 * b, 256 * b + 256)
        qbd = block_diagonal(unit16_s[rows, 128 * b : 128 * b + 128])
        qbd_s[256 * n : 256 * n + 256, :] = qbd
        score = mm_nt(unit16_s[rows, ATT + 128 * b : ATT + 128 * b + 128], qbd)
        weight = jnp.exp(score) * ebias[:, wide] * allowed[w]
        prob = weight * (1.0 / col_total(weight))
        prob_s[rows, wide] = prob
        prob16_s[rows, wide] = prob.astype(bf16)
    for w, b in pairs:
        rows = slice(64 * w, 64 * w + 64)
        vals = qkv_s[rows, 2 * ATT + 128 * b : 2 * ATT + 128 * b + 128]
        att = diagonal(mm_tn(prob16_s[rows, 256 * b : 256 * b + 256], vals))
        att_s[rows, 128 * b : 128 * b + 128] = att.astype(bf16)

    total = jnp.zeros((128, 128), f32)
    square = jnp.zeros((128, 128), f32)
    for n in range(4):
        cols = slice(256 * n, 256 * n + 256)
        part = mm(att_s[...], w_proj[:, cols])
        proj_s[:, cols] = part
        left, right = part[:, 0:128], part[:, 128:256]
        total = total + left + right
        square = square + left * left + right * right

    spans = [slice(16 * n, 16 * n + 16) for n in range(8)]

    def ghat_of(n):
        ref, _, lo = quads[n]
        return ref[lo : lo + 16, D : 2 * D].astype(f32) * mgain[...]

    for s in range(4):
        mgain[4 * s : 4 * s + 4, :] = jnp.broadcast_to(merge[:, s * D : (s + 1) * D], (4, D))
    mean_p = row_total(total) * (1.0 / D)
    var_p = row_total(square) * (1.0 / D) - mean_p * mean_p
    inv_p = lax.rsqrt(jnp.maximum(var_p, 0.0) + norm_eps)
    mean = [mean_p[rows] for rows in spans]
    inv_std = [inv_p[rows] for rows in spans]
    mean_m, mean_g, merge_inv, slope = [], [], [], []
    for n, rows in enumerate(spans):
        normed = (proj_s[rows, :] - mean[n]) * inv_std[n]
        proj_s[rows, :] = normed
        mixed = x_s[rows, :].astype(f32) + normed * gain[...] + shift[...]
        mixed_s[rows, :] = mixed
        ghat = ghat_of(n)
        mu = group_total(row_total(mixed)) * (0.25 / D)
        mg = group_total(row_total(ghat)) * (0.25 / D)
        mm2 = group_total(row_total(mixed * mixed)) * (0.25 / D)
        mgm = group_total(row_total(ghat * mixed)) * (0.25 / D)
        inv = lax.rsqrt(jnp.maximum(mm2 - mu * mu, 0.0) + norm_eps)
        mean_m.append(mu)
        mean_g.append(mg)
        merge_inv.append(inv)
        slope.append((mgm - mg * mu) * inv * inv)
    mean_e, mean_en = [], []
    for n, rows in enumerate(spans):
        cent = mixed_s[rows, :] - mean_m[n]
        gmixed = merge_inv[n] * (ghat_of(n) - mean_g[n] - cent * slope[n])
        mixed_s[rows, :] = gmixed
        gnorm = gmixed * gain[...]
        mean_e.append(row_total(gnorm) * (1.0 / D))
        mean_en.append(row_total(gnorm * proj_s[rows, :]) * (1.0 / D))
    for n, rows in enumerate(spans):
        gnorm = mixed_s[rows, :] * gain[...]
        gproj = inv_std[n] * (gnorm - mean_e[n] - proj_s[rows, :] * mean_en[n])
        gproj_s[rows, :] = gproj.astype(bf16)

    for n in range(2):
        cols = slice(256 * n, 256 * n + 256)
        ga_s[:, cols] = mm_nt(gproj_s[...], w_proj[cols, :]).astype(bf16)

    grad_k, grad_q = [], []
    for n, (w, b) in enumerate(pairs):
        rows = slice(64 * w, 64 * w + 64)
        wide = slice(256 * b, 256 * b + 256)
        vcols = slice(2 * ATT + 128 * b, 2 * ATT + 128 * b + 128)
        gabd = block_diagonal(ga_s[rows, 128 * b : 128 * b + 128])
        gprob = mm_nt(qkv_s[rows, vcols], gabd)
        gpack_s[rows, vcols] = mm(prob16_s[rows, wide], gabd).astype(bf16)
        prob = prob_s[rows, wide]
        gscore = prob * (gprob - col_total(prob * gprob))
        prob16_s[rows, wide] = gscore.astype(bf16)
    for n, (w, b) in enumerate(pairs):
        rows = slice(64 * w, 64 * w + 64)
        gscore = prob16_s[rows, 256 * b : 256 * b + 256]
        qcols = slice(128 * b, 128 * b + 128)
        kcols = slice(ATT + 128 * b, ATT + 128 * b + 128)
        gk = mm(gscore, qbd_s[256 * n : 256 * n + 256, :])
        gq = diagonal(mm_tn(gscore, unit16_s[rows, kcols])) * temper[:, qcols]
        proj_s[rows, qcols] = gq
        proj_s[rows, kcols] = gk
    for n in range(8):
        cols = slice(128 * n, 128 * n + 128)
        store_terms(n, unit_s[:, cols] * proj_s[:, cols])
    along = mm(seg_s[...], seg)
    for n in range(8):
        cols = slice(128 * n, 128 * n + 128)
        grad = inv_s[:, cols] * (proj_s[:, cols] - unit_s[:, cols] * along[cols])
        gpack_s[:, cols] = grad.astype(bf16)

    for n in range(4):
        cols = slice(256 * n, 256 * n + 256)
        total = (mixed_s[:, cols] + mm_nt(gpack_s[...], w_qkv[cols, :])).astype(bf16)
        for m, (_, ref, lo) in enumerate(quads):
            ref[lo : lo + 16, cols] = total[16 * m : 16 * m + 16]


def main(own, lon, dia, lat, *params):
    return pl.pallas_call(
        main_kernel,
        out_shape=[jax.ShapeDtypeStruct((n, D), bf16) for n in (48, 48, 16, 16)],
        scratch_shapes=[
            pltpu.VMEM((128, D), bf16),
            pltpu.VMEM((128, 3 * ATT), bf16),
            pltpu.VMEM((128, 2 * ATT), f32),
            pltpu.VMEM((128, 2 * ATT), f32),
            pltpu.VMEM((128, 2 * ATT), bf16),
            pltpu.VMEM((1024, 128), bf16),
            pltpu.VMEM((2048, 128), bf16),
            pltpu.VMEM((128, HEADS * CELLS), f32),
            pltpu.VMEM((128, HEADS * CELLS), bf16),
            pltpu.VMEM((128, ATT), bf16),
            pltpu.VMEM((128, D), f32),
            pltpu.VMEM((128, D), f32),
            pltpu.VMEM((128, D), bf16),
            pltpu.VMEM((128, ATT), bf16),
            pltpu.VMEM((128, 3 * ATT), bf16),
            pltpu.VMEM((16, D), f32),
        ],
        compiler_params=pltpu.CompilerParams(vmem_limit_bytes=24 * MIB),
        cost_estimate=pl.CostEstimate(
            flops=1_500_000_000, bytes_accessed=6_000_000, transcendentals=150_000
        ),
        name="main",
    )(own, lon, dia, lat, *params)


def final_kernel(own, lat, lon, dia, out):
    rows = jnp.concatenate([own[...], lon[...], lat[...], dia[...]], axis=0)
    row, col, _ = sorted_place(iota((128, 128), 1))
    token_place = onehot(iota((128, 128), 0) == row * 8 + col)
    out[...] = mm(token_place, rows).reshape(16, 8, D).astype(bf16)


def final(own, lon, lat, dia):
    return pl.pallas_call(
        final_kernel,
        out_shape=jax.ShapeDtypeStruct((16, 8, D), bf16),
        compiler_params=pltpu.CompilerParams(vmem_limit_bytes=8 * MIB),
        name="final",
    )(own, lat, lon, dia)


def shift_by(block, lat_step, lon_step):
    lats, lons = lax.axis_size("lat"), lax.axis_size("lon")
    route = [
        (j * lats + i, ((j + lon_step) % lons) * lats + (i + lat_step) % lats)
        for j in range(lons)
        for i in range(lats)
    ]
    return lax.ppermute(block, ("lon", "lat"), route)


def shards(
    tokens,
    labels,
    w_qkv,
    w_proj,
    logit_scale,
    bias_table,
    norm_gain,
    norm_shift,
    merge_gain,
    cotangent,
):
    own, lon, lat, dia = pack(tokens, labels.T, cotangent, places())
    lon = shift_by(lon, 0, 1)
    dia = shift_by(dia, 1, 1)
    lat = shift_by(lat, 1, 0)
    ebias, temper = prep(bias_table, logit_scale.reshape(1, HEADS))
    own, lon, lat, dia = main(
        own,
        lon,
        dia,
        lat,
        ebias,
        temper,
        w_qkv,
        w_proj,
        norm_gain.reshape(1, D),
        norm_shift.reshape(1, D),
        merge_gain.reshape(1, 4 * D),
    )
    lon = shift_by(lon, 0, -1)
    dia = shift_by(dia, -1, -1)
    lat = shift_by(lat, -1, 0)
    return final(own, lon, lat, dia)


def solution(mesh):
    placed = (
        P("lat", "lon", None),
        P("lat", "lon"),
        P(),
        P(),
        P(),
        P(),
        P(),
        P(),
        P(),
        P("lat", "lon", None),
    )
    return jax.shard_map(
        shards, mesh=mesh, in_specs=placed, out_specs=P("lat", "lon", None), check_vma=False
    )
```

```python
import math

import jax
import jax.numpy as jnp
from jax import lax
from jax.experimental import pallas as pl
from jax.experimental.pallas import tpu as pltpu
from jax.sharding import PartitionSpec as P

WIN = 8
D = 1024
HEADS = 16
ATT = 512
QUAD = 16
CELLS = 64
BLOCKS = 4
WIDE = 2 * D + 128

norm_eps = 1e-05
unit_eps = 1e-06
f32 = jnp.float32
bf16 = jnp.bfloat16
MIB = 1024 * 1024
BUSY = pl.CostEstimate(flops=10_000_000_000, bytes_accessed=30_000_000, transcendentals=0)


def sorted_place(n):
    quad = n // 16
    s = (n // 4) % 4
    g = n % 4
    row = 4 * (quad % 4) + 2 * (g // 2) + s % 2
    col = 4 * (quad // 4) + 2 * (g % 2) + s // 2
    return row, col, s


def window_place(n):
    row = 4 * (n // 32) + 2 * ((n // 2) % 2) + (n // 4) % 2
    col = 4 * ((n // 16) % 2) + 2 * (n % 2) + (n // 8) % 2
    return row, col


def iota(shape, axis):
    return lax.broadcasted_iota(jnp.int32, shape, axis)


def onehot(match):
    return match.astype(f32).astype(bf16)


def halves(value):
    high = value.astype(bf16)
    low = (value - high.astype(f32)).astype(bf16)
    return high, low


def mm(a, b):
    return jnp.dot(a, b, preferred_element_type=f32)


def mm_nt(a, b):
    return lax.dot_general(a, b, (((1,), (1,)), ((), ())), preferred_element_type=f32)


def mm_tn(a, b):
    return lax.dot_general(a, b, (((0,), (0,)), ((), ())), preferred_element_type=f32)


def places_kernel(token_sort, cot_sort, label_row, label_col):
    row, col, s = sorted_place(iota((128, 128), 0))
    lane = iota((128, 128), 1)
    token_sort[...] = onehot(lane == row * 8 + col)
    cot_sort[...] = onehot(lane == s * 32 + (row // 2) * 4 + col // 2)
    row, _, _ = sorted_place(iota((128, 16), 0))
    label_row[...] = (iota((128, 16), 1) == row).astype(f32)
    _, col, _ = sorted_place(iota((128, 8), 0))
    label_col[...] = onehot(iota((128, 8), 1) == col)


def places():
    return pl.pallas_call(
        places_kernel,
        out_shape=[
            jax.ShapeDtypeStruct((128, 128), bf16),
            jax.ShapeDtypeStruct((128, 128), bf16),
            jax.ShapeDtypeStruct((128, 16), f32),
            jax.ShapeDtypeStruct((128, 8), bf16),
        ],
        compiler_params=pltpu.CompilerParams(vmem_limit_bytes=8 * MIB),
        cost_estimate=BUSY,
        name="places",
    )()


def pack_kernel(
    token_sort, cot_sort, label_row, label_col, tokens, labels, cot, own, lon, cot_rows
):
    outs = ((own, 0, 64), (lon, 64, 128))
    moved = mm(token_sort[...], tokens[...].reshape(128, D)).astype(bf16)
    for ref, lo, hi in outs:
        ref[:, 0:D] = moved[lo:hi]
    first = lax.axis_index("lat") == 0
    code = labels[...] + jnp.where(iota((8, 16), 1) < 4, jnp.where(first, 4, 0), 0)
    spread = mm(label_col[...], code.astype(f32).astype(bf16)) * label_row[...]
    column = jnp.sum(spread, axis=1, keepdims=True)
    wide = jnp.broadcast_to(column, (128, 128)).astype(bf16)
    for ref, lo, hi in outs:
        ref[:, 2 * D :] = wide[lo:hi]
    for r in range(8):
        cot_rows[4 * r : 4 * r + 4, :] = cot[r].astype(f32)
    stacked = jnp.concatenate(
        [cot_rows[:, s * D : (s + 1) * D].astype(bf16) for s in range(4)], axis=0
    )
    moved_cot = mm(cot_sort[...], stacked).astype(bf16)
    for ref, lo, hi in outs:
        ref[:, D : 2 * D] = moved_cot[lo:hi]


def pack(tokens, labels, cot, sorts):
    shapes = [jax.ShapeDtypeStruct((64, WIDE), bf16)] * 2
    return pl.pallas_call(
        pack_kernel,
        out_shape=shapes,
        scratch_shapes=[pltpu.VMEM((32, 4 * D), f32)],
        compiler_params=pltpu.CompilerParams(vmem_limit_bytes=12 * MIB),
        cost_estimate=BUSY,
        name="pack",
    )(*sorts, tokens, labels, cot)


def strips_kernel(own, lon, top, bottom):
    top[0:16, :] = lon[0:16, :]
    top[16:32, :] = own[0:16, :]
    bottom[0:16, :] = lon[48:64, :]
    bottom[16:32, :] = own[48:64, :]


def strips(own, lon):
    return pl.pallas_call(
        strips_kernel,
        out_shape=[jax.ShapeDtypeStruct((32, WIDE), bf16)] * 2,
        compiler_params=pltpu.CompilerParams(vmem_limit_bytes=4 * MIB),
        name="strips",
    )(own, lon)


def relative_bias(table, natural, ebias):
    entry, place = iota((225, 256), 0), iota((225, 256), 1)
    table_spread = onehot((entry == 15 * (place // 16) + place % 16) & (place % 16 < 15))
    entry, place = iota((256, 512), 0), iota((256, 512), 1)
    row, col = window_place(place % 64)
    toeplitz = onehot(entry == 16 * (row - place // 64 + 7) + col)
    row, col = window_place(iota((64, 64), 0))
    row_order = onehot(iota((64, 64), 1) == row * 8 + col)
    gate = 16.0 / (1.0 + jnp.exp(-table))
    high, low = halves(gate)
    spread = mm(high, table_spread) + mm(low, table_spread)
    pieces = []
    for h in range(HEADS):
        line = jnp.broadcast_to(spread[h : h + 1, :], (8, 256))
        pieces.append(pltpu.roll(line, 249, 1, stride=1, stride_axis=0))
    high, low = halves(jnp.concatenate(pieces, axis=0))
    blocks = mm(high, toeplitz) + mm(low, toeplitz)
    left = iota((8, 128), 1) < 64
    for q in range(8):
        for p in range(4):
            even = blocks[16 * q : 16 * q + 8, 128 * p : 128 * p + 128]
            odd = blocks[16 * q + 8 : 16 * q + 16, 128 * p : 128 * p + 128]
            lanes = slice(128 * q, 128 * q + 128)
            natural[16 * p : 16 * p + 8, lanes] = jnp.where(left, even, pltpu.roll(odd, 64, 1))
            natural[16 * p + 8 : 16 * p + 16, lanes] = jnp.where(
                left, pltpu.roll(even, 64, 1), odd
            )
    high, low = halves(natural[...])
    ebias[...] = jnp.exp(mm(row_order, high) + mm(row_order, low))


def prep_kernel(table, scale, ebias, temper, natural):
    relative_bias(table[...], natural, ebias)
    per_head = jnp.exp(jnp.minimum(scale[...], math.log(100.0)))
    head_of = iota((1, ATT), 1) // 32
    line = jnp.zeros((1, ATT), f32)
    for h in range(HEADS):
        line = jnp.where(head_of == h, per_head[0:1, h : h + 1], line)
    temper[...] = line


def prep(table, scale):
    return pl.pallas_call(
        prep_kernel,
        out_shape=[
            jax.ShapeDtypeStruct((CELLS, HEADS * CELLS), f32),
            jax.ShapeDtypeStruct((1, ATT), f32),
        ],
        scratch_shapes=[pltpu.VMEM((CELLS, HEADS * CELLS), f32)],
        compiler_params=pltpu.CompilerParams(vmem_limit_bytes=12 * MIB),
        cost_estimate=pl.CostEstimate(
            flops=100_000_000, bytes_accessed=400_000, transcendentals=80_000
        ),
        name="prep",
    )(table, scale)


def group_total(column):
    pair = column[0:8] + column[8:16]
    pair = pair + pltpu.roll(pair, 4, 0)
    return jnp.concatenate([pair, pair], axis=0)


def row_total(value):
    return jnp.sum(value, axis=1, keepdims=True)


def col_total(value):
    return jnp.sum(value, axis=0, keepdims=True)


def windows(quads, kept, emit, params, scratch):
    ebias, temper, w_qkv, w_proj, gain, shift, merge = params
    (
        x_s,
        qkv_s,
        unit_s,
        inv_s,
        unit16_s,
        seg_s,
        qbd_s,
        prob_s,
        prob16_s,
        att_s,
        proj_s,
        mixed_s,
        gproj_s,
        ga_s,
        gpack_s,
        mgain,
    ) = scratch
    count = 16 * len(quads)
    pairs = [(w, b) for w in range(count // 64) for b in range(BLOCKS)]
    for n, (ref, lo) in enumerate(quads):
        x_s[16 * n : 16 * n + 16, :] = ref[lo : lo + 16, 0:D]
    for n in range(6):
        cols = slice(256 * n, 256 * n + 256)
        qkv_s[:, cols] = mm(x_s[...], w_qkv[:, cols]).astype(bf16)

    seg = onehot(iota((128, 128), 0) // 32 == iota((128, 128), 1) // 32)
    head_lane = iota((64, 128), 1) // 32
    head_mask = [onehot(head_lane == h) for h in range(4)]

    def store_terms(n, value):
        seg_s[count * n : count * n + count, :] = value.astype(bf16)

    def block_diagonal(value):
        return jnp.concatenate([value * head_mask[h] for h in range(4)], axis=0)

    def diagonal(value):
        out = value[192:256]
        for h in range(3):
            out = jnp.where(head_lane == h, value[64 * h : 64 * h + 64], out)
        return out

    for n in range(8):
        raw = qkv_s[:, 128 * n : 128 * n + 128].astype(f32)
        store_terms(n, raw * raw)
    squares = mm(seg_s[...], seg)
    for n in range(8):
        cols = slice(128 * n, 128 * n + 128)
        inv = lax.rsqrt(squares[count * n : count * n + count] + unit_eps)
        unit = qkv_s[:, cols].astype(f32) * inv
        inv_s[:, cols] = inv
        unit_s[:, cols] = unit
        if n < BLOCKS:
            unit = unit * temper[:, cols]
        unit16_s[:, cols] = unit.astype(bf16)

    code_lane = iota((16, 128), 1)
    allowed = []
    for w in range(count // 64):
        hot = jnp.concatenate(
            [
                onehot(ref[lo : lo + 16, 2 * D :].astype(f32).astype(jnp.int32) == code_lane)
                for ref, lo in quads[4 * w : 4 * w + 4]
            ],
            axis=0,
        )
        allowed.append(mm_nt(hot, jnp.concatenate([hot] * 4, axis=0)))
    for n, (w, b) in enumerate(pairs):
        rows = slice(64 * w, 64 * w + 64)
        wide = slice(256 * b, 256 * b + 256)
        qbd = block_diagonal(unit16_s[rows, 128 * b : 128 * b + 128])
        qbd_s[256 * n : 256 * n + 256, :] = qbd
        score = mm_nt(unit16_s[rows, ATT + 128 * b : ATT + 128 * b + 128], qbd)
        weight = jnp.exp(score) * ebias[:, wide] * allowed[w]
        prob = weight * (1.0 / col_total(weight))
        prob_s[rows, wide] = prob
        prob16_s[rows, wide] = prob.astype(bf16)
    for w, b in pairs:
        rows = slice(64 * w, 64 * w + 64)
        vals = qkv_s[rows, 2 * ATT + 128 * b : 2 * ATT + 128 * b + 128]
        att = diagonal(mm_tn(prob16_s[rows, 256 * b : 256 * b + 256], vals))
        att_s[rows, 128 * b : 128 * b + 128] = att.astype(bf16)

    total = jnp.zeros((count, 128), f32)
    square = jnp.zeros((count, 128), f32)
    for n in range(4):
        cols = slice(256 * n, 256 * n + 256)
        part = mm(att_s[...], w_proj[:, cols])
        proj_s[:, cols] = part
        left, right = part[:, 0:128], part[:, 128:256]
        total = total + left + right
        square = square + left * left + right * right

    spans = [slice(16 * n, 16 * n + 16) for n in range(len(quads))]

    def ghat_of(n):
        ref, lo = quads[n]
        return ref[lo : lo + 16, D : 2 * D].astype(f32) * mgain[...]

    for s in range(4):
        mgain[4 * s : 4 * s + 4, :] = jnp.broadcast_to(merge[:, s * D : (s + 1) * D], (4, D))
    mean_p = row_total(total) * (1.0 / D)
    var_p = row_total(square) * (1.0 / D) - mean_p * mean_p
    inv_p = lax.rsqrt(jnp.maximum(var_p, 0.0) + norm_eps)
    mean = [mean_p[rows] for rows in spans]
    inv_std = [inv_p[rows] for rows in spans]
    mean_m, mean_g, merge_inv, slope = [], [], [], []
    for n, rows in enumerate(spans):
        normed = (proj_s[rows, :] - mean[n]) * inv_std[n]
        proj_s[rows, :] = normed
        mixed = x_s[rows, :].astype(f32) + normed * gain[...] + shift[...]
        mixed_s[rows, :] = mixed
        ghat = ghat_of(n)
        mu = group_total(row_total(mixed)) * (0.25 / D)
        mg = group_total(row_total(ghat)) * (0.25 / D)
        mm2 = group_total(row_total(mixed * mixed)) * (0.25 / D)
        mgm = group_total(row_total(ghat * mixed)) * (0.25 / D)
        inv = lax.rsqrt(jnp.maximum(mm2 - mu * mu, 0.0) + norm_eps)
        mean_m.append(mu)
        mean_g.append(mg)
        merge_inv.append(inv)
        slope.append((mgm - mg * mu) * inv * inv)
    mean_e, mean_en = [], []
    for n, rows in enumerate(spans):
        cent = mixed_s[rows, :] - mean_m[n]
        gmixed = merge_inv[n] * (ghat_of(n) - mean_g[n] - cent * slope[n])
        mixed_s[rows, :] = gmixed
        gnorm = gmixed * gain[...]
        mean_e.append(row_total(gnorm) * (1.0 / D))
        mean_en.append(row_total(gnorm * proj_s[rows, :]) * (1.0 / D))
    for n, rows in enumerate(spans):
        gnorm = mixed_s[rows, :] * gain[...]
        gproj = inv_std[n] * (gnorm - mean_e[n] - proj_s[rows, :] * mean_en[n])
        gproj_s[rows, :] = gproj.astype(bf16)

    for n in range(2):
        cols = slice(256 * n, 256 * n + 256)
        ga_s[:, cols] = mm_nt(gproj_s[...], w_proj[cols, :]).astype(bf16)

    grad_k, grad_q = [], []
    for n, (w, b) in enumerate(pairs):
        rows = slice(64 * w, 64 * w + 64)
        wide = slice(256 * b, 256 * b + 256)
        vcols = slice(2 * ATT + 128 * b, 2 * ATT + 128 * b + 128)
        gabd = block_diagonal(ga_s[rows, 128 * b : 128 * b + 128])
        gprob = mm_nt(qkv_s[rows, vcols], gabd)
        gpack_s[rows, vcols] = mm(prob16_s[rows, wide], gabd).astype(bf16)
        prob = prob_s[rows, wide]
        gscore = prob * (gprob - col_total(prob * gprob))
        prob16_s[rows, wide] = gscore.astype(bf16)
    for n, (w, b) in enumerate(pairs):
        rows = slice(64 * w, 64 * w + 64)
        gscore = prob16_s[rows, 256 * b : 256 * b + 256]
        qcols = slice(128 * b, 128 * b + 128)
        kcols = slice(ATT + 128 * b, ATT + 128 * b + 128)
        gk = mm(gscore, qbd_s[256 * n : 256 * n + 256, :])
        gq = diagonal(mm_tn(gscore, unit16_s[rows, kcols])) * temper[:, qcols]
        proj_s[rows, qcols] = gq
        proj_s[rows, kcols] = gk
    for n in range(8):
        cols = slice(128 * n, 128 * n + 128)
        store_terms(n, unit_s[:, cols] * proj_s[:, cols])
    along = mm(seg_s[...], seg)
    for n in range(8):
        cols = slice(128 * n, 128 * n + 128)
        grad = inv_s[:, cols] * (proj_s[:, cols] - unit_s[:, cols] * along[count * n : count * n + count])
        gpack_s[:, cols] = grad.astype(bf16)

    for n in range(4):
        cols = slice(256 * n, 256 * n + 256)
        total = mixed_s[kept, cols] + mm_nt(gpack_s[kept, :], w_qkv[cols, :])
        emit(cols, total.astype(bf16))


def scratch_for(count):
    return [
        pltpu.VMEM((count, D), bf16),
        pltpu.VMEM((count, 3 * ATT), bf16),
        pltpu.VMEM((count, 2 * ATT), f32),
        pltpu.VMEM((count, 2 * ATT), f32),
        pltpu.VMEM((count, 2 * ATT), bf16),
        pltpu.VMEM((8 * count, 128), bf16),
        pltpu.VMEM((16 * count, 128), bf16),
        pltpu.VMEM((count, HEADS * CELLS), f32),
        pltpu.VMEM((count, HEADS * CELLS), bf16),
        pltpu.VMEM((count, ATT), bf16),
        pltpu.VMEM((count, D), f32),
        pltpu.VMEM((count, D), f32),
        pltpu.VMEM((count, D), bf16),
        pltpu.VMEM((count, ATT), bf16),
        pltpu.VMEM((count, 3 * ATT), bf16),
        pltpu.VMEM((16, D), f32),
    ]


def inner_kernel(own, lon, *refs):
    params, (out_own, out_lon), scratch = refs[:7], refs[7:9], refs[9:]
    quads = ((lon, 16), (own, 16), (lon, 32), (own, 32))

    def emit(cols, total):
        out_lon[0:16, cols] = total[0:16]
        out_own[0:16, cols] = total[16:32]
        out_lon[16:32, cols] = total[32:48]
        out_own[16:32, cols] = total[48:64]

    windows(quads, slice(0, 64), emit, params, scratch)


def inner(own, lon, params):
    return pl.pallas_call(
        inner_kernel,
        out_shape=[jax.ShapeDtypeStruct((32, D), bf16)] * 2,
        scratch_shapes=scratch_for(64),
        compiler_params=pltpu.CompilerParams(vmem_limit_bytes=16 * MIB),
        cost_estimate=pl.CostEstimate(
            flops=3_000_000_000, bytes_accessed=6_000_000, transcendentals=150_000
        ),
        name="inner",
    )(own, lon, *params)


def outer_kernel(own, lon, above, below, in_own, in_lon, *refs):
    params, (out_own, out_lon), scratch = refs[:7], refs[7:9], refs[9:]
    quads = (
        (above, 0),
        (above, 16),
        (lon, 0),
        (own, 0),
        (lon, 48),
        (own, 48),
        (below, 0),
        (below, 16),
    )
    out_own[16:48, :] = in_own[...]
    out_lon[16:48, :] = in_lon[...]

    def emit(cols, total):
        out_lon[0:16, cols] = total[0:16]
        out_own[0:16, cols] = total[16:32]
        out_lon[48:64, cols] = total[32:48]
        out_own[48:64, cols] = total[48:64]

    windows(quads, slice(32, 96), emit, params, scratch)


def outer(own, lon, above, below, in_own, in_lon, params):
    return pl.pallas_call(
        outer_kernel,
        out_shape=[jax.ShapeDtypeStruct((64, D), bf16)] * 2,
        scratch_shapes=scratch_for(128),
        compiler_params=pltpu.CompilerParams(vmem_limit_bytes=24 * MIB),
        cost_estimate=pl.CostEstimate(
            flops=3_000_000_000, bytes_accessed=6_000_000, transcendentals=150_000
        ),
        name="outer",
    )(own, lon, above, below, in_own, in_lon, *params)


def final_kernel(own, lon, out):
    rows = jnp.concatenate([own[...], lon[...]], axis=0)
    row, col, _ = sorted_place(iota((128, 128), 1))
    token_place = onehot(iota((128, 128), 0) == row * 8 + col)
    out[...] = mm(token_place, rows).reshape(16, 8, D).astype(bf16)


def final(own, lon):
    return pl.pallas_call(
        final_kernel,
        out_shape=jax.ShapeDtypeStruct((16, 8, D), bf16),
        compiler_params=pltpu.CompilerParams(vmem_limit_bytes=8 * MIB),
        name="final",
    )(own, lon)


def passed_along(block, axis, distance):
    count = lax.axis_size(axis)
    route = [(i, (i + distance) % count) for i in range(count)]
    return lax.ppermute(block, axis, route)


def shards(
    tokens,
    labels,
    w_qkv,
    w_proj,
    logit_scale,
    bias_table,
    norm_gain,
    norm_shift,
    merge_gain,
    cotangent,
):
    own, lon = pack(tokens, labels.T, cotangent, places())
    lon = passed_along(lon, "lon", 1)
    ebias, temper = prep(bias_table, logit_scale.reshape(1, HEADS))
    params = (
        ebias,
        temper,
        w_qkv,
        w_proj,
        norm_gain.reshape(1, D),
        norm_shift.reshape(1, D),
        merge_gain.reshape(1, 4 * D),
    )
    top, bottom = strips(own, lon)
    below = passed_along(top, "lat", -1)
    above = passed_along(bottom, "lat", 1)
    in_own, in_lon = inner(own, lon, params)
    own, lon = outer(own, lon, above, below, in_own, in_lon, params)
    lon = passed_along(lon, "lon", -1)
    return final(own, lon)


def solution(mesh):
    placed = (
        P("lat", "lon", None),
        P("lat", "lon"),
        P(),
        P(),
        P(),
        P(),
        P(),
        P(),
        P(),
        P("lat", "lon", None),
    )
    return jax.shard_map(
        shards, mesh=mesh, in_specs=placed, out_specs=P("lat", "lon", None), check_vma=False
    )
```
